32 devices in a mesh: dp: 8 (over y, x, core), tensor: 4 (over z).
Axes of the slice: x: 2, y: 2, z: 4, core: 2. Of those that a mesh axis runs over, the one named last changes fastest.
Arguments:
- tokens: bfloat16 [8, 2048, 1024], P('dp', 'tensor'), may hold values from -6 to 6
- cotangent: bfloat16 [8, 2048, 1024], P('dp', 'tensor'), may hold values from -6 to 6
- doc_ids: int32 [8, 2048], P('dp'), may hold values from 0 to 21, as said below
- adapter_pick: int32 [8], P('dp'), may hold values from 0 to 7, as said below
- norm_gain: float32 [1024], replicated, may hold values from 0.25 to 1.75
- gate_x_weight: bfloat16 [1024, 2, 2048], P('dp', None, 'tensor'), may hold values from -0.1875 to 0.1875
- bc_weight: bfloat16 [1024, 256], P('dp'), may hold values from -0.1875 to 0.1875
- dt_weight: bfloat16 [1024, 32], P('dp', 'tensor'), may hold values from -0.1875 to 0.1875
- conv_x_weight: float32 [4, 2048], P(None, 'tensor'), may hold values from -3 to 3
- conv_bc_weight: float32 [4, 256], replicated, may hold values from -3 to 3
- conv_x_bias: float32 [2048], P('tensor'), may hold values from -3 to 3
- conv_bc_bias: float32 [256], replicated, may hold values from -3 to 3
- dt_bias: float32 [32], P('tensor'), may hold values from -6 to -2
- a_log: float32 [32], P('tensor'), may hold values from 0 to 2.77
- skip_gain: float32 [32], P('tensor'), may hold values from 0.5 to 1.5
- inner_gain: float32 [2048], P('tensor'), may hold values from 0.25 to 1.75
- out_weight: bfloat16 [2048, 1024], P('tensor', 'dp'), may hold values from -0.125 to 0.125
- in_down: bfloat16 [8, 1024, 16], P(None, 'dp'), may hold values from -0.1875 to 0.1875
- in_up: bfloat16 [8, 16, 2, 32, 64], P(None, None, None, 'tensor', 'dp'), may hold values from -1.5 to 1.5
- out_down: bfloat16 [8, 32, 64, 16], P(None, 'tensor', 'dp'), may hold values from -0.125 to 0.125
- out_up: bfloat16 [8, 16, 1024], P(None, None, 'dp'), may hold values from -1.5 to 1.5
Outputs:
- mixed: float32 [8, 2048, 1024], P('dp', 'tensor')
- tokens_grad: float32 [8, 2048, 1024], P('dp', 'tensor')
- grad_in_down: float32 [8, 1024, 16], P(None, 'dp')
- grad_in_up: float32 [8, 16, 2, 32, 64], P(None, None, None, 'tensor', 'dp')
- grad_out_down: float32 [8, 32, 64, 16], P(None, 'tensor', 'dp')
- grad_out_up: float32 [8, 16, 1024], P(None, None, 'dp')
The draws below stay inside these ranges and needn't reach their ends.
Inputs may be any that keep to these rules, and one draw needn't show every extreme that they name: `doc_ids`: within each sequence the document numbers start at 0 and rise by one at each document start. Every document has 60 to 800 tokens except the last of a sequence, which may be cut shorter; of the first two documents of each sequence one has 800 tokens and the other 60. `adapter_pick`: each adapter serves exactly 1 sequence.
All inputs are finite; a program needn't handle non-finite values.
Results may differ from the reference program's by a relative error of at most 0.0059.
Values may be sent and summed in bfloat16 or wider, within the bound.
No kernel may reach another device: no remote copies, remote signals or barrier semaphores. Data moves between devices by JAX's collectives and lax.ppermute only.
A program may use at most 192 MiB of HBM per device.

```python
from functools import partial
import jax
import jax.numpy as jnp
from jax import lax

D = 1024
E = 2048
H = 32
P_SIZE = 64
N = 128
CONV = 4
GROUP = 256
RANK = 16
ADAPTERS = 8
LENGTH = 2048
DOC_LEAST = 60
DOC_MOST = 800
SEQUENCES = 8


def draw_doc_ids(key, part):
    key = jax.random.fold_in(key, 11)
    doc_slots = LENGTH // DOC_LEAST + 2
    doc_lengths = jax.random.randint(key, (SEQUENCES, doc_slots), DOC_LEAST, DOC_MOST + 1)
    first_long = jax.random.randint(jax.random.fold_in(key, 1), (SEQUENCES, 1), 0, 2)
    shortest_seq = jax.random.randint(jax.random.fold_in(key, 2), (), 0, SEQUENCES)
    slot_index = jnp.arange(doc_slots)[None, :]
    seq_index = jnp.arange(SEQUENCES)[:, None]
    doc_lengths = jnp.where(seq_index == shortest_seq, DOC_LEAST, doc_lengths)
    doc_lengths = jnp.where(slot_index == first_long, DOC_MOST, doc_lengths)
    doc_lengths = jnp.where(slot_index == 1 - first_long, DOC_LEAST, doc_lengths)
    doc_ends = jnp.cumsum(doc_lengths, axis=1)
    positions = jnp.arange(LENGTH)
    passed = (doc_ends[:, None, :] <= positions[None, :, None]).astype(jnp.int32)
    return jnp.sum(passed, axis=2).astype(jnp.int32)


def draw_adapter_pick(key, part):
    key = jax.random.fold_in(key, 23)
    shuffled = jax.random.permutation(key, SEQUENCES)
    return (shuffled % ADAPTERS).astype(jnp.int32)


def levels(key, extent, cuts, smallest, largest):
    def one(axis_at, blocks):
        heights = jax.random.uniform(jax.random.fold_in(jax.random.fold_in(key, 6), axis_at), (blocks,), jnp.float32, smallest / len(cuts), largest / len(cuts))
        return jnp.repeat(jnp.exp(heights), extent[axis_at] // blocks).reshape((-1,) + (1,) * (len(extent) - axis_at - 1))

    level = one(*cuts[0])
    for cut in cuts[1:]:
        level = level * one(*cut)
    return level


def centred(rng, extent, width, limit, cuts=(), dtype=jnp.bfloat16):
    values = jax.random.normal(rng, extent, jnp.float32) * width
    if len(cuts) > 0:
        values = levels(rng, extent, cuts, -0.22, 0.18) * values
    return jnp.clip(values, min=-limit, max=limit).astype(dtype)


def setup_inputs(seed: int = 0) -> dict:
    key_list = jax.random.split(jax.random.key(seed), 22)
    return {
        "tokens": centred(key_list[0], (SEQUENCES, LENGTH, D), 1.0, 6.0, ((0, 8), (1, 4))),
        "cotangent": centred(key_list[1], (SEQUENCES, LENGTH, D), 1.0, 6.0, ((0, 8), (1, 4))),
        "doc_ids": draw_doc_ids(jax.random.fold_in(key_list[21], 71), 0),
        "adapter_pick": draw_adapter_pick(jax.random.fold_in(key_list[21], 71), 0),
        "norm_gain": jnp.clip(1.0 + 0.15 * jax.random.normal(key_list[4], (D,), jnp.float32), 0.25, 1.75),
        "gate_x_weight": centred(key_list[5], (D, 2, E), D ** -0.5, 0.1875, ((0, 8), (2, 4))),
        "bc_weight": centred(key_list[6], (D, 2 * N), D ** -0.5, 0.1875, ((0, 8),)),
        "dt_weight": centred(key_list[7], (D, H), D ** -0.5, 0.1875, ((0, 8), (1, 4))),
        "conv_x_weight": centred(key_list[8], (CONV, E), CONV ** -0.5, 3.0, ((1, 4),), jnp.float32),
        "conv_bc_weight": centred(key_list[9], (CONV, 2 * N), CONV ** -0.5, 3.0, (), jnp.float32),
        "conv_x_bias": centred(key_list[10], (E,), 0.5, 3.0, ((0, 4),), jnp.float32),
        "conv_bc_bias": centred(key_list[11], (2 * N,), 0.5, 3.0, (), jnp.float32),
        "dt_bias": jnp.clip(-6.0 + 4.0 * jax.random.uniform(key_list[12], (H,), jnp.float32) ** levels(key_list[12], (H,), ((0, 4),), -0.2, 0.2), -6.0, -2.0),
        "a_log": jnp.clip(2.77 * jax.random.uniform(key_list[13], (H,), jnp.float32) ** levels(key_list[13], (H,), ((0, 4),), -0.2, 0.2), 0.0, 2.77),
        "skip_gain": jnp.clip(0.5 + 1.0 * jax.random.uniform(key_list[14], (H,), jnp.float32) ** levels(key_list[14], (H,), ((0, 4),), -0.2, 0.2), 0.5, 1.5),
        "inner_gain": jnp.clip(1.0 + 0.15 * jax.random.normal(key_list[15], (E,), jnp.float32), 0.25, 1.75),
        "out_weight": centred(key_list[16], (E, D), E ** -0.5, 0.125, ((0, 4), (1, 8))),
        "in_down": centred(key_list[17], (ADAPTERS, D, RANK), D ** -0.5, 0.1875, ((1, 8),)),
        "in_up": centred(key_list[18], (ADAPTERS, RANK, 2, H, P_SIZE), RANK ** -0.5, 1.5, ((3, 4), (4, 8))),
        "out_down": centred(key_list[19], (ADAPTERS, H, P_SIZE, RANK), E ** -0.5, 0.125, ((1, 4), (2, 8))),
        "out_up": centred(key_list[20], (ADAPTERS, RANK, D), RANK ** -0.5, 1.5, ((2, 8),)),
    }


exact_product = lax.Precision.HIGHEST
epsilon = 1e-05

@jax.custom_vjp
def low(v):
    return lax.optimization_barrier(v.astype(jnp.bfloat16)).astype(jnp.float32)

@jax.custom_vjp
def low_back(v):
    return v

def low_keep(v):
    return (low(v), None)

def low_pass(kept, grad):
    return (grad,)

def back_keep(v):
    return (v, None)

def back_low(kept, grad):
    return (low(grad),)
low.defvjp(low_keep, low_pass)
low_back.defvjp(back_keep, back_low)

def precise_dot(left, right):
    return jnp.dot(left, right, precision=exact_product, preferred_element_type=jnp.float32)

def causal_conv(inputs, seg_ids, kernel, offset):
    length = inputs.shape[0]
    summed = kernel[-1] * inputs + offset
    for shift_by in range(1, kernel.shape[0]):
        earlier = jnp.pad(inputs, ((shift_by, 0), (0, 0)))[:length]
        earlier_seg = jnp.pad(seg_ids, (shift_by, 0), constant_values=-1)[:length]
        summed = summed + kernel[-1 - shift_by] * earlier * (earlier_seg == seg_ids).astype(jnp.float32)[:, None]
    return summed

def scan_block(decays, carry, pieces):
    carry_state, last_seg = carry
    values, dt_vals, inputs_b, inputs_c, seg_ids = pieces
    log_sums = jnp.cumsum(dt_vals * decays[None, :], axis=0)
    positions = jnp.arange(seg_ids.shape[0])
    allowed = (seg_ids[:, None] == seg_ids[None, :]) & (positions[:, None] >= positions[None, :])
    log_gaps = jnp.where(allowed[:, :, None], log_sums[:, None, :] - log_sums[None, :, :], 0.0)
    weights = jnp.exp(log_gaps) * allowed[:, :, None].astype(jnp.float32)
    scores = precise_dot(inputs_c, inputs_b.T)
    mixing = weights * scores[:, :, None] * dt_vals[None, :, :]
    within = jnp.einsum('ijh,jhp->ihp', mixing, values, precision=exact_product)
    carried = (seg_ids == last_seg).astype(jnp.float32)
    across = jnp.einsum('in,hpn->ihp', inputs_c, carry_state, precision=exact_product)
    across = across * (jnp.exp(log_sums) * carried[:, None])[:, :, None]
    final_seg = seg_ids[-1]
    to_state = jnp.exp(log_sums[-1][None, :] - log_sums) * dt_vals
    to_state = to_state * (seg_ids == final_seg).astype(jnp.float32)[:, None]
    new_part = jnp.einsum('jh,jn,jhp->hpn', to_state, inputs_b, values, precision=exact_product)
    keep_state = (final_seg == last_seg).astype(jnp.float32)
    carry_state = new_part + carry_state * (jnp.exp(log_sums[-1]) * keep_state)[:, None, None]
    return ((carry_state, final_seg), within + across)

def run_ssd(values, dt_vals, decays, inputs_b, inputs_c, seg_ids, block_len):
    length, head_count, head_size = values.shape
    blocks = length // block_len
    state_dim = inputs_b.shape[1]
    pieces = (values.reshape(blocks, block_len, head_count, head_size), dt_vals.reshape(blocks, block_len, head_count), inputs_b.reshape(blocks, block_len, state_dim), inputs_c.reshape(blocks, block_len, state_dim), seg_ids.reshape(blocks, block_len))
    initial = (jnp.zeros((head_count, head_size, state_dim), jnp.float32), jnp.array(-1, jnp.int32))
    ignored, outputs = lax.scan(jax.checkpoint(partial(scan_block, decays)), initial, pieces)
    return outputs.reshape(length, head_count, head_size)

def block_layer(tokens, tables, frozen, seg_ids, pick):
    norm_gain, gate_x_weight, bc_weight, dt_weight, conv_x_weight, conv_bc_weight, conv_x_bias, conv_bc_bias, dt_bias, a_log, skip_gain, inner_gain, out_weight = frozen
    in_down, in_up, out_down, out_up = tables
    length = tokens.shape[0]
    row_scale = lax.rsqrt(lax.optimization_barrier(jnp.mean(tokens * tokens, axis=1, keepdims=True)) + epsilon)
    normed_rows = low(tokens * row_scale * norm_gain)
    rank_in = precise_dot(normed_rows, in_down[pick])
    projected = precise_dot(normed_rows, gate_x_weight.reshape(D, 2 * E)) + precise_dot(rank_in, in_up[pick].reshape(RANK, 2 * E))
    projected = low_back(projected)
    gate_z = projected[:, :E]
    conv_in = projected[:, E:]
    bc_proj = low_back(precise_dot(normed_rows, bc_weight))
    dt_proj = low_back(precise_dot(normed_rows, dt_weight))
    values = jax.nn.silu(causal_conv(conv_in, seg_ids, conv_x_weight, conv_x_bias)).reshape(length, H, P_SIZE)
    state_in = jax.nn.silu(causal_conv(bc_proj, seg_ids, conv_bc_weight, conv_bc_bias))
    inputs_b = state_in[:, :N]
    inputs_c = state_in[:, N:]
    dt_vals = jax.nn.softplus(dt_proj + dt_bias)
    decays = -jnp.exp(a_log)
    heads_out = run_ssd(values, dt_vals, decays, inputs_b, inputs_c, seg_ids, GROUP) + skip_gain[None, :, None] * values
    gated = heads_out.reshape(length, E) * jax.nn.silu(gate_z)
    inner_scale = lax.rsqrt(lax.optimization_barrier(jnp.mean(gated * gated, axis=1, keepdims=True)) + epsilon)
    normed_inner = gated * inner_scale * inner_gain
    rank_output = precise_dot(normed_inner, out_down[pick].reshape(E, RANK))
    return tokens + precise_dot(low(normed_inner), out_weight) + precise_dot(rank_output, out_up[pick])

def reference(tokens, cotangent, doc_ids, adapter_pick, norm_gain, gate_x_weight, bc_weight, dt_weight, conv_x_weight, conv_bc_weight, conv_x_bias, conv_bc_bias, dt_bias, a_log, skip_gain, inner_gain, out_weight, in_down, in_up, out_down, out_up):
    frozen = tuple((array.astype(jnp.float32) for array in (norm_gain, gate_x_weight, bc_weight, dt_weight, conv_x_weight, conv_bc_weight, conv_x_bias, conv_bc_bias, dt_bias, a_log, skip_gain, inner_gain, out_weight)))
    tables = tuple((array.astype(jnp.float32) for array in (in_down, in_up, out_down, out_up)))

    def per_sequence(totals, items):
        seq_tokens, seq_cot, seg_ids, pick = items

        def forward(x_in, adapter_tables):
            return block_layer(x_in, adapter_tables, frozen, seg_ids, pick)
        result, pullback = jax.vjp(forward, seq_tokens.astype(jnp.float32), tables)
        grad_x, grad_tables = pullback(seq_cot.astype(jnp.float32))
        totals = jax.tree.map(jnp.add, totals, grad_tables)
        return (totals, (result, grad_x))
    zeros = jax.tree.map(jnp.zeros_like, tables)
    totals, (mixed, tokens_grad) = lax.scan(per_sequence, zeros, (tokens, cotangent, doc_ids, adapter_pick))
    return (mixed, tokens_grad, totals[0], totals[1], totals[2], totals[3])
```

```python
import math

import jax
import jax.numpy as jnp
from jax import lax
from jax.experimental import pallas as pl
from jax.experimental.pallas import tpu as pltpu
from jax.sharding import PartitionSpec as P

epsilon = 1e-05
chunk = 128
lanes = 128
doc_most = 800
edge = 16
f32, bf16 = jnp.float32, jnp.bfloat16
exact = lax.Precision.HIGHEST
vmem_bytes = 48 * 1024 * 1024


def dot(a, b):
    return jnp.dot(a, b, preferred_element_type=f32)


def dot_nt(a, b):
    return lax.dot_general(a, b, (((1,), (1,)), ((), ())), preferred_element_type=f32)


def dot_tn(a, b):
    return lax.dot_general(a, b, (((0,), (0,)), ((), ())), preferred_element_type=f32)


def halves(x):
    high = x.astype(bf16)
    return high, (x - high.astype(f32)).astype(bf16)


def pieces(x, count):
    out = []
    for _ in range(count):
        part = lax.reduce_precision(x, 8, 7)
        out.append(part.astype(bf16))
        x = x - part
    return jnp.concatenate(out, axis=-1)


def dot2(x, w):
    high, low = halves(x)
    return dot(high, w) + dot(low, w)


def dot2_nt(x, w):
    high, low = halves(x)
    return dot_nt(high, w) + dot_nt(low, w)


def dot2_tn(x, w):
    high, low = halves(x)
    return dot_tn(high, w) + dot_tn(low, w)


def tile_lanes(m, width):
    return m if width == lanes else jnp.concatenate([m] * (width // lanes), axis=1)


def silu_parts(u):
    s = 1.0 / (1.0 + jnp.exp(-u))
    return u * s, s * (1.0 + u * (1.0 - s))


def weight_block(refs):
    out = []
    for own, other in ((refs[0], refs[1]), (refs[2], refs[3])):
        cols = own.shape[-1]
        out.append((own[...].reshape(-1, cols), other[...].reshape(-1, cols)))
    return out


def times_weight(left, refs, put):
    for j, (own, other) in enumerate(weight_block(refs)):
        k = own.shape[0]
        cols = own.shape[1]
        put(slice(j * cols, (j + 1) * cols), dot(left[:, :k], own) + dot(left[:, k : 2 * k], other))


def add_times_transposed(acc, low, refs):
    (own_a, other_a), (own_b, other_b) = weight_block(refs)
    k, cols = own_a.shape
    a, b = low[:, :cols], low[:, cols:]
    acc[:, :k] += dot_nt(a, own_a) + dot_nt(b, own_b)
    acc[:, k : 2 * k] += dot_nt(a, other_a) + dot_nt(b, other_b)


def bring_order(sel, source, target):
    for k in range(8):
        at = pl.multiple_of(sel[k] * lanes, lanes)
        target[:, k * lanes : (k + 1) * lanes] = source[:, pl.ds(at, lanes)]


def rows_of(c):
    return slice(c * chunk, (c + 1) * chunk)


def proj_kernel(sel, normed, own_a, oth_a, own_b, oth_b, ranks, a_up, params, masks, dt2, eo2, ex, b_t,
                u_out, sc_out, f_out, left, xs, moved):
    @pl.when(pl.program_id(0) == 0)
    def _():
        bring_order(sel, normed, left)

    def put(cols, value):
        xs[:, cols] = value + dot(ranks[...], a_up[:, cols])

    times_weight(left, (own_a, oth_a, own_b, oth_b), put)
    own, width = u_out.shape
    step = min(width, 256)
    for c in range(own // chunk):
        rows = rows_of(c)
        for n in range(width // step):
            cols = slice(n * step, (n + 1) * step)
            cur = xs[edge + c * chunk - 8 : edge + (c + 1) * chunk, cols]
            total = params[3:4, cols] * cur[8:] + params[4:5, cols]
            for k in range(1, 4):
                shifted = pltpu.roll(cur, k, 0)[8:]
                total = total + params[3 - k : 4 - k, cols] * (
                    shifted * tile_lanes(masks[k - 1, rows, :], step)
                )
            u_out[rows, cols] = total
            value = total / (1.0 + jnp.exp(-total))
            scaled = (dot(dt2[rows, :], ex[:, cols]) * value).astype(bf16)
            sc_out[rows, cols] = scaled
            moved[rows, cols] = (dot(eo2[rows, :], ex[:, cols]) * scaled.astype(f32)).astype(bf16)
    f_out[...] = dot(b_t[...], moved[...]).astype(bf16)


def pair_parts(lcol, cums_t, p):
    lc = lcol[:, p * 2 * lanes : (p + 1) * 2 * lanes]
    lr = jnp.concatenate([cums_t[2 * p : 2 * p + 1, :], cums_t[2 * p + 1 : 2 * p + 2, :]], axis=1)
    return jnp.exp2(jnp.minimum(lc - lr, 0.0))


def two_heads(v, head_size):
    lane = lax.broadcasted_iota(jnp.int32, v.shape, 1)
    zero = jnp.zeros_like(v)
    return jnp.concatenate([jnp.where(lane < head_size, v, zero), jnp.where(lane < head_size, zero, v)], 0)


def within_kernel(sc, cums3, cums_t, scores, exl, y_out):
    own, width = y_out.shape
    for c in range(own // chunk):
        rows = rows_of(c)
        lcol = dot(cums3[rows, :], exl[...])
        allowed = tile_lanes(scores[c], 2 * lanes)
        for p in range(width // lanes):
            e = pair_parts(lcol, cums_t[0, c], p)
            m = (e * allowed).astype(bf16)
            cols = slice(p * lanes, (p + 1) * lanes)
            y_out[rows, cols] = dot(m, two_heads(sc[rows, cols], lanes // 2))


def gate_kernel(sel, normed, own_a, oth_a, own_b, oth_b, ranks, a_up, params, yw, u, sc, s_in, ei2, eo2,
                keep, ex, b_t, in_c, y_out, z_out, gated_out, states, sumsq, left):
    @pl.when(pl.program_id(0) == 0)
    def _():
        bring_order(sel, normed, left)
        sumsq[...] = jnp.zeros_like(sumsq)

    def put(cols, value):
        z_out[:, cols] = value + dot(ranks[...], a_up[:, cols])

    times_weight(left, (own_a, oth_a, own_b, oth_b), put)
    own, width = y_out.shape
    step = min(width, 256)
    for n in range(width // step):
        cols = slice(n * step, (n + 1) * step)
        s = s_in[:, cols]
        for c in range(own // chunk):
            rows = rows_of(c)
            low_s = s.astype(bf16)
            states[c, :, cols] = low_s
            y = yw[rows, cols] + dot(ei2[rows, :], ex[:, cols]) * dot(in_c[rows, :], low_s)
            y_out[rows, cols] = y
            v, _ = silu_parts(u[rows, cols])
            g, _ = silu_parts(z_out[rows, cols])
            gated = (y + params[6:7, cols] * v) * g
            gated_out[rows, cols] = gated
            sq = gated * gated
            part = sq[:, :lanes]
            for i in range(1, step // lanes):
                part = part + sq[:, i * lanes : (i + 1) * lanes]
            sumsq[rows, :] += part
            moved = (dot(eo2[rows, :], ex[:, cols]) * sc[rows, cols].astype(f32)).astype(bf16)
            s = s * keep[c : c + 1, cols] + dot(b_t[:, rows], moved)


def row_scale_of(sumsq, inner):
    return lax.rsqrt(jnp.sum(sumsq, axis=1, keepdims=True) / inner + epsilon)


def out_kernel(sel, gated, own_a, oth_a, own_b, oth_b, params, sumsq, cot, tokens, b_up, b_down,
               gg_out, mixed, p_down, p_up, dots, acc, cots, g_rank, rank, low, *, inner):
    g = pl.program_id(0)

    @pl.when(g == 0)
    def _():
        bring_order(sel, cot, cots)
        g_rank[...] = dot_nt(cot[...], b_up[...])
        acc[...] = jnp.zeros_like(acc)
        rank[...] = jnp.zeros_like(rank)
        dots[...] = jnp.zeros_like(dots)

    own, width = gg_out.shape
    scale = row_scale_of(sumsq[...], inner)

    def put(cols, value):
        gg = (value + dot2(g_rank[...], b_down[:, cols])) * params[5:6, cols]
        gg_out[:, cols] = gg
        prod = gg * gated[:, cols]
        for i in range(prod.shape[1] // lanes):
            dots[...] += prod[:, i * lanes : (i + 1) * lanes]

    times_weight(cots, (own_a, oth_a, own_b, oth_b), put)
    normed_inner = gated[...] * scale * params[5:6, :]
    high, rest = halves(normed_inner)
    low[...] = high
    rank[...] += dot_nt(high, b_down[...]) + dot_nt(rest, b_down[...])
    r_high, r_low = halves(g_rank[...])
    p_down[...] = dot_tn(r_high, high) + dot_tn(r_low, high) + dot_tn(r_high, rest)
    add_times_transposed(acc, low, (own_a, oth_a, own_b, oth_b))

    @pl.when(g == pl.num_programs(0) - 1)
    def _():
        p_up[...] = dot2_tn(rank[...], cot[...])
        mixed[...] = tokens[...].astype(f32) + dot2(rank[...], b_up[...])
        for k in range(8):
            at = pl.ds(pl.multiple_of(sel[k] * lanes, lanes), lanes)
            mixed[:, at] += acc[:, k * lanes : (k + 1) * lanes]


def split_kernel(gg, gated, y, u, z, params, sumsq, dots, ei2, ex, c_t, gh_out, lz_out, g_out, moved, *, inner):
    own, width = gh_out.shape
    scale = row_scale_of(sumsq[...], inner)
    coef = scale * scale * scale * (jnp.sum(dots[...], axis=1, keepdims=True) / inner)
    step = min(width, 256)
    for c in range(own // chunk):
        rows = rows_of(c)
        sc, co = scale[rows], coef[rows]
        for n in range(width // step):
            cols = slice(n * step, (n + 1) * step)
            g_gated = gg[rows, cols] * sc - gated[rows, cols] * co
            v, _ = silu_parts(u[rows, cols])
            gate, slope = silu_parts(z[rows, cols])
            heads = y[rows, cols] + params[6:7, cols] * v
            lz_out[rows, cols] = (g_gated * heads * slope).astype(bf16)
            gh = g_gated * gate
            gh_out[rows, cols] = gh
            moved[rows, cols] = (dot(ei2[rows, :], ex[:, cols]) * gh).astype(bf16)
    g_out[...] = dot(c_t[...], moved[...]).astype(bf16)


def back_within_kernel(gh, y, sc, cums3, cums_t, scores, exl, red, dv_out, ds_out, ahead, prod):
    g = pl.program_id(0)

    @pl.when(g == 0)
    def _():
        ds_out[...] = jnp.zeros_like(ds_out)
        ahead[...] = jnp.zeros_like(ahead)

    own, width = dv_out.shape
    for c in range(own // chunk):
        rows = rows_of(c)
        lcol = dot(cums3[rows, :], exl[...])
        allowed = tile_lanes(scores[c], 2 * lanes)
        ds = jnp.zeros((chunk, lanes), f32)
        for p in range(width // lanes):
            cols = slice(p * lanes, (p + 1) * lanes)
            e = pair_parts(lcol, cums_t[0, c], p)
            m = (e * allowed).astype(bf16)
            v = sc[rows, cols]
            dy = gh[rows, cols]
            high, low = halves(dy)
            both = two_heads(v, lanes // 2)
            dm = dot_nt(high, both) + dot_nt(low, both)
            eds = e * dm
            ds = ds + eds[:, :lanes] + eds[:, lanes:]
            dvb = dot_tn(m, high) + dot_tn(m, low)
            lane = lax.broadcasted_iota(jnp.int32, (chunk, lanes), 1)
            dv = jnp.where(lane < lanes // 2, dvb[:chunk], dvb[chunk:])
            dv_out[rows, cols] = dv
            prod[:, cols] = y[rows, cols] * dy - v.astype(f32) * dv
        ds_out[c] += ds
        ahead[rows, :] += dot2(prod[...], red[...])


def back_state_kernel(gs_in, states, gh, sc, dv, u, params, in_b, in_c, b_t, c_t, dt2, ei2, eo2, keep, ex, red,
                      ds, ahead, allowed, u_bc, dt_slope, decays,
                      gu_out, gbc_out, ldt_out, db, dc, behind, direct, carry, prod):
    g = pl.program_id(0)

    @pl.when(g == 0)
    def _():
        for ref in (db, dc, behind, direct, carry):
            ref[...] = jnp.zeros_like(ref)

    own, width = gu_out.shape
    step = min(width, 256)
    blocks = own // chunk
    for n in range(width // step):
        cols = slice(n * step, (n + 1) * step)
        gs = gs_in[:, cols]
        for c in reversed(range(blocks)):
            rows = rows_of(c)
            low_g = gs.astype(bf16)
            kept = keep[c : c + 1, cols]
            low_s = states[c, :, cols]
            scaled = sc[rows, cols].astype(f32)
            eo = dot(eo2[rows, :], ex[:, cols])
            dvs = eo * dot(in_b[rows, :], low_g)
            db[rows, :] += dot_nt((eo * scaled).astype(bf16), low_g)
            dy = gh[rows, cols]
            moved = (dot(ei2[rows, :], ex[:, cols]) * dy).astype(bf16)
            dc[rows, :] += dot_nt(moved, low_s)
            carried = jnp.sum(low_s.astype(f32) * gs, axis=0, keepdims=True) * kept
            carry[c : c + 1, :] += dot2(jnp.broadcast_to(carried, (8, step)), red[cols, :])[:1]
            gs = gs * kept + dot(c_t[:, rows], moved)
            g_sc = dv[rows, cols] + dvs
            v, slope = silu_parts(u[rows, cols])
            behind[rows, :] += dot2(scaled * dvs, red[cols, :])
            direct[rows, :] += dot2(v * g_sc, red[cols, :])
            g_v = dot(dt2[rows, :], ex[:, cols]) * g_sc + params[6:7, cols] * dy
            gu_out[rows, cols] = g_v * slope

    @pl.when(g == pl.num_programs(0) - 1)
    def _():
        i = lax.broadcasted_iota(jnp.int32, (chunk, chunk), 0)
        j = lax.broadcasted_iota(jnp.int32, (chunk, chunk), 1)
        at_most = jnp.where(i <= j, 1.0, 0.0).astype(bf16)
        below = jnp.where(j < i, 1.0, 0.0).astype(bf16)
        for c in range(blocks):
            rows = rows_of(c)

            def sums(tri, x):
                high, mid = halves(x)
                low = (x - high.astype(f32) - mid.astype(f32)).astype(bf16)
                return dot(tri, high) + dot(tri, mid) + dot(tri, low)

            g_logs = sums(at_most, ahead[rows, :]) + sums(below, behind[rows, :]) + carry[c : c + 1, :]
            heads = dt_slope.shape[1]
            g_dt = (direct[rows, :] + g_logs * decays[...])[:, :heads] * dt_slope[rows, :]
            ldt_out[rows, :] = g_dt.astype(bf16)
            g_scores = ds[c] * allowed[c]
            low_ds = g_scores.astype(bf16)
            gc = dc[rows, :] + dot(low_ds, in_b[rows, :])
            gb = db[rows, :] + dot_tn(low_ds, in_c[rows, :])
            g_bc = jnp.concatenate([gb, gc], axis=1)
            _, slope = silu_parts(u_bc[rows, :])
            gbc_out[rows, :] = g_bc * slope


def in_z_kernel(sel, lz, own_a, oth_a, own_b, oth_b, a_up, rank_in, acc, g_rank, p_up):
    @pl.when(pl.program_id(0) == 0)
    def _():
        acc[...] = jnp.zeros_like(acc)
        g_rank[...] = jnp.zeros_like(g_rank)

    g_rank[...] += dot_nt(lz[...], a_up[...])
    p_up[...] = dot2_tn(rank_in[...], lz[...])
    add_times_transposed(acc, lz, (own_a, oth_a, own_b, oth_b))


def conv_back(cur, params, masks, rows, width):
    total = params[3:4, :] * cur[:chunk]
    for k in range(1, 4):
        shifted = pltpu.roll(cur, cur.shape[0] - k, 0)[:chunk]
        total = total + params[3 - k : 4 - k, :] * (shifted * tile_lanes(masks[k - 1, rows, :], width))
    return total


def in_x_kernel(sel, gu, halo, own_a, oth_a, own_b, oth_b, a_up, rank_in, params, masks, acc_z, g_rank_z,
                gbc, halo_bc, params_bc, w_bc, ldt, w_dt, a_down, normed, tokens, cot, norm_gain,
                grad, p_up, p_down, acc, g_rank, low, lbc, small):
    g = pl.program_id(0)

    @pl.when(g == 0)
    def _():
        acc[...] = acc_z[...]
        g_rank[...] = g_rank_z[...]

    own, width = gu.shape
    step = min(width, 256)
    blocks = own // chunk
    for c in range(blocks):
        rows = rows_of(c)
        for n in range(width // step):
            cols = slice(n * step, (n + 1) * step)
            if c < blocks - 1:
                cur = gu[c * chunk : (c + 1) * chunk + 8, cols]
            else:
                cur = jnp.concatenate([gu[rows, cols], halo[:, cols].astype(f32)[:8]], axis=0)
            low[rows, cols] = conv_back(cur, params[:, cols], masks, rows, step).astype(bf16)
    g_rank[...] += dot_nt(low[...], a_up[...])
    p_up[...] = dot2_tn(rank_in[...], low[...])
    add_times_transposed(acc, low, (own_a, oth_a, own_b, oth_b))

    @pl.when(g == pl.num_programs(0) - 1)
    def _():
        for c in range(blocks):
            rows = rows_of(c)
            if c < blocks - 1:
                cur = gbc[c * chunk : (c + 1) * chunk + 8, :]
            else:
                cur = jnp.concatenate([gbc[rows, :], halo_bc[...].astype(f32)[:8]], axis=0)
            lbc[rows, :] = conv_back(cur, params_bc[...], masks, rows, gbc.shape[1]).astype(bf16)
        small[...] = (
            dot_nt(lbc[...], w_bc[...]) + dot_nt(ldt[...], w_dt[...]) + dot2_nt(g_rank[...], a_down[...])
        )
        p_down[...] = dot2_tn(g_rank[...], normed[...])
        for k in range(8):
            at = pl.ds(pl.multiple_of(sel[k] * lanes, lanes), lanes)
            small[:, at] += acc[:, k * lanes : (k + 1) * lanes]
        for c in range(blocks):
            rows = rows_of(c)
            wide = tokens[rows, :].astype(f32)
            size = wide.shape[1]
            scale = lax.rsqrt(jnp.sum(wide * wide, axis=1, keepdims=True) / size + epsilon)
            g_norm = small[rows, :] * norm_gain[...]
            row_dot = jnp.sum(g_norm * wide, axis=1, keepdims=True)
            grad[rows, :] = (
                cot[rows, :].astype(f32) + g_norm * scale - wide * (scale * scale * scale * row_dot / size)
            )


def up(x):
    n = lax.axis_size("tensor")
    return lax.ppermute(x, "tensor", [(i, i + 1) for i in range(n - 1)])


def down(x):
    n = lax.axis_size("tensor")
    return lax.ppermute(x, "tensor", [(i + 1, i) for i in range(n - 1)])


def around_tensor(x):
    n = lax.axis_size("tensor")
    return jnp.stack(
        [x] + [lax.ppermute(x, "tensor", [(i, (i + s) % n) for i in range(n)]) for s in range(1, n)]
    )


def swap(x, bit):
    n = lax.axis_size("dp")
    return lax.ppermute(x, "dp", [(i, i ^ (1 << bit)) for i in range(n)])


def all_dp(x):
    n = lax.axis_size("dp")
    cur = x[None]
    for bit in range(n.bit_length() - 1):
        cur = jnp.concatenate([cur, swap(cur, bit)])
    return jnp.take(cur, jnp.arange(n) ^ lax.axis_index("dp"), axis=0)


def gather_weight(x):
    n, tp = lax.axis_size("dp"), lax.axis_size("tensor")
    rows, cols = x.shape
    half = cols // 2
    if rows % lanes == 0:
        placed = around_tensor(x)
        bits = list(range(1, n.bit_length() - 1))
        out = []
        for j in range(2):
            cur = placed[:, :, j * half : (j + 1) * half]
            cur = cur.reshape((1,) * len(bits) + cur.shape)
            for bit in bits if j == 0 else bits[::-1]:
                cur = jnp.concatenate([cur, swap(cur, bit)], axis=len(bits) - bit)
            cur = cur.reshape(-1, tp, rows, half)
            out += [cur, swap(cur, 0)]
        return out
    whole = lax.all_gather(x, ("dp", "tensor")).reshape(n, tp, rows, cols)
    whole = whole.transpose(1, 0, 2, 3).reshape(tp, 2, n * rows // 2, 2, half)
    return [whole[:, i, :, j][None] for j in range(2) for i in range(2)]


def shards(
    tokens,
    cotangent,
    doc_ids,
    adapter_pick,
    norm_gain,
    gate_x_weight,
    bc_weight,
    dt_weight,
    conv_x_weight,
    conv_bc_weight,
    conv_x_bias,
    conv_bc_bias,
    dt_bias,
    a_log,
    skip_gain,
    inner_gain,
    out_weight,
    in_down,
    in_up,
    out_down,
    out_up,
):
    dp_size, tp_size = lax.axis_size("dp"), lax.axis_size("tensor")
    both = ("dp", "tensor")
    seq_count, own, width = tokens.shape
    assert seq_count == 1 and width == 8 * lanes
    group = gate_x_weight.shape[2]
    inner = group * tp_size
    heads_part = dt_weight.shape[1]
    heads = heads_part * tp_size
    head_size = inner // heads
    assert head_size * 2 == lanes
    state = bc_weight.shape[1] // 2
    rank = in_down.shape[2]
    adapters = in_down.shape[0]
    hops = min(1 + (doc_most - 2) // own, tp_size - 1)
    blocks = own // chunk
    place, mine = lax.axis_index("tensor"), lax.axis_index("dp")

    d_rows = gate_x_weight.shape[0]
    if d_rows % lanes == 0:
        order = jnp.concatenate([jnp.arange(0, dp_size, 2), jnp.arange(1, dp_size, 2)]) ^ mine
        places = (place - jnp.arange(tp_size)) % tp_size
    else:
        order, places = jnp.arange(8), jnp.arange(tp_size)
    sel = jnp.concatenate([order, places]).astype(jnp.int32)

    wide_rows = jnp.concatenate(
        [conv_x_weight, conv_x_bias[None], inner_gain[None], jnp.repeat(skip_gain, head_size)[None],
         jnp.zeros((1, group), f32)]
    )
    flat = jnp.concatenate([wide_rows.reshape(-1), dt_bias, a_log, dt_weight.astype(f32).reshape(-1)])
    flat = around_tensor(flat)[(place - jnp.arange(tp_size)) % tp_size]
    cut0 = wide_rows.size
    params = flat[:, :cut0].reshape(tp_size, 8, group).transpose(1, 0, 2).reshape(8, inner)
    dt_shift = flat[:, cut0 : cut0 + heads_part].reshape(heads)
    decays = -jnp.exp(flat[:, cut0 + heads_part : cut0 + 2 * heads_part].reshape(heads))
    dt_cols = flat[:, cut0 + 2 * heads_part :].reshape(tp_size, d_rows, heads_part).transpose(1, 0, 2)
    small_w = jnp.concatenate([bc_weight, dt_cols.reshape(d_rows, heads).astype(bf16)], axis=1)
    small_w = all_dp(small_w).reshape(width, 2 * state + heads)
    w_bc, w_dt = small_w[:, : 2 * state], small_w[:, 2 * state :]

    picks = all_dp(adapter_pick).reshape(-1)
    one_hot = (picks[:, None] == jnp.arange(adapters)[None, :]).astype(bf16)
    sizes = [math.prod(t.shape[1:]) for t in (in_down, in_up, out_down, out_up)]
    tables = jnp.concatenate([t.reshape(adapters, -1) for t in (in_down, out_up, in_up, out_down)], 1)
    sent = jnp.dot(one_hot, tables, preferred_element_type=f32).astype(bf16)
    own_tables = lax.all_to_all(sent, "dp", 0, 0, tiled=True)
    cut = sizes[0] + sizes[3]
    a_down = own_tables[:, : sizes[0]].reshape(width, rank)
    b_up = own_tables[:, sizes[0] : cut].reshape(dp_size, rank, -1)
    b_up = b_up.transpose(1, 0, 2).reshape(rank, width)
    inner_tables = around_tensor(own_tables[:, cut:])[(place - jnp.arange(tp_size)) % tp_size]
    p_part = in_up.shape[4]
    a_up = inner_tables[:, :, : sizes[1]].reshape(tp_size, dp_size, rank, 2, heads_part, p_part)
    a_up = a_up.transpose(2, 3, 0, 4, 1, 5).reshape(rank, 2, inner)
    b_down = inner_tables[:, :, sizes[1] :].reshape(tp_size, dp_size, heads_part, p_part, rank)
    b_down = b_down.transpose(4, 0, 2, 1, 3).reshape(rank, inner)
    up_z, up_x = a_up[:, 0], a_up[:, 1]
    up_z2, up_x2 = jnp.concatenate([up_z, up_z]), jnp.concatenate([up_x, up_x])

    w_x = gather_weight(gate_x_weight[:, 1])
    w_z = gather_weight(gate_x_weight[:, 0])
    w_out = gather_weight(out_weight.T)

    docs = doc_ids[0]
    padded = jnp.concatenate([jnp.full((4,), -1, jnp.int32), docs, jnp.full((4,), -2, jnp.int32)])
    near = lax.dynamic_slice_in_dim(padded, place * own, own + 8)
    seg = near[4 : 4 + own]

    def masks_at(sign):
        rows = [(near[4 + sign * k : 4 + sign * k + own] == seg).astype(f32) for k in range(1, 4)]
        return jnp.broadcast_to(jnp.stack(rows)[:, :, None], (3, own, lanes))

    masks, masks_after = masks_at(-1), masks_at(1)
    before_seg, last_seg = near[3], near[own + 3]
    seg_c = seg.reshape(blocks, chunk)
    before_c = jnp.concatenate([before_seg[None], seg_c[:-1, -1]])
    last_c = seg_c[:, -1]
    at = jnp.arange(chunk)
    tril = (at[:, None] >= at[None, :]).astype(f32)
    allowed = (seg_c[:, :, None] == seg_c[:, None, :]).astype(f32) * tril

    wide = tokens[0].astype(f32)
    row_scale = lax.rsqrt(jnp.mean(wide * wide, axis=1, keepdims=True) + epsilon)
    normed = (wide * row_scale * norm_gain).astype(bf16)
    normed_ext = jnp.concatenate([up(normed[-edge:]), normed])
    rank_in = dot(normed_ext, a_down)
    ranks = pieces(rank_in, 2)
    bc_ext = dot(normed_ext, w_bc)
    dt_raw = dot(normed, w_dt) + dt_shift
    u_bc = conv_bc_weight[3] * bc_ext[edge:] + conv_bc_bias
    for k in range(1, 4):
        u_bc = u_bc + conv_bc_weight[3 - k] * (bc_ext[edge - k : edge - k + own] * masks[k - 1, :, :1])
    state_in = jax.nn.silu(u_bc)
    in_b, in_c = state_in[:, :state].astype(bf16), state_in[:, state:].astype(bf16)
    b_t, c_t = in_b.T, in_c.T
    scores = jnp.einsum(
        "cin,cjn->cij",
        in_c.reshape(blocks, chunk, state),
        in_b.reshape(blocks, chunk, state),
        preferred_element_type=f32,
    )
    scores = scores * allowed
    dt = jax.nn.softplus(dt_raw)
    dt_slope = jax.nn.sigmoid(dt_raw)

    logs = (dt * decays) * math.log2(math.e)
    cums = jnp.einsum("ij,cjh->cih", tril, logs.reshape(blocks, chunk, heads), precision=exact)
    ends = cums[:, -1]
    prior = jnp.concatenate([jnp.zeros((1, heads), f32), jnp.cumsum(ends, axis=0)[:-1]])
    whole_end = prior[-1] + ends[-1]
    cums_own = (cums + prior[:, None]).reshape(own, heads)
    e_in_own = jnp.exp2(cums_own) * (seg == before_seg).astype(f32)[:, None]
    e_out_own = jnp.exp2(whole_end - cums_own) * (seg == last_seg).astype(f32)[:, None]
    keep_own = jnp.exp2(whole_end) * (before_seg == last_seg).astype(f32)
    e_in = jnp.exp2(cums) * (seg_c == before_c[:, None]).astype(f32)[:, :, None]
    e_out = jnp.exp2(ends[:, None] - cums) * (seg_c == last_c[:, None]).astype(f32)[:, :, None]
    keep = jnp.exp2(ends) * (before_c == last_c).astype(f32)[:, None]
    keep = jnp.repeat(keep, head_size, axis=1)
    keep_row = jnp.repeat(keep_own, head_size)[None]
    dt2, ei_own2, eo_own2 = pieces(dt, 2), pieces(e_in_own, 2), pieces(e_out_own, 2)
    ei2, eo2 = pieces(e_in.reshape(own, heads), 2), pieces(e_out.reshape(own, heads), 2)
    cums3 = pieces(cums.reshape(own, heads), 3)
    cums_t = cums.reshape(blocks, chunk, tp_size, heads_part).transpose(2, 0, 3, 1)

    def spread(width_each, copies):
        head = jnp.arange(heads)[:, None]
        cols = jnp.arange(heads * width_each)[None, :] // width_each
        return jnp.tile((head == cols).astype(bf16), (copies, 1))

    ex, exl = spread(head_size, 2), spread(lanes, 3)
    red = (jnp.arange(inner)[:, None] // head_size == jnp.arange(lanes)[None, :]).astype(bf16)

    def full(*shape):
        return pl.BlockSpec(shape, lambda g, *s: (0,) * len(shape))

    def cols(rows, size=group):
        return pl.BlockSpec((rows, size), lambda g, *s: (0, g))

    def weight(w):
        q, _, rows, half = w.shape
        return pl.BlockSpec((q, 1, rows, half), lambda g, s: (0, s[8 + g], 0, 0))

    def call(kernel, out, in_specs, out_specs, scratch, prefetch, flops, moved):
        return pl.pallas_call(
            kernel,
            out_shape=[jax.ShapeDtypeStruct(s, d) for s, d in out],
            grid_spec=pltpu.PrefetchScalarGridSpec(
                num_scalar_prefetch=prefetch,
                grid=(tp_size,),
                in_specs=in_specs,
                out_specs=out_specs,
                scratch_shapes=scratch,
            ),
            compiler_params=pltpu.CompilerParams(
                dimension_semantics=("arbitrary",), vmem_limit_bytes=vmem_bytes
            ),
            cost_estimate=pl.CostEstimate(flops=flops, bytes_accessed=moved, transcendentals=0),
        )

    big = (own, inner)
    ext = own + edge
    mat = 2 * own * width * inner
    mega = 1 << 20
    chunk_rows = pl.BlockSpec((1, blocks, heads_part, chunk), lambda g, *s: (g, 0, 0, 0))
    w_specs = [weight(w) for w in w_x]
    p_spec = cols(8)
    u, scaled, sent_state = call(
        proj_kernel,
        [(big, f32), (big, bf16), ((state, inner), bf16)],
        [full(ext, width)] + w_specs
        + [full(ext, 2 * rank), cols(2 * rank), p_spec, full(3, own, lanes), full(own, 2 * heads),
           full(own, 2 * heads), cols(2 * heads), full(state, own)],
        [cols(own), cols(own), cols(state)],
        [pltpu.VMEM((ext, width), bf16), pltpu.VMEM((ext, group), f32), pltpu.VMEM((own, group), bf16)],
        1, mat, 12 * mega,
    )(sel, normed_ext, *w_x, ranks, up_x2, params, masks, dt2, eo_own2, ex, b_t)

    def pass_on(x, step):
        moving, total = x, jnp.zeros(x.shape, f32)
        for hop in range(hops):
            moving = step(moving)
            total = total + moving.astype(f32)
            if hop < hops - 1:
                moving = (moving.astype(f32) * keep_row).astype(bf16)
        return total

    state_first = pass_on(sent_state, up)

    within_specs = [cols(own), full(own, 3 * heads), chunk_rows, full(blocks, chunk, chunk),
                    cols(3 * heads, heads_part * lanes)]
    (y_within,) = call(
        within_kernel, [(big, f32)], within_specs, [cols(own)], [], 0, mat, 6 * mega
    )(scaled, cums3, cums_t, scores, exl)

    y, z, gated, states, sumsq = call(
        gate_kernel,
        [(big, f32), (big, f32), (big, f32), ((blocks, state, inner), bf16), ((own, lanes), f32)],
        [full(own, width)] + w_specs
        + [full(own, 2 * rank), cols(2 * rank), p_spec, cols(own), cols(own), cols(own), cols(state),
           full(own, 2 * heads), full(own, 2 * heads), cols(blocks), cols(2 * heads), full(state, own),
           full(own, state)],
        [cols(own), cols(own), cols(own),
         pl.BlockSpec((blocks, state, group), lambda g, *s: (0, 0, g)), full(own, lanes)],
        [pltpu.VMEM((own, width), bf16)],
        1, mat, 24 * mega,
    )(sel, normed, *w_z, ranks[edge:], up_z2, params, y_within, u, scaled, state_first, ei2, eo2, keep, ex,
      b_t, in_c)

    def with_inner(kernel):
        def body(*refs):
            return kernel(*refs, inner=inner)

        return body

    cot, tok = cotangent[0], tokens[0]
    gg, mixed, p_out_down, p_out_up, dots = call(
        with_inner(out_kernel),
        [(big, f32), ((own, width), f32), ((rank, inner), f32), ((rank, width), f32), ((own, lanes), f32)],
        [cols(own)] + w_specs
        + [p_spec, full(own, lanes), full(own, width), full(own, width), full(rank, width), cols(rank)],
        [cols(own), full(own, width), cols(rank), full(rank, width), full(own, lanes)],
        [pltpu.VMEM((own, width), f32), pltpu.VMEM((own, width), bf16), pltpu.VMEM((own, rank), f32),
         pltpu.VMEM((own, rank), f32), pltpu.VMEM((own, group), bf16)],
        1, 2 * mat, 14 * mega,
    )(sel, gated, *w_out, params, sumsq, cot, tok, b_up, b_down)

    g_heads, low_z, sent_grad = call(
        with_inner(split_kernel),
        [(big, f32), (big, bf16), ((state, inner), bf16)],
        [cols(own)] * 5
        + [p_spec, full(own, lanes), full(own, lanes), full(own, 2 * heads), cols(2 * heads), full(state, own)],
        [cols(own), cols(own), cols(state)],
        [pltpu.VMEM((own, group), bf16)],
        0, mat // 8, 28 * mega,
    )(gg, gated, y, u, z, params, sumsq, dots, ei_own2, ex, c_t)
    g_state_last = pass_on(sent_grad, down)

    d_within, d_scores, ahead = call(
        back_within_kernel,
        [(big, f32), ((blocks, chunk, chunk), f32), ((own, lanes), f32)],
        [cols(own), cols(own)] + within_specs + [pl.BlockSpec((group, lanes), lambda g, *s: (g, 0))],
        [cols(own), full(blocks, chunk, chunk), full(own, lanes)],
        [pltpu.VMEM((chunk, group), f32)],
        0, 2 * mat, 14 * mega,
    )(g_heads, y, scaled, cums3, cums_t, scores, exl, red)

    rank_own = rank_in[edge:]
    acc_z, g_rank_z, p_up_z = call(
        in_z_kernel,
        [((own, width), f32), ((own, rank), f32), ((rank, inner), f32)],
        [cols(own)] + w_specs + [cols(rank), full(own, rank)],
        [full(own, width), full(own, rank), cols(rank)],
        [],
        1, mat, 8 * mega,
    )(sel, low_z, *w_z, up_z, rank_own)

    decay_row = jnp.pad(decays, (0, lanes - heads))[None]
    g_u, g_u_bc, low_dt = call(
        back_state_kernel,
        [(big, f32), ((own, 2 * state), f32), ((own, heads), bf16)],
        [cols(state), pl.BlockSpec((blocks, state, group), lambda g, *s: (0, 0, g)), cols(own), cols(own),
         cols(own), cols(own), p_spec, full(own, state), full(own, state), full(state, own), full(state, own),
         full(own, 2 * heads), full(own, 2 * heads), full(own, 2 * heads), cols(blocks), cols(2 * heads),
         pl.BlockSpec((group, lanes), lambda g, *s: (g, 0)), full(blocks, chunk, chunk), full(own, lanes),
         full(blocks, chunk, chunk), full(own, 2 * state), full(own, heads), full(1, lanes)],
        [cols(own), full(own, 2 * state), full(own, heads)],
        [pltpu.VMEM((own, state), f32), pltpu.VMEM((own, state), f32), pltpu.VMEM((own, lanes), f32),
         pltpu.VMEM((own, lanes), f32), pltpu.VMEM((8, lanes), f32), pltpu.VMEM((8, lanes), f32)],
        0, mat, 24 * mega,
    )(g_state_last, states, g_heads, scaled, d_within, u, params, in_b, in_c, b_t, c_t, dt2, ei2, eo2, keep,
      ex, red, d_scores, ahead, allowed, u_bc, dt_slope, decay_row)

    halo = down(jnp.concatenate([g_u[:edge], g_u_bc[:edge]], axis=1).astype(bf16))
    params_bc = jnp.concatenate([conv_bc_weight, jnp.zeros((4, 2 * state), f32)])
    tokens_grad, p_up_x, p_in_down = call(
        in_x_kernel,
        [((own, width), f32), ((rank, inner), f32), ((rank, width), f32)],
        [cols(own), cols(edge)] + w_specs
        + [cols(rank), full(own, rank), p_spec, full(3, own, lanes), full(own, width), full(own, rank),
           full(own, 2 * state), full(edge, 2 * state), full(8, 2 * state), full(width, 2 * state),
           full(own, heads), full(width, heads), full(width, rank), full(own, width), full(own, width),
           full(own, width), full(1, width)],
        [full(own, width), cols(rank), full(rank, width)],
        [pltpu.VMEM((own, width), f32), pltpu.VMEM((own, rank), f32), pltpu.VMEM((own, group), bf16),
         pltpu.VMEM((own, 2 * state), bf16), pltpu.VMEM((own, width), f32)],
        1, mat, 14 * mega,
    )(sel, g_u, halo[:, :inner], *w_x, up_x, rank_own, params, masks_after, acc_z, g_rank_z, g_u_bc,
      halo[:, inner:], params_bc, w_bc, low_dt, w_dt, a_down, normed, tok, cot, norm_gain[None])

    def deliver(parts):
        parts = jnp.concatenate(parts, axis=2).astype(bf16).reshape(dp_size * tp_size, -1)
        arrived = lax.all_to_all(parts, both, 0, 0, tiled=True)
        arrived = arrived.reshape(dp_size, tp_size, -1).astype(f32).sum(1)
        return jnp.dot(one_hot.astype(f32).T, arrived, precision=exact)

    def by_width(part):
        part = part.reshape(rank, dp_size, 1, -1).transpose(1, 2, 0, 3)
        return jnp.broadcast_to(part, (dp_size, tp_size) + part.shape[2:]).reshape(dp_size, tp_size, -1)

    def by_inner(part):
        part = part.reshape(rank, -1, tp_size, heads_part, dp_size, p_part)
        return part.transpose(4, 2, 0, 1, 3, 5).reshape(dp_size, tp_size, -1)

    out_grads = deliver([by_width(p_out_up), by_inner(p_out_down)])
    in_grads = deliver([by_width(p_in_down), by_inner(jnp.stack([p_up_z, p_up_x], axis=1))])
    grad_out_up = out_grads[:, : sizes[3]].reshape(out_up.shape)
    grad_out_down = out_grads[:, sizes[3] :].reshape(adapters, rank, heads_part, p_part).transpose(0, 2, 3, 1)
    grad_in_down = in_grads[:, : sizes[0]].reshape(adapters, rank, d_rows).transpose(0, 2, 1)
    grad_in_up = in_grads[:, sizes[0] :].reshape(in_up.shape)
    return (mixed[None], tokens_grad[None], grad_in_down, grad_in_up, grad_out_down, grad_out_up)


def solution(mesh):
    placed = (
        P("dp", "tensor", None),
        P("dp", "tensor", None),
        P("dp", None),
        P("dp"),
        P(),
        P("dp", None, "tensor"),
        P("dp", None),
        P("dp", "tensor"),
        P(None, "tensor"),
        P(),
        P("tensor"),
        P(),
        P("tensor"),
        P("tensor"),
        P("tensor"),
        P("tensor"),
        P("tensor", "dp"),
        P(None, "dp", None),
        P(None, None, None, "tensor", "dp"),
        P(None, "tensor", "dp", None),
        P(None, None, "dp"),
    )
    return jax.shard_map(
        shards,
        mesh=mesh,
        in_specs=placed,
        out_specs=(
            P("dp", "tensor", None),
            P("dp", "tensor", None),
            P(None, "dp", None),
            P(None, None, None, "tensor", "dp"),
            P(None, "tensor", "dp", None),
            P(None, None, "dp"),
        ),
        check_vma=False,
    )
```

```python
import math

import jax
import jax.numpy as jnp
import numpy as np
from jax import lax
from jax.experimental import pallas as pl
from jax.experimental.pallas import tpu as pltpu
from jax.sharding import PartitionSpec as P

epsilon = 1e-05
chunk = 128
lanes = 128
doc_most = 800
edge = 16
f32, bf16 = jnp.float32, jnp.bfloat16
exact = lax.Precision.HIGHEST
vmem_bytes = 48 * 1024 * 1024


def dot(a, b):
    return jnp.dot(a, b, preferred_element_type=f32)


def dot_nt(a, b):
    return lax.dot_general(a, b, (((1,), (1,)), ((), ())), preferred_element_type=f32)


def dot_tn(a, b):
    return lax.dot_general(a, b, (((0,), (0,)), ((), ())), preferred_element_type=f32)


def halves(x):
    high = x.astype(bf16)
    return high, (x - high.astype(f32)).astype(bf16)


def pieces(x, count):
    out = []
    for _ in range(count):
        part = lax.reduce_precision(x, 8, 7)
        out.append(part.astype(bf16))
        x = x - part
    return jnp.concatenate(out, axis=-1)


def dot2(x, w):
    high, low = halves(x)
    return dot(high, w) + dot(low, w)


def dot2_nt(x, w):
    high, low = halves(x)
    return dot_nt(high, w) + dot_nt(low, w)


def dot2_tn(x, w):
    high, low = halves(x)
    return dot_tn(high, w) + dot_tn(low, w)


def tile_lanes(m, width):
    return m if width == lanes else jnp.concatenate([m] * (width // lanes), axis=1)


def sigmoid(u):
    return 0.5 + 0.5 * jnp.tanh(0.5 * u)


def silu(u):
    return u * sigmoid(u)


def silu_parts(u):
    s = sigmoid(u)
    v = u * s
    return v, s + v * (1.0 - s)


korder = (0, 2, 4, 6, 1, 3, 5, 7)


def weight_pieces(refs, at=0):
    if len(refs) == 1:
        return [refs[0][...].reshape(-1, refs[0].shape[-1])]
    a01, a23, c01, c23 = (refs[4 * at + j] for j in range(4))
    if at == 0:
        parts = [a01[0, 0], a01[1, 0], a23[0, 0], a23[1, 0], c01[0, 0], c01[1, 0], c23[0, 0], c23[1, 0]]
    else:
        parts = [a01[0, 0], a23[0, 0], a01[1, 0], a23[1, 0], c01[0, 0], c23[0, 0], c01[1, 0], c23[1, 0]]
    return [jnp.concatenate(parts[j : j + 2], axis=0) for j in range(0, 8, 2)]


def with_weight(refs, body, half):
    if len(refs) == 1:
        body(weight_pieces(refs))
        return
    if isinstance(half, int):
        body(weight_pieces(refs * 2, half))
        return

    @pl.when(half == 0)
    def _():
        body(weight_pieces(refs, 0))

    @pl.when(half == 1)
    def _():
        body(weight_pieces(refs, 1))


def times(left, parts):
    total, k = None, 0
    for w in parts:
        term = dot(left[:, k : k + w.shape[0]], w)
        total = term if total is None else total + term
        k += w.shape[0]
    return total


def add_times_transposed(acc, low, parts):
    k = 0
    for w in parts:
        acc[:, k : k + w.shape[0]] += dot_nt(low, w)
        k += w.shape[0]


def rows_of(c):
    return slice(c * chunk, (c + 1) * chunk)


def sums3(tri, x):
    high, mid = halves(x)
    low = (x - high.astype(f32) - mid.astype(f32)).astype(bf16)
    return dot(tri, high) + dot(tri, mid) + dot(tri, low)


def parts_of(x, count):
    out = []
    for _ in range(count):
        part = x.astype(bf16)
        out.append(part)
        x = x - part.astype(f32)
    return jnp.concatenate(out, axis=1)


def table_of(x, count):
    parts = parts_of(x, count)
    return jnp.concatenate([parts, jnp.zeros((x.shape[0], lanes - parts.shape[1]), bf16)], axis=1)


def column(row):
    return jnp.broadcast_to(row, (lanes, lanes)).T


def prep_kernel(sel, tokens, halo, norm_gain, small, dt_t, inner_t, place, params, params_bc, segs, ex, no_out,
                normed, ranks, ranks_own, tables, bc_out, bct_out, scores, rows_out, cums_t, keep, ups, wides, w_bc,
                masks, ext, *, rank, state, moved_blocks):
    own, width = tokens.shape
    blocks = own // chunk
    tp, _, group = params.shape
    heads = dt_t.shape[0]
    part = heads // tp
    bc_rows = 2 * lanes
    turn, pick, bound, small_at = 8 + tp, sel[8 + 2 * tp], 9 + 2 * tp, 9 + 2 * tp + 2 * blocks

    for c in range(blocks):
        wide = tokens[rows_of(c), :].astype(f32)
        scale = lax.rsqrt(jnp.sum(wide * wide, axis=1, keepdims=True) / width + epsilon)
        ext[edge + c * chunk : edge + (c + 1) * chunk, :] = (wide * scale * norm_gain[...]).astype(bf16)
    ext[:edge, :] = halo[...]
    for j in range(8):
        k = korder[j]
        at = pl.ds(pl.multiple_of(sel[k] * lanes, lanes), lanes)
        cols = slice(j * lanes, (j + 1) * lanes)
        no_out[:, cols] = ext[:, at]
        at = sel[small_at + j]
        wides[:, cols] = small[at, pl.ds(pl.multiple_of(bc_rows + pick * 2 * rank, 2 * rank), 2 * rank), :]
        w_bc[j * lanes : (j + 1) * lanes, :state] = small[at, :lanes, :]
        w_bc[j * lanes : (j + 1) * lanes, state:] = small[at, lanes : 2 * lanes, :]
    normed[...] = ext[edge:, :]
    ranks[...] = parts_of(dot_nt(ext[...], wides[:rank, :]), 2)
    ranks_own[...] = ranks[edge:, :]
    bc = dot(ext[...], w_bc[...])

    hp = place.shape[1]
    for s in range(tp):
        cols = slice(s * group, (s + 1) * group)
        z = x = d = None
        for k in range(inner_t.shape[1]):
            where = place[sel[korder[k]]] if moved_blocks else place[k]
            piece = inner_t[sel[turn + s], k]
            terms = (dot(piece[:rank, :hp], where), dot(piece[:rank, hp : 2 * hp], where),
                     dot(piece[rank:, :hp], where))
            z, x, d = terms if z is None else (z + terms[0], x + terms[1], d + terms[2])
        z, x = z.astype(bf16), x.astype(bf16)
        ups[:, cols] = jnp.concatenate([z, z, x, x, d.astype(bf16)], axis=0)

    i = lax.broadcasted_iota(jnp.int32, (chunk, chunk), 0)
    j = lax.broadcasted_iota(jnp.int32, (chunk, chunk), 1)
    tril = jnp.where(j <= i, 1.0, 0.0)
    segs_at = []
    for c in range(blocks):
        rows = rows_of(c)
        seg = column(segs[3, c : c + 1, :])
        segs_at.append(seg[:, :heads])
        for k in range(1, 4):
            masks[k - 1, rows, :] = jnp.where(column(segs[3 - k, c : c + 1, :]) == seg, 1.0, 0.0)
            masks[k + 2, rows, :] = jnp.where(column(segs[3 + k, c : c + 1, :]) == seg, 1.0, 0.0)
        cur = bc[edge + c * chunk - 8 : edge + (c + 1) * chunk]
        total = params_bc[3:4, :] * cur[8:] + params_bc[4:5, :]
        for k in range(1, 4):
            shifted = pltpu.roll(cur, k, 0)[8:]
            total = total + params_bc[3 - k : 4 - k, :] * (
                shifted * tile_lanes(masks[k - 1, rows, :], 2 * state)
            )
        rows_out[rows, : 2 * state] = total
        value = silu(total)
        inb, inc = value[:, :state], value[:, state:]
        bc_out[rows, :] = value.astype(bf16)
        bct_out[:state, rows] = inb.T.astype(bf16)
        bct_out[state:, rows] = inc.T.astype(bf16)
        okay = jnp.where(seg == segs[3, c : c + 1, :], tril, 0.0)
        scores[1, c] = okay
        scores[0, c] = dot_nt(inc.astype(bf16), inb.astype(bf16)) * okay

    bias = jnp.concatenate([params[sel[turn + s], 7:8, :part] for s in range(tp)], axis=1)
    a_log = jnp.concatenate([params[sel[turn + s], 7:8, part : 2 * part] for s in range(tp)], axis=1)
    decays = -jnp.exp(a_log)
    raw = dot_nt(ext[edge:, :], dt_t[...]) + bias
    dt = jnp.maximum(raw, 0.0) + jnp.log1p(jnp.exp(-jnp.abs(raw)))
    rows_out[:, 2 * state :] = jnp.concatenate([sigmoid(raw), jnp.zeros((own, lanes - heads), f32)], axis=1)
    tables[:, :lanes] = table_of(dt, 2)
    logs = dt * decays * math.log2(math.e)
    bounds = [sel[bound + n].astype(f32) for n in range(2 * blocks)]
    before_seg, last_seg = bounds[0], bounds[-1]
    prior = jnp.zeros((1, heads), f32)
    all_cums, keeps = [], []
    tri = tril.astype(bf16)
    for c in range(blocks):
        rows = rows_of(c)
        before_c, last_c = bounds[2 * c], bounds[2 * c + 1]
        cums = sums3(tri, logs[rows])
        end = cums[chunk - 1 : chunk]
        seg = segs_at[c]
        tables[rows, 5 * lanes :] = table_of(cums, 3)
        flipped = jnp.concatenate([cums, jnp.zeros((chunk, lanes - heads), f32)], axis=1).T
        for s in range(tp):
            cums_t[s, c] = flipped[s * part : (s + 1) * part]
        tables[rows, 2 * lanes : 3 * lanes] = table_of(jnp.where(seg == before_c, jnp.exp2(cums), 0.0), 2)
        tables[rows, 3 * lanes : 4 * lanes] = table_of(jnp.where(seg == last_c, jnp.exp2(end - cums), 0.0), 2)
        keeps.append(jnp.where(before_c == last_c, jnp.exp2(end), 0.0))
        all_cums.append(cums + prior)
        prior = prior + end
    for c in range(blocks):
        rows = rows_of(c)
        seg = segs_at[c]
        tables[rows, 4 * lanes : 5 * lanes] = table_of(jnp.where(seg == before_seg, jnp.exp2(all_cums[c]), 0.0), 2)
        tables[rows, lanes : 2 * lanes] = table_of(jnp.where(seg == last_seg, jnp.exp2(prior - all_cums[c]), 0.0), 2)
    whole = jnp.where(before_seg == last_seg, jnp.exp2(prior), 0.0)
    table = jnp.concatenate(keeps + [jnp.zeros((7 - blocks, heads), f32), whole], axis=0)
    high, mid = halves(table)
    low = (table - high.astype(f32) - mid.astype(f32)).astype(bf16)
    spread = ex[:heads, :]
    keep[...] = dot(high, spread) + dot(mid, spread) + dot(low, spread)
    keep[6:7, :lanes] = jnp.concatenate([decays, jnp.zeros((1, lanes - heads), f32)], axis=1)


def pack_kernel(bc, dt_weight, in_down, out_up, in_up, out_down, pick, out):
    rows, two = bc.shape
    part = dt_weight.shape[0]
    count, rank, _ = in_down.shape
    at = 2 * rows
    out[:rows, :] = bc[:, : two // 2]
    out[rows:at, :] = bc[:, two // 2 :]
    for b in range(count):
        out[at + 2 * rank * b : at + 2 * rank * b + rank, :] = in_down[b]
        out[at + 2 * rank * b + rank : at + 2 * rank * (b + 1), :] = out_up[b]
    at += 2 * rank * count
    for b in range(count):
        out[at + 2 * rank * b : at + 2 * rank * b + rank, :] = in_up[b].astype(f32).T.astype(bf16)
        flipped = out_down[b].astype(f32).T
        out[at + 2 * rank * b + rank : at + 2 * rank * (b + 1), :] = jnp.concatenate(
            [flipped, jnp.zeros_like(flipped)], axis=1
        ).astype(bf16)
    at += 2 * rank * count
    wide = jnp.concatenate([dt_weight[...].astype(f32), jnp.zeros((16 - part, rows), f32)], axis=0)
    out[at : at + 16, :] = wide.astype(bf16)
    out[at + 16 : at + 32, :] = jnp.zeros((16, lanes), bf16) + pick[0].astype(f32).astype(bf16)


def proj_kernel(left, *refs, weights):
    refs, ws = refs[weights:], refs[:weights]
    ranks, a_up, params, masks, tables, ex, b_t, u_out, sc_out, f_out, xs, moved = refs

    def body(parts):
        xs[...] = times(left, parts) + dot(ranks[...], a_up[...])

    with_weight(ws, body, pl.program_id(0) // 2)
    own, width = u_out.shape
    step = min(width, 256)
    for c in range(own // chunk):
        rows = rows_of(c)
        for n in range(width // step):
            cols = slice(n * step, (n + 1) * step)
            cur = xs[edge + c * chunk - 8 : edge + (c + 1) * chunk, cols]
            total = params[0, 3:4, cols] * cur[8:] + params[0, 4:5, cols]
            for k in range(1, 4):
                shifted = pltpu.roll(cur, k, 0)[8:]
                total = total + params[0, 3 - k : 4 - k, cols] * (
                    shifted * tile_lanes(masks[k - 1, rows, :], step)
                )
            u_out[rows, cols] = total
            value = silu(total)
            scaled = (dot(tables[rows, :lanes], ex[:, cols]) * value).astype(bf16)
            sc_out[rows, cols] = scaled
            moved[rows, cols] = (dot(tables[rows, lanes:], ex[:, cols]) * scaled.astype(f32)).astype(bf16)
    f_out[...] = dot(b_t[...], moved[...]).astype(bf16)

def pair_parts(lcol, cums_t, p):
    lc = lcol[:, p * 2 * lanes : (p + 1) * 2 * lanes]
    lr = jnp.concatenate([cums_t[2 * p : 2 * p + 1, :], cums_t[2 * p + 1 : 2 * p + 2, :]], axis=1)
    return jnp.exp2(jnp.minimum(lc - lr, 0.0))


def two_heads(v, head_size):
    lane = lax.broadcasted_iota(jnp.int32, v.shape, 1)
    zero = jnp.zeros_like(v)
    return jnp.concatenate([jnp.where(lane < head_size, v, zero), jnp.where(lane < head_size, zero, v)], 0)


def within_kernel(sc, cums3, cums_t, scores, exl, y_out):
    own, width = y_out.shape
    for c in range(own // chunk):
        rows = rows_of(c)
        lcol = dot(cums3[rows, :], exl[...])
        allowed = tile_lanes(scores[0, c], 2 * lanes)
        for p in range(width // lanes):
            e = pair_parts(lcol, cums_t[0, c], p)
            m = (e * allowed).astype(bf16)
            cols = slice(p * lanes, (p + 1) * lanes)
            y_out[rows, cols] = dot(m, two_heads(sc[rows, cols], lanes // 2))


def row_scale_of(sumsq, inner):
    return lax.rsqrt(jnp.sum(sumsq, axis=1, keepdims=True) / inner + epsilon)


def put_width_parts(sent, value):
    rank = value.shape[0]
    dp, tp, _, _ = sent.shape
    size = value.shape[1] // dp
    for d in range(dp):
        piece = value[:, d * size : (d + 1) * size].astype(bf16)
        for t in range(tp):
            sent[d, t, :rank, :size] = piece


def put_inner_parts(sent, to, value, order, offset):
    rank = value.shape[0]
    dp = sent.shape[0]
    hp = value.shape[1] // dp
    moved = dot(value.astype(bf16), order[...]).astype(bf16)
    for d in range(dp):
        sent[d, to, rank : 2 * rank, offset : offset + hp] = moved[:, d * hp : (d + 1) * hp]


def middle_kernel(sel, left, *refs, weights, hops, inner):
    zs, outs, refs = refs[:weights], refs[weights : 2 * weights], refs[2 * weights :]
    s_ins, refs = refs[:hops], refs[hops:]
    (ranks, a_up, params, yw, u, sc, tables, own_in, keep, ex, b_t, c_t, in_c, cot, tokens, b_up, b_down, order,
     y_out, states, mixed, sent, gh_out, lz_out, g_out,
     heads, gate_z, gated, gg, sumsq, dots, acc, cots, g_rank, rank, low) = refs
    phase, g = pl.program_id(0), pl.program_id(1)
    last = pl.num_programs(1) - 1
    half = g // 2
    own, width = y_out.shape
    step = min(width, 256)
    blocks = own // chunk

    @pl.when((phase == 0) & (g == 0))
    def _():
        sumsq[...] = jnp.zeros_like(sumsq)
        acc[...] = jnp.zeros_like(acc)
        rank[...] = jnp.zeros_like(rank)
        dots[...] = jnp.zeros_like(dots)
        sent[...] = jnp.zeros_like(sent)
        for j in range(8):
            at = pl.ds(pl.multiple_of(sel[korder[j]] * lanes, lanes), lanes)
            cots[:, j * lanes : (j + 1) * lanes] = cot[:, at]
        g_rank[...] = dot_nt(cot[...], b_up[...])

    @pl.when(phase == 0)
    def _():
        def body(parts):
            gate_z[g] = times(left[left.shape[0] - own :, :], parts) + dot(ranks[...], a_up[...])

        with_weight(zs, body, half)
        for n in range(width // step):
            cols = slice(n * step, (n + 1) * step)
            new = []
            for c in range(blocks):
                rows = rows_of(c)
                moved = (dot(tables[rows, lanes:], ex[:, cols]) * sc[rows, cols].astype(f32)).astype(bf16)
                new.append(dot(b_t[:, rows], moved))
            s = sum(r[:, cols].astype(f32) for r in s_ins)
            for c in range(blocks):
                states[c, :, cols] = s.astype(bf16)
                s = s * keep[c : c + 1, cols] + new[c]
            for c in range(blocks):
                rows = rows_of(c)
                y = yw[rows, cols] + dot(tables[rows, :lanes], ex[:, cols]) * dot(in_c[rows, :], states[c, :, cols])
                y_out[rows, cols] = y
                head = y + params[0, 6:7, cols] * silu(u[rows, cols])
                heads[g, rows, cols] = head
                gd = head * silu(gate_z[g, rows, cols])
                gated[g, rows, cols] = gd
                sq = gd * gd
                total = sumsq[rows, :]
                for i in range(step // lanes):
                    total = total + sq[:, i * lanes : (i + 1) * lanes]
                sumsq[rows, :] = total

    @pl.when(phase == 1)
    def _():
        scale = row_scale_of(sumsq[...], inner)
        normed_inner = gated[g] * scale * params[0, 5:6, :]
        high, rest = halves(normed_inner)
        low[...] = high
        rank[...] += dot_nt(high, b_down[...]) + dot_nt(rest, b_down[...])
        r_high, r_low = halves(g_rank[...])
        p_down = dot_tn(r_high, high) + dot_tn(r_low, high) + dot_tn(r_high, rest)
        put_inner_parts(sent, sel[8 + g], p_down, order, 0)

        def body(parts):
            value = (times(cots, parts) + dot2(g_rank[...], b_down[...])) * params[0, 5:6, :]
            gg[g] = value
            prod = value * gated[g]
            total = dots[...]
            for i in range(width // lanes):
                total = total + prod[:, i * lanes : (i + 1) * lanes]
            dots[...] = total
            add_times_transposed(acc, low[...], parts)

        with_weight(outs, body, half)

    @pl.when((phase == 1) & (g == last))
    def _():
        put_width_parts(sent, dot2_tn(rank[...], cot[...]))
        mixed[...] = tokens[...].astype(f32) + dot2(rank[...], b_up[...])
        for j in range(8):
            at = pl.ds(pl.multiple_of(sel[korder[j]] * lanes, lanes), lanes)
            mixed[:, at] += acc[:, j * lanes : (j + 1) * lanes]

    @pl.when(phase == 2)
    def _():
        scale = row_scale_of(sumsq[...], inner)
        coef = scale * scale * scale * (jnp.sum(dots[...], axis=1, keepdims=True) / inner)
        for c in range(blocks):
            rows = rows_of(c)
            sc_rows, co_rows = scale[rows], coef[rows]
            for n in range(width // step):
                cols = slice(n * step, (n + 1) * step)
                g_gated = gg[g, rows, cols] * sc_rows - gated[g, rows, cols] * co_rows
                gate, slope = silu_parts(gate_z[g, rows, cols])
                lz_out[rows, cols] = (g_gated * heads[g, rows, cols] * slope).astype(bf16)
                gh = g_gated * gate
                gh_out[rows, cols] = gh
                low[rows, cols] = (dot(own_in[rows, :], ex[:, cols]) * gh).astype(bf16)
        g_out[...] = dot(c_t[...], low[...]).astype(bf16)


def back_within_kernel(gh, y, sc, cums3, cums_t, scores, exl, red, dv_out, ds_out, ahead, prod):
    g = pl.program_id(0)

    @pl.when(g == 0)
    def _():
        ds_out[...] = jnp.zeros_like(ds_out)
        ahead[...] = jnp.zeros_like(ahead)

    own, width = dv_out.shape
    for c in range(own // chunk):
        rows = rows_of(c)
        lcol = dot(cums3[rows, :], exl[...])
        allowed = tile_lanes(scores[0, c], 2 * lanes)
        ds = jnp.zeros((chunk, lanes), f32)
        for p in range(width // lanes):
            cols = slice(p * lanes, (p + 1) * lanes)
            e = pair_parts(lcol, cums_t[0, c], p)
            m = (e * allowed).astype(bf16)
            v = sc[rows, cols]
            dy = gh[rows, cols]
            high, low = halves(dy)
            both = two_heads(v, lanes // 2)
            parts = jnp.concatenate([high, low], axis=1)
            dm = dot_nt(parts, jnp.concatenate([both, both], axis=1))
            eds = e * dm
            ds = ds + eds[:, :lanes] + eds[:, lanes:]
            dvb = dot_tn(m, high) + dot_tn(m, low)
            lane = lax.broadcasted_iota(jnp.int32, (chunk, lanes), 1)
            dv = jnp.where(lane < lanes // 2, dvb[:chunk], dvb[chunk:])
            dv_out[rows, cols] = dv
            prod[:, cols] = y[rows, cols] * dy - v.astype(f32) * dv
        ds_out[c] += ds
        ahead[rows, :] += dot2(prod[...], red[...])


def back_state_kernel(*refs, hops):
    grads_in, refs = refs[:hops], refs[hops:]
    (states, gh, sc, dv, u, params, bc, c_t, tables, keep, decays, ex, red, ds, ahead, allowed, rows_in, gu_out, gbc_out,
     ldt_out, edges, db, dc, behind, direct, carry) = refs
    state = c_t.shape[0]
    g = pl.program_id(0)

    @pl.when(g == 0)
    def _():
        for ref in (db, dc, behind, direct, carry):
            ref[...] = jnp.zeros_like(ref)

    own, width = gu_out.shape
    step = min(width, 256)
    blocks = own // chunk
    for n in range(width // step):
        cols = slice(n * step, (n + 1) * step)
        gs = sum(r[:, cols].astype(f32) for r in grads_in)
        for c in reversed(range(blocks)):
            rows = rows_of(c)
            low_g = gs.astype(bf16)
            kept = keep[c : c + 1, cols]
            low_s = states[c, :, cols]
            scaled = sc[rows, cols].astype(f32)
            eo = dot(tables[rows, 3 * lanes :], ex[:, cols])
            dvs = eo * dot(bc[rows, :state], low_g)
            db[rows, :] += dot_nt((eo * scaled).astype(bf16), low_g)
            dy = gh[rows, cols]
            moved = (dot(tables[rows, 2 * lanes : 3 * lanes], ex[:, cols]) * dy).astype(bf16)
            dc[rows, :] += dot_nt(moved, low_s)
            carried = jnp.sum(low_s.astype(f32) * gs, axis=0, keepdims=True) * kept
            carry[c : c + 1, :] += dot2(jnp.broadcast_to(carried, (8, step)), red[cols, :])[:1]
            gs = gs * kept + dot(c_t[:, rows], moved)
            g_sc = dv[rows, cols] + dvs
            v, slope = silu_parts(u[rows, cols])
            behind[rows, :] += dot2(scaled * dvs, red[cols, :])
            direct[rows, :] += dot2(v * g_sc, red[cols, :])
            g_v = dot(tables[rows, :lanes], ex[:, cols]) * g_sc + params[0, 6:7, cols] * dy
            gu_out[rows, cols] = g_v * slope
            if c == 0:
                at = pl.ds(pl.multiple_of(g * width + n * step, lanes), step)
                edges[:, at] = (g_v * slope)[:edge].astype(bf16)

    @pl.when(g == pl.num_programs(0) - 1)
    def _():
        i = lax.broadcasted_iota(jnp.int32, (chunk, chunk), 0)
        j = lax.broadcasted_iota(jnp.int32, (chunk, chunk), 1)
        at_most = jnp.where(i <= j, 1.0, 0.0).astype(bf16)
        below = jnp.where(j < i, 1.0, 0.0).astype(bf16)
        decay_row = decays[6:7, :]
        for c in range(blocks):
            rows = rows_of(c)

            g_logs = sums3(at_most, ahead[rows, :]) + sums3(below, behind[rows, :]) + carry[c : c + 1, :]
            heads = ldt_out.shape[1]
            g_dt = (direct[rows, :] + g_logs * decay_row) * rows_in[rows, 2 * state :]
            ldt_out[rows, :] = g_dt[:, :heads].astype(bf16)
            g_scores = ds[c] * allowed[0, c]
            low_ds = g_scores.astype(bf16)
            gc = dc[rows, :] + dot(low_ds, bc[rows, :state])
            gb = db[rows, :] + dot_tn(low_ds, bc[rows, state:])
            g_bc = jnp.concatenate([gb, gc], axis=1)
            _, slope = silu_parts(rows_in[rows, : 2 * state])
            gbc_out[rows, :] = g_bc * slope
            if c == 0:
                edges[:, edges.shape[1] - g_bc.shape[1] :] = (g_bc * slope)[:edge].astype(bf16)


def in_z_kernel(lz, *refs, weights):
    ws, refs = refs[:weights], refs[weights:]
    a_up, ranks, acc, g_rank, p_up = refs

    @pl.when(pl.program_id(0) == 0)
    def _():
        acc[...] = jnp.zeros_like(acc)
        g_rank[...] = jnp.zeros_like(g_rank)

    size = g_rank.shape[1]
    g_rank[...] += dot_nt(lz[...], a_up[...])
    both = dot_tn(ranks[...], lz[...])
    p_up[0] = both[:size] + both[size:]
    with_weight(ws, lambda parts: add_times_transposed(acc, lz[...], parts), pl.program_id(0) // 2)


def conv_back(cur, params, masks, rows, width):
    total = params[3:4, :] * cur[:chunk]
    for k in range(1, 4):
        shifted = pltpu.roll(cur, cur.shape[0] - k, 0)[:chunk]
        total = total + params[3 - k : 4 - k, :] * (shifted * tile_lanes(masks[k - 1, rows, :], width))
    return total


def in_x_kernel(sel, gu, halo, a_up, ranks, params, masks, g_rank_z, p_up_z, order, normed, lx_out, g_rank, sent):
    g = pl.program_id(0)

    @pl.when(g == 0)
    def _():
        g_rank[...] = g_rank_z[...]
        sent[...] = jnp.zeros_like(sent)

    own, width = gu.shape
    step = min(width, 256)
    blocks = own // chunk
    for c in range(blocks):
        rows = rows_of(c)
        for n in range(width // step):
            cols = slice(n * step, (n + 1) * step)
            if c < blocks - 1:
                cur = gu[c * chunk : (c + 1) * chunk + 8, cols]
            else:
                cur = jnp.concatenate([gu[rows, cols], halo[:, cols].astype(f32)[:8]], axis=0)
            lx_out[rows, cols] = conv_back(cur, params[0, :, cols], masks, rows, step).astype(bf16)
    size = g_rank.shape[1]
    g_rank[...] += dot_nt(lx_out[...], a_up[...])
    both = dot_tn(ranks[...], lx_out[...])
    to = sel[8 + g]
    put_inner_parts(sent, to, p_up_z[0], order, 0)
    put_inner_parts(sent, to, both[:size] + both[size:], order, width // sent.shape[0])

    @pl.when(g == pl.num_programs(0) - 1)
    def _():
        put_width_parts(sent, dot2_tn(g_rank[...], normed[...]))


def tokens_kernel(sel, lx, *refs, weights):
    ws, refs = refs[:weights], refs[weights:]
    (acc_z, g_rank, gbc, halo_bc, params_bc, w_bc, ldt, dt_t, ad, masks, tokens, cot, norm_gain, grad, acc, lbc,
     g_norm) = refs
    g = pl.program_id(0)

    @pl.when(g == 0)
    def _():
        acc[...] = acc_z[...]

    with_weight(ws, lambda parts: add_times_transposed(acc, lx[...], parts), pl.program_id(0) // 2)

    @pl.when(g == pl.num_programs(0) - 1)
    def _():
        own, width = grad.shape
        blocks = own // chunk
        for c in range(blocks):
            rows = rows_of(c)
            if c < blocks - 1:
                cur = gbc[c * chunk : (c + 1) * chunk + 8, :]
            else:
                cur = jnp.concatenate([gbc[rows, :], halo_bc[...].astype(f32)[:8]], axis=0)
            lbc[rows, :] = conv_back(cur, params_bc[...], masks, rows, gbc.shape[1]).astype(bf16)
        g_norm[...] = (
            dot_nt(lbc[...], w_bc[...]) + dot(ldt[...], dt_t[...]) + dot2(g_rank[...], ad[...])
        )
        for j in range(8):
            at = pl.ds(pl.multiple_of(sel[korder[j]] * lanes, lanes), lanes)
            g_norm[:, at] += acc[:, j * lanes : (j + 1) * lanes]
        for c in range(blocks):
            rows = rows_of(c)
            wide = tokens[rows, :].astype(f32)
            scale = lax.rsqrt(jnp.sum(wide * wide, axis=1, keepdims=True) / width + epsilon)
            gn = g_norm[rows, :] * norm_gain[...]
            row_dot = jnp.sum(gn * wide, axis=1, keepdims=True)
            grad[rows, :] = (
                cot[rows, :].astype(f32) + gn * scale - wide * (scale * scale * scale * row_dot / width)
            )


def collect_kernel(picks, arrived, up_out, down_out, down_in, up_in):
    dp, tp, rows, _ = arrived.shape
    rank = rows // 4
    for b in range(up_out.shape[0]):
        total = jnp.zeros(arrived.shape[2:], f32)
        for d in range(dp):
            one = arrived[d, 0].astype(f32)
            for t in range(1, tp):
                one = one + arrived[d, t].astype(f32)
            total = total + jnp.where(picks[d] == b, one, 0.0)
        up_out[b] = total[:rank, : up_out.shape[2]]
        down_out[b] = total[rank : 2 * rank].T[: down_out.shape[1]]
        down_in[b] = total[2 * rank : 3 * rank, : down_in.shape[2]]
        up_in[b] = total[3 * rank :].T[: up_in.shape[1]]


def up(x):
    n = lax.axis_size("tensor")
    return lax.ppermute(x, "tensor", [(i, i + 1) for i in range(n - 1)])


def down(x):
    n = lax.axis_size("tensor")
    return lax.ppermute(x, "tensor", [(i + 1, i) for i in range(n - 1)])


def around_tensor(x):
    n = lax.axis_size("tensor")
    return [x] + [lax.ppermute(x, "tensor", [(i, (i + s) % n) for i in range(n)]) for s in range(1, n)]


def swap(x, bit):
    n = lax.axis_size("dp")
    return lax.ppermute(x, "dp", [(i, i ^ (1 << bit)) for i in range(n)])


def all_dp(x):
    count = lax.axis_size("dp").bit_length() - 1
    cur = x.reshape((1,) * count + x.shape)
    for bit in list(range(1, count)) + [0]:
        cur = jnp.concatenate([cur, swap(cur, bit)], axis=count - 1 - bit)
    return cur.reshape((-1,) + x.shape)


def joined_with(x, axis, bit):
    n = lax.axis_size(axis)
    return jnp.concatenate([x, lax.ppermute(x, axis, [(i, i ^ (1 << bit)) for i in range(n)])])


def after(x, *events):
    return lax.optimization_barrier((x, events))[0]


def spread_dp(rotated, events):
    out = []
    curs = [after(jnp.stack(rotated[2 * j : 2 * j + 2]), *events) for j in range(2)]
    firsts = [swap(cur, 1 + j) for j, cur in enumerate(curs)]
    pairs = [jnp.stack([cur, first]) for cur, first in zip(curs, firsts)]
    fars = [swap(pair, 2 - j) for j, pair in enumerate(pairs)]
    for pair, far in zip(pairs, fars):
        out += [pair, far, swap(pair, 0), swap(far, 0)]
    return out, firsts


def gather_plain(x):
    n, tp = lax.axis_size("dp"), lax.axis_size("tensor")
    whole = lax.all_gather(x, ("dp", "tensor")).reshape((n, tp) + x.shape)
    return [whole.transpose(1, 0, 2, 3).reshape(tp, n * x.shape[0], x.shape[1])]


def pad_lanes(x):
    return jnp.pad(x, ((0, 0), (0, lanes - x.shape[1])))


def shards(
    tokens,
    cotangent,
    doc_ids,
    adapter_pick,
    norm_gain,
    gate_x_weight,
    bc_weight,
    dt_weight,
    conv_x_weight,
    conv_bc_weight,
    conv_x_bias,
    conv_bc_bias,
    dt_bias,
    a_log,
    skip_gain,
    inner_gain,
    out_weight,
    in_down,
    in_up,
    out_down,
    out_up,
):
    dp_size, tp_size = lax.axis_size("dp"), lax.axis_size("tensor")
    both = ("dp", "tensor")
    seq_count, own, width = tokens.shape
    assert seq_count == 1 and width == 8 * lanes
    group = gate_x_weight.shape[2]
    inner = group * tp_size
    part = dt_weight.shape[1]
    heads = part * tp_size
    head_size = inner // heads
    assert head_size * 2 == lanes
    state = bc_weight.shape[1] // 2
    rank = in_down.shape[2]
    adapters = in_down.shape[0]
    hops = min(1 + (doc_most - 2) // own, tp_size - 1)
    blocks = own // chunk
    d_rows = gate_x_weight.shape[0]
    p_part = in_up.shape[4]
    hp = part * p_part
    mine, place_at = lax.axis_index("dp"), lax.axis_index("tensor")
    by_exchange = dp_size == 8 and tp_size == 4 and d_rows == lanes
    cot, tok = cotangent[0], tokens[0]

    local_x, local_z, local_out = gate_x_weight[:, 1], gate_x_weight[:, 0], out_weight.T
    if by_exchange:
        ring_x = around_tensor(local_x)

    cuts = [d_rows, d_rows, adapters * 2 * rank, adapters * 2 * rank, 16, 16]
    starts = [sum(cuts[:n]) for n in range(len(cuts))]
    if by_exchange:
        small_in = [
            bc_weight, dt_weight.T, in_down.transpose(0, 2, 1), out_up,
            in_up.transpose(0, 2, 3, 4, 1).reshape(adapters, 2 * hp, rank), out_down.reshape(adapters, hp, rank),
        ]
        vmem = pl.BlockSpec(memory_space=pltpu.VMEM)
        small = pl.pallas_call(
            pack_kernel,
            name="pack_kernel",
            out_shape=jax.ShapeDtypeStruct((sum(cuts), lanes), bf16),
            in_specs=[vmem] * 6 + [pl.BlockSpec(memory_space=pltpu.SMEM)],
            out_specs=vmem,
        )(*small_in, adapter_pick)
    else:
        small = [
            bc_weight[:, :state],
            bc_weight[:, state:],
            jnp.concatenate([in_down.transpose(0, 2, 1), out_up], axis=1).reshape(-1, d_rows),
            jnp.concatenate(
                [in_up.reshape(adapters, rank, 2 * hp),
                 jnp.pad(out_down.reshape(adapters, hp, rank).transpose(0, 2, 1), ((0, 0), (0, 0), (0, hp)))],
                axis=1,
            ).reshape(-1, 2 * hp),
            jnp.pad(dt_weight.T, ((0, 16 - part), (0, 0))),
            jnp.broadcast_to(adapter_pick.astype(bf16)[:, None], (16, lanes)),
        ]
        small = lax.all_gather(jnp.concatenate([pad_lanes(x) for x in small]), "dp")
    if by_exchange:
        natural = jnp.arange(8) ^ mine
    else:
        natural, small_at = jnp.asarray(np.argsort(korder)), jnp.arange(8)

    last = tok[-edge:].astype(f32)
    last_scale = lax.rsqrt(jnp.mean(last * last, axis=1, keepdims=True) + epsilon)
    halo_in = up((last * last_scale * norm_gain).astype(bf16))

    heads_row = jnp.pad(jnp.concatenate([dt_bias, a_log])[None], ((0, 0), (0, group - 2 * part)))
    params = jnp.concatenate(
        [conv_x_weight, conv_x_bias[None], inner_gain[None], jnp.repeat(skip_gain, head_size)[None], heads_row]
    )

    if by_exchange:
        params = jnp.stack(around_tensor(params))
        small = joined_with(joined_with(small[None], "dp", 1), "dp", 2)
        small = jnp.concatenate([small, swap(small, 0)])
        w_x, near_x = spread_dp(ring_x, [])
        ring_z = around_tensor(after(local_z, *ring_x[1:]))
        w_z, near_z = spread_dp(ring_z, near_x)
        small_at = jnp.asarray(np.argsort(korder))[natural]
    else:
        w_x, w_z, w_out = gather_plain(local_x), gather_plain(local_z), gather_plain(local_out)
        params = jnp.stack(around_tensor(params))
    pick = adapter_pick[0]
    taken = [small[:, a : a + c] for a, c in zip(starts, cuts)]
    picks = taken[5][:, 0, 0].astype(jnp.int32)
    inner_t = lax.dynamic_slice_in_dim(taken[3], pick * 2 * rank, 2 * rank, 1)
    dt_own = taken[4][:, :part]
    if by_exchange:
        picks, dt_own = picks[small_at], dt_own[small_at]
    if d_rows != lanes:
        fold = lanes // d_rows

        def rows_first(x):
            return x.reshape(8, fold * d_rows, lanes)

        def lanes_last(x):
            x = x[:, :, :d_rows].reshape(8, fold, x.shape[1], d_rows)
            return x.transpose(0, 2, 1, 3).reshape(8, -1, lanes)

        small = jnp.concatenate([rows_first(taken[0]), rows_first(taken[1]), lanes_last(taken[2])], 1)
        dt_own = lanes_last(dt_own)
    dt_own = dt_own.transpose(1, 0, 2).reshape(part, width)
    inner_rows = inner_t.reshape(-1, lanes)
    dt_rows = dt_own.reshape(-1, lanes)
    ring = jnp.concatenate([inner_rows, dt_rows])
    ring = around_tensor(ring)
    if by_exchange:
        ring_out = around_tensor(after(local_out, *ring[1:], *ring_z[1:]))
        w_out, _ = spread_dp(ring_out, near_z)
    ring = jnp.stack(ring)
    inner_t = ring[:, : inner_rows.shape[0]].reshape(tp_size, dp_size, 2 * rank, lanes)
    dt_t = ring[:, inner_rows.shape[0] :]
    dt_t = dt_t.reshape(heads, width)

    docs = doc_ids[0]
    padded = jnp.concatenate([jnp.full((4,), -1, jnp.int32), docs, jnp.full((4,), -2, jnp.int32)])
    near = lax.dynamic_slice_in_dim(padded, place_at * own, own + 8)
    segs = jnp.stack([near[1 + k : 1 + k + own] for k in range(7)]).astype(f32).reshape(7, blocks, chunk)
    bounds = jnp.stack([near[3 : 3 + own : chunk], near[3 + chunk :: chunk][:blocks]], axis=1).reshape(-1)
    groups = (place_at - jnp.arange(tp_size)) % tp_size
    sel = jnp.concatenate([natural, groups, jnp.arange(tp_size), pick[None], bounds, small_at]).astype(jnp.int32)

    def spread(width_each, copies):
        out = np.zeros((lanes, heads * width_each), np.float32)
        at = np.arange(heads * width_each)
        for n in range(copies):
            out[n * heads + at // width_each, at] = 1.0
        return jnp.asarray(out, bf16)

    ex, exl = spread(head_size, 2), spread(lanes, 3)
    red = jnp.asarray(np.arange(inner)[:, None] // head_size == np.arange(lanes)[None, :], bf16)
    at = np.arange(group)
    place = np.zeros((dp_size, hp, group), np.float32)
    place[at % head_size // p_part, at // head_size * p_part + at % p_part, at] = 1.0
    order = jnp.asarray(place.reshape(group, group).T, bf16)
    place = jnp.asarray(place, bf16)

    def full(*shape):
        return pl.BlockSpec(shape, lambda *s: (0,) * len(shape))

    def cols(rows, size=group, turn=0):
        return pl.BlockSpec((rows, size), lambda g, *s: (0, (g + turn) % tp_size))

    def stacked(*shape, base=0):
        return pl.BlockSpec((1,) + shape, lambda g, *s: (g + base,) + (0,) * len(shape))

    def params_at(base=0):
        return stacked(8, group, base=base)

    def weight_specs(ws, half=None):
        if len(ws) == 1:
            base = (half or 0) * tp_size // 2
            return [pl.BlockSpec((1,) + ws[0].shape[1:], lambda g, s: (s[8 + base + g], 0, 0))]
        shape = (2, 1) + ws[0].shape[2:]
        if half is not None:
            return [pl.BlockSpec(shape, lambda g, *s: (0, g, 0, 0))] * 4
        first = pl.BlockSpec(shape, lambda g, *s: (0, jnp.minimum(g, 1), 0, 0))
        second = pl.BlockSpec(shape, lambda g, *s: (0, jnp.maximum(g - 2, 0), 0, 0))
        return [first] * 4 + [second] * 4

    def call(kernel, out, in_specs, out_specs, scratch, flops, moved, steps=tp_size, fill=(), grant=vmem_bytes):
        kernel, kernel_takes_sel, name = kernel

        def body(sel_ref, *refs):
            refs = refs[: len(in_specs)] + refs[len(in_specs) + len(fill) :]
            return kernel(sel_ref, *refs) if kernel_takes_sel else kernel(*refs)

        return pl.pallas_call(
            body,
            name=name,
            input_output_aliases={1 + len(in_specs) + i: to for i, to in enumerate(fill)},
            out_shape=[jax.ShapeDtypeStruct(s, d) for s, d in out],
            grid_spec=pltpu.PrefetchScalarGridSpec(
                num_scalar_prefetch=1,
                grid=steps if isinstance(steps, tuple) else (steps,),
                in_specs=in_specs + [pl.BlockSpec(memory_space=pl.ANY)] * len(fill),
                out_specs=out_specs,
                scratch_shapes=scratch,
            ),
            compiler_params=pltpu.CompilerParams(
                dimension_semantics=("arbitrary",) * (len(steps) if isinstance(steps, tuple) else 1),
                vmem_limit_bytes=grant,
            ),
            cost_estimate=pl.CostEstimate(flops=flops, bytes_accessed=moved, transcendentals=0),
        )

    def plain(kernel, **static):
        return (lambda *refs: kernel(*refs, **static)), False, kernel.__name__

    def selecting(kernel, **static):
        return (lambda *refs: kernel(*refs, **static)), True, kernel.__name__

    n_w = len(w_x)
    big = (own, inner)
    ext = own + edge
    mat = 2 * own * width * inner
    mega = 1 << 20
    params_bc = jnp.concatenate([conv_bc_weight, conv_bc_bias[None], jnp.zeros((3, 2 * state), f32)])
    prep_out = [
        ((ext, width), bf16), ((own, width), bf16), ((ext, 2 * rank), bf16), ((own, 2 * rank), bf16),
        ((own, 6 * lanes), bf16), ((own, 2 * state), bf16),
        ((2 * state, own), bf16), ((2, blocks, chunk, chunk), f32), ((own, 2 * state + lanes), f32),
        ((tp_size, blocks, part, chunk), f32), ((8, inner), f32), ((5 * rank, inner), bf16),
        ((2 * rank, width), bf16), ((width, 2 * state), bf16), ((6, own, lanes), f32),
    ]
    prep_in = [tok, halo_in, norm_gain[None], small, dt_t, inner_t, place, params, params_bc, segs, ex]
    normed_moved, normed, ranks, ranks_own, tables, bc, bc_t, scores, rows_f32, cums_t, keep, ups, wides, w_bc, masks = call(
        selecting(prep_kernel, rank=rank, state=state, moved_blocks=by_exchange),
        prep_out,
        [full(*x.shape) for x in prep_in],
        [full(*s) for s, _ in prep_out],
        [pltpu.VMEM((ext, width), bf16)],
        mat // 4, 6 * mega, 1, grant=vmem_bytes * 5 // 4,
    )(sel, *prep_in)

    def part_at(row, col, *shape):
        return pl.BlockSpec(shape, lambda *s: (row, col))

    def up_at(row, rows, base=0):
        return pl.BlockSpec((rows, group), lambda g, *s: (row, g + base))

    def first_at(row, *shape):
        return pl.BlockSpec(shape, lambda g, *s: (row,) + (0,) * (len(shape) - 1))

    scores_spec, allowed_spec = (first_at(n, 1, blocks, chunk, chunk) for n in range(2))
    b_t_spec, c_t_spec = part_at(0, 0, state, own), part_at(1, 0, state, own)
    masks_spec, masks_after_spec = first_at(0, 3, own, lanes), first_at(1, 3, own, lanes)
    ad_spec, b_up_spec = part_at(0, 0, rank, width), part_at(1, 0, rank, width)
    chunk_rows = stacked(blocks, part, chunk)
    z_specs = weight_specs(w_z)
    p_spec = params_at()
    order_spec = full(group, group)
    u, scaled, sent_state = call(
        plain(proj_kernel, weights=n_w),
        [(big, f32), (big, bf16), ((state, inner), bf16)],
        [full(ext, width)] + weight_specs(w_x)
        + [full(ext, 2 * rank), up_at(1, 2 * rank), p_spec, masks_spec, part_at(0, 0, own, 2 * lanes), cols(lanes),
           b_t_spec],
        [cols(own), cols(own), cols(state)],
        [pltpu.VMEM((ext, group), f32), pltpu.VMEM((own, group), bf16)],
        mat, 12 * mega, grant=vmem_bytes * 5 // 4,
    )(sel, normed_moved, *w_x, ranks, ups, params, masks, tables, ex, bc_t)

    def chain(x, step, sign, *events):
        out, moved = [step(x)], x
        for hop in range(1, hops):
            kept = jnp.roll(keep[7:8], sign * hop * group, axis=1)
            moved = (after(out[-1], *events).astype(f32) * kept).astype(bf16)
            out.append(step(moved))
        return out, moved

    within_specs = [cols(own), part_at(0, 5, own, lanes), chunk_rows, scores_spec, cols(lanes, part * lanes)]
    (y_within,) = call(
        plain(within_kernel), [(big, f32)], within_specs, [cols(own)], [], mat, 6 * mega
    )(sel, scaled, tables, cums_t, scores, exl)
    states_in, _ = chain(sent_state, up, -1, y_within)

    states_spec = pl.BlockSpec((blocks, state, group), lambda g, *s: (0, 0, g))
    def steps_in(phase, first, then):
        return lambda p, g: jnp.where(p == phase, g, jnp.where(p < phase, first, then))

    def moving(phase, make):
        at = steps_in(phase, 0, tp_size - 1)
        return lambda p, g, s: make(at(p, g), s)

    def cols_in(phase, rows, size=group, turn=0):
        return pl.BlockSpec((rows, size), moving(phase, lambda i, s: (0, (i + turn) % tp_size)))

    def up_in(phase, row, rows):
        return pl.BlockSpec((rows, group), moving(phase, lambda i, s: (row, i)))

    def weights_in(phase, ws):
        if len(ws) == 1:
            return [pl.BlockSpec((1,) + ws[0].shape[1:], moving(phase, lambda i, s: (s[8 + i], 0, 0)))]
        shape = (2, 1) + ws[0].shape[2:]
        first = pl.BlockSpec(shape, moving(phase, lambda i, s: (0, jnp.minimum(i, 1), 0, 0)))
        second = pl.BlockSpec(shape, moving(phase, lambda i, s: (0, jnp.maximum(i - 2, 0), 0, 0)))
        return [first] * 4 + [second] * 4

    def cols_always(rows, size):
        return pl.BlockSpec((rows, size), lambda p, g, s: (0, g))

    sent_shape = (dp_size, tp_size, 2 * rank, max(d_rows, 2 * hp))
    cot = cotangent[0]
    big3 = (tp_size, own, group)
    y, states, mixed, sent_out, g_heads, low_z, sent_grad = call(
        selecting(middle_kernel, weights=n_w, hops=hops, inner=inner),
        [(big, f32), ((blocks, state, inner), bf16), ((own, width), f32), (sent_shape, bf16), (big, f32), (big, bf16),
         ((state, inner), bf16)],
        [full(ext, width)] + weights_in(0, w_z) + weights_in(1, w_out)
        + [cols_in(0, state, group, -h) for h in range(1, hops + 1)]
        + [full(own, 2 * rank), up_in(0, 0, 2 * rank), pl.BlockSpec((1, 8, group), lambda p, g, s: (g, 0, 0)),
           cols_in(0, own), cols_in(0, own), cols_in(0, own), part_at(0, 1, own, 2 * lanes),
           part_at(0, 4, own, lanes), cols_in(0, 8), cols_always(lanes, group), b_t_spec, c_t_spec,
           part_at(0, 1, own, state), full(own, width), full(own, width), b_up_spec, up_in(1, 4, rank), order_spec],
        [cols_in(0, own), pl.BlockSpec((blocks, state, group), moving(0, lambda i, s: (0, 0, i))), full(own, width),
         full(*sent_shape), cols_in(2, own), cols_in(2, own), cols_in(2, state)],
        [pltpu.VMEM(big3, f32), pltpu.VMEM(big3, f32), pltpu.VMEM(big3, f32), pltpu.VMEM(big3, f32),
         pltpu.VMEM((own, lanes), f32), pltpu.VMEM((own, lanes), f32), pltpu.VMEM((own, width), f32),
         pltpu.VMEM((own, width), bf16), pltpu.VMEM((own, rank), f32), pltpu.VMEM((own, rank), f32),
         pltpu.VMEM((own, group), bf16)],
        4 * mat, 40 * mega, (3, tp_size), grant=vmem_bytes * 5 // 4,
    )(sel, normed_moved, *w_z, *w_out, *states_in, ranks_own, ups, params, y_within, u, scaled, tables, tables, keep,
      ex, bc_t, bc_t, bc, cot, tok, wides, ups, order)
    red_spec = pl.BlockSpec((group, lanes), lambda g, *s: (g, 0))
    d_within, d_scores, ahead = call(
        plain(back_within_kernel),
        [(big, f32), ((blocks, chunk, chunk), f32), ((own, lanes), f32)],
        [cols(own), cols(own)] + within_specs + [red_spec],
        [cols(own), full(blocks, chunk, chunk), full(own, lanes)],
        [pltpu.VMEM((chunk, group), f32)],
        2 * mat, 14 * mega, grant=vmem_bytes * 5 // 4,
    )(sel, g_heads, y, scaled, tables, cums_t, scores, exl, red)
    grads_in, moved_grad = chain(sent_grad, down, 1, ahead)
    low_z = after(low_z, moved_grad)

    acc_z, g_rank_z, p_up_z = call(
        plain(in_z_kernel, weights=n_w),
        [((own, width), f32), ((own, rank), f32), ((tp_size, rank, group), f32)],
        [cols(own)] + z_specs + [up_at(0, rank), full(own, 2 * rank)],
        [full(own, width), full(own, rank), stacked(rank, group)],
        [],
        mat, 8 * mega,
    )(sel, low_z, *w_z, ups, ranks_own)

    grads_in = [after(x, acc_z) for x in grads_in]
    edges_shape = (edge, inner + 2 * state)
    g_u, g_u_bc, low_dt, edges = call(
        plain(back_state_kernel, hops=hops),
        [(big, f32), ((own, 2 * state), f32), ((own, heads), bf16), (edges_shape, bf16)],
        [cols(state, group, h) for h in range(1, hops + 1)]
        + [states_spec, cols(own), cols(own), cols(own), cols(own), p_spec, full(own, 2 * state), c_t_spec,
           part_at(0, 0, own, 4 * lanes), cols(8), part_at(0, 0, 8, lanes), cols(lanes), red_spec,
           full(blocks, chunk, chunk), full(own, lanes), allowed_spec, full(own, 2 * state + lanes)],
        [cols(own), full(own, 2 * state), full(own, heads), full(*edges_shape)],
        [pltpu.VMEM((own, state), f32), pltpu.VMEM((own, state), f32), pltpu.VMEM((own, lanes), f32),
         pltpu.VMEM((own, lanes), f32), pltpu.VMEM((8, lanes), f32)],
        mat, 24 * mega,
    )(sel, *grads_in, states, g_heads, scaled, d_within, u, params, bc, bc_t, tables, keep, keep, ex, red, d_scores,
      ahead, scores, rows_f32)

    halo = down(edges)
    low_x, g_rank, sent_in = call(
        selecting(in_x_kernel),
        [(big, bf16), ((own, rank), f32), (sent_shape, bf16)],
        [cols(own), cols(edge, group, 1), up_at(2, rank), full(own, 2 * rank), p_spec, masks_after_spec,
         full(own, rank), stacked(rank, group), order_spec, full(own, width)],
        [cols(own), full(own, rank), full(*sent_shape)],
        [],
        mat // 8, 8 * mega,
    )(sel, g_u, halo, ups, ranks_own, params, masks, g_rank_z, p_up_z, order, normed)

    (tokens_grad,) = call(
        selecting(tokens_kernel, weights=n_w),
        [((own, width), f32)],
        [cols(own)] + weight_specs(w_x)
        + [full(own, width), full(own, rank), full(own, 2 * state),
           pl.BlockSpec((edge, 2 * state), lambda g, *s: (0, inner // (2 * state))),
           full(8, 2 * state), full(width, 2 * state), full(own, heads), full(heads, width), ad_spec,
           masks_after_spec, full(own, width), full(own, width), full(1, width)],
        [full(own, width)],
        [pltpu.VMEM((own, width), f32), pltpu.VMEM((own, 2 * state), bf16), pltpu.VMEM((own, width), f32)],
        mat, 14 * mega, grant=vmem_bytes * 5 // 4,
    )(sel, low_x, *w_x, acc_z, g_rank, g_u_bc, halo, params_bc, w_bc, low_dt, dt_t, wides, masks, tok, cot,
      norm_gain[None])

    sent = jnp.concatenate([sent_out, sent_in], axis=2)
    arrived = lax.all_to_all(sent.reshape((-1,) + sent.shape[2:]), both, 0, 0, tiled=True)
    arrived = arrived.reshape(sent.shape)
    shapes = [(adapters, rank, d_rows), (adapters, hp, rank), (adapters, rank, d_rows), (adapters, 2 * hp, rank)]
    grad_out_up, grad_out_down, grad_in_down, grad_in_up = call(
        selecting(collect_kernel), [(s, f32) for s in shapes], [full(*sent.shape)],
        [full(*s) for s in shapes], [], mega, mega, 1,
    )(picks, arrived)

    grad_out_down = grad_out_down.reshape(out_down.shape)
    grad_in_down = grad_in_down.transpose(0, 2, 1)
    grad_in_up = grad_in_up.reshape(adapters, 2, part, p_part, rank).transpose(0, 4, 1, 2, 3)
    return (mixed[None], tokens_grad[None], grad_in_down, grad_in_up, grad_out_down, grad_out_up)


def solution(mesh):
    placed = (
        P("dp", "tensor", None),
        P("dp", "tensor", None),
        P("dp", None),
        P("dp"),
        P(),
        P("dp", None, "tensor"),
        P("dp", None),
        P("dp", "tensor"),
        P(None, "tensor"),
        P(),
        P("tensor"),
        P(),
        P("tensor"),
        P("tensor"),
        P("tensor"),
        P("tensor"),
        P("tensor", "dp"),
        P(None, "dp", None),
        P(None, None, None, "tensor", "dp"),
        P(None, "tensor", "dp", None),
        P(None, None, "dp"),
    )
    return jax.shard_map(
        shards,
        mesh=mesh,
        in_specs=placed,
        out_specs=(
            P("dp", "tensor", None),
            P("dp", "tensor", None),
            P(None, "dp", None),
            P(None, None, None, "tensor", "dp"),
            P(None, "tensor", "dp", None),
            P(None, None, "dp"),
        ),
        check_vma=False,
    )
```

```python
import math

import jax
import jax.numpy as jnp
import numpy as np
from jax import lax
from jax.experimental import pallas as pl
from jax.experimental.pallas import tpu as pltpu
from jax.sharding import PartitionSpec as P

epsilon = 1e-05
chunk = 128
lanes = 128
doc_most = 800
edge = 16
f32, bf16 = jnp.float32, jnp.bfloat16
exact = lax.Precision.HIGHEST
vmem_bytes = 48 * 1024 * 1024


def dot(a, b):
    return jnp.dot(a, b, preferred_element_type=f32)


def dot_nt(a, b):
    return lax.dot_general(a, b, (((1,), (1,)), ((), ())), preferred_element_type=f32)


def dot_tn(a, b):
    return lax.dot_general(a, b, (((0,), (0,)), ((), ())), preferred_element_type=f32)


def halves(x):
    high = x.astype(bf16)
    return high, (x - high.astype(f32)).astype(bf16)


def pieces(x, count):
    out = []
    for _ in range(count):
        part = lax.reduce_precision(x, 8, 7)
        out.append(part.astype(bf16))
        x = x - part
    return jnp.concatenate(out, axis=-1)


def dot2(x, w):
    high, low = halves(x)
    return dot(high, w) + dot(low, w)


def dot2_nt(x, w):
    high, low = halves(x)
    return dot_nt(high, w) + dot_nt(low, w)


def dot2_tn(x, w):
    high, low = halves(x)
    return dot_tn(high, w) + dot_tn(low, w)


def tile_lanes(m, width):
    return m if width == lanes else jnp.concatenate([m] * (width // lanes), axis=1)


def sigmoid(u):
    return 0.5 + 0.5 * jnp.tanh(0.5 * u)


def silu(u):
    return u * sigmoid(u)


def silu_parts(u):
    s = sigmoid(u)
    v = u * s
    return v, s + v * (1.0 - s)


korder = (0, 2, 4, 6, 1, 3, 5, 7)


def weight_pieces(refs, at=0):
    if len(refs) == 1:
        return [(refs[0][...].reshape(-1, refs[0].shape[-1]), None)]
    pairs = ((0, 1), (2, 3), (4, 5), (6, 7)) if at == 0 else ((0, 2), (1, 3), (4, 6), (5, 7))
    return [
        (ref[...].reshape(2 * lanes, ref.shape[-1]), pair) for ref, pair in zip(refs[4 * at : 4 * at + 4], pairs)
    ]


def block_at(n):
    return slice(n * lanes, (n + 1) * lanes)


def with_weight(refs, body, half):
    if len(refs) == 1:
        body(weight_pieces(refs))
        return
    if isinstance(half, int):
        body(weight_pieces(refs * 2, half))
        return

    @pl.when(half == 0)
    def _():
        body(weight_pieces(refs, 0))

    @pl.when(half == 1)
    def _():
        body(weight_pieces(refs, 1))


def times(left, parts):
    total = None
    for w, pair in parts:
        if pair is None:
            value = left(slice(None))
        elif pair[1] == pair[0] + 1:
            value = left(slice(pair[0] * lanes, (pair[1] + 1) * lanes))
        else:
            value = jnp.concatenate([left(block_at(n)) for n in pair], axis=1)
        term = dot(value, w)
        total = term if total is None else total + term
    return total


def add_times_transposed(acc, low, parts):
    for w, pair in parts:
        term = dot_nt(low, w)
        if pair is None:
            acc[...] += term
        elif pair[1] == pair[0] + 1:
            acc[:, pair[0] * lanes : (pair[1] + 1) * lanes] += term
        else:
            for i, n in enumerate(pair):
                acc[:, block_at(n)] += term[:, block_at(i)]


def rows_of(c):
    return slice(c * chunk, (c + 1) * chunk)


def sums3(tri, x):
    high, mid = halves(x)
    low = (x - high.astype(f32) - mid.astype(f32)).astype(bf16)
    return dot(tri, high) + dot(tri, mid) + dot(tri, low)


def parts_of(x, count):
    out = []
    for _ in range(count):
        part = x.astype(bf16)
        out.append(part)
        x = x - part.astype(f32)
    return jnp.concatenate(out, axis=1)


def table_of(x, count):
    parts = parts_of(x, count)
    return jnp.concatenate([parts, jnp.zeros((x.shape[0], lanes - parts.shape[1]), bf16)], axis=1)


def column(row):
    return jnp.broadcast_to(row, (lanes, lanes)).T


def prep_kernel(sel, tokens, halo, norm_gain, small, dt_t, inner_t, place, params, params_bc, segs, ex, no_out,
                normed, ranks, ranks_own, tables, bc_out, bct_out, scores, rows_out, cums_t, keep, ups, wides, w_bc,
                masks, ext, *, rank, state, moved_blocks):
    own, width = tokens.shape
    blocks = own // chunk
    tp, _, group = params.shape
    heads = dt_t.shape[0]
    part = heads // tp
    bc_rows = 2 * lanes
    turn, pick, bound, small_at = 8 + tp, sel[8 + 2 * tp], 9 + 2 * tp, 9 + 2 * tp + 2 * blocks

    for c in range(blocks):
        wide = tokens[rows_of(c), :].astype(f32)
        scale = lax.rsqrt(jnp.sum(wide * wide, axis=1, keepdims=True) / width + epsilon)
        ext[edge + c * chunk : edge + (c + 1) * chunk, :] = (wide * scale * norm_gain[...]).astype(bf16)
    ext[:edge, :] = halo[...]
    for j in range(8):
        k = korder[j]
        at = pl.ds(pl.multiple_of(sel[k] * lanes, lanes), lanes)
        cols = slice(j * lanes, (j + 1) * lanes)
        no_out[:, cols] = ext[:, at]
        at = sel[small_at + j]
        wides[:, cols] = small[at, pl.ds(pl.multiple_of(bc_rows + pick * 2 * rank, 2 * rank), 2 * rank), :]
        w_bc[j * lanes : (j + 1) * lanes, :state] = small[at, :lanes, :]
        w_bc[j * lanes : (j + 1) * lanes, state:] = small[at, lanes : 2 * lanes, :]
    normed[...] = ext[edge:, :]
    ranks[...] = parts_of(dot_nt(ext[...], wides[:rank, :]), 2)
    ranks_own[...] = ranks[edge:, :]
    bc = dot(ext[...], w_bc[...])

    hp = place.shape[1]
    for s in range(tp):
        cols = slice(s * group, (s + 1) * group)
        z = x = d = None
        for k in range(inner_t.shape[1]):
            where = place[sel[korder[k]]] if moved_blocks else place[k]
            piece = inner_t[sel[turn + s], k]
            terms = (dot(piece[:rank, :hp], where), dot(piece[:rank, hp : 2 * hp], where),
                     dot(piece[rank:, :hp], where))
            z, x, d = terms if z is None else (z + terms[0], x + terms[1], d + terms[2])
        z, x = z.astype(bf16), x.astype(bf16)
        ups[:, cols] = jnp.concatenate([z, z, x, x, d.astype(bf16)], axis=0)

    i = lax.broadcasted_iota(jnp.int32, (chunk, chunk), 0)
    j = lax.broadcasted_iota(jnp.int32, (chunk, chunk), 1)
    tril = jnp.where(j <= i, 1.0, 0.0)
    segs_at = []
    for c in range(blocks):
        rows = rows_of(c)
        seg = column(segs[3, c : c + 1, :])
        segs_at.append(seg[:, :heads])
        for k in range(1, 4):
            masks[k - 1, rows, :] = jnp.where(column(segs[3 - k, c : c + 1, :]) == seg, 1.0, 0.0)
            masks[k + 2, rows, :] = jnp.where(column(segs[3 + k, c : c + 1, :]) == seg, 1.0, 0.0)
        cur = bc[edge + c * chunk - 8 : edge + (c + 1) * chunk]
        total = params_bc[3:4, :] * cur[8:] + params_bc[4:5, :]
        for k in range(1, 4):
            shifted = pltpu.roll(cur, k, 0)[8:]
            total = total + params_bc[3 - k : 4 - k, :] * (
                shifted * tile_lanes(masks[k - 1, rows, :], 2 * state)
            )
        rows_out[rows, : 2 * state] = total
        value = silu(total)
        inb, inc = value[:, :state], value[:, state:]
        bc_out[rows, :] = value.astype(bf16)
        bct_out[:state, rows] = inb.T.astype(bf16)
        bct_out[state:, rows] = inc.T.astype(bf16)
        okay = jnp.where(seg == segs[3, c : c + 1, :], tril, 0.0)
        scores[1, c] = okay
        scores[0, c] = dot_nt(inc.astype(bf16), inb.astype(bf16)) * okay

    bias = jnp.concatenate([params[sel[turn + s], 7:8, :part] for s in range(tp)], axis=1)
    a_log = jnp.concatenate([params[sel[turn + s], 7:8, part : 2 * part] for s in range(tp)], axis=1)
    decays = -jnp.exp(a_log)
    raw = dot_nt(ext[edge:, :], dt_t[...]) + bias
    dt = jnp.maximum(raw, 0.0) + jnp.log1p(jnp.exp(-jnp.abs(raw)))
    rows_out[:, 2 * state :] = jnp.concatenate([sigmoid(raw), jnp.zeros((own, lanes - heads), f32)], axis=1)
    tables[:, :lanes] = table_of(dt, 2)
    logs = dt * decays * math.log2(math.e)
    bounds = [sel[bound + n].astype(f32) for n in range(2 * blocks)]
    before_seg, last_seg = bounds[0], bounds[-1]
    prior = jnp.zeros((1, heads), f32)
    all_cums, keeps = [], []
    tri = tril.astype(bf16)
    for c in range(blocks):
        rows = rows_of(c)
        before_c, last_c = bounds[2 * c], bounds[2 * c + 1]
        cums = sums3(tri, logs[rows])
        end = cums[chunk - 1 : chunk]
        seg = segs_at[c]
        tables[rows, 5 * lanes :] = table_of(cums, 3)
        flipped = jnp.concatenate([cums, jnp.zeros((chunk, lanes - heads), f32)], axis=1).T
        for s in range(tp):
            cums_t[s, c] = flipped[s * part : (s + 1) * part]
        tables[rows, 2 * lanes : 3 * lanes] = table_of(jnp.where(seg == before_c, jnp.exp2(cums), 0.0), 2)
        tables[rows, 3 * lanes : 4 * lanes] = table_of(jnp.where(seg == last_c, jnp.exp2(end - cums), 0.0), 2)
        keeps.append(jnp.where(before_c == last_c, jnp.exp2(end), 0.0))
        all_cums.append(cums + prior)
        prior = prior + end
    for c in range(blocks):
        rows = rows_of(c)
        seg = segs_at[c]
        tables[rows, 4 * lanes : 5 * lanes] = table_of(jnp.where(seg == before_seg, jnp.exp2(all_cums[c]), 0.0), 2)
        tables[rows, lanes : 2 * lanes] = table_of(jnp.where(seg == last_seg, jnp.exp2(prior - all_cums[c]), 0.0), 2)
    whole = jnp.where(before_seg == last_seg, jnp.exp2(prior), 0.0)
    table = jnp.concatenate(keeps + [jnp.zeros((7 - blocks, heads), f32), whole], axis=0)
    high, mid = halves(table)
    low = (table - high.astype(f32) - mid.astype(f32)).astype(bf16)
    spread = ex[:heads, :]
    keep[...] = dot(high, spread) + dot(mid, spread) + dot(low, spread)
    keep[6:7, :lanes] = jnp.concatenate([decays, jnp.zeros((1, lanes - heads), f32)], axis=1)


def pack_kernel(bc, dt_weight, in_down, out_up, in_up, out_down, pick, out):
    rows, two = bc.shape
    part = dt_weight.shape[0]
    count, rank, _ = in_down.shape
    at = 2 * rows
    out[:rows, :] = bc[:, : two // 2]
    out[rows:at, :] = bc[:, two // 2 :]
    for b in range(count):
        out[at + 2 * rank * b : at + 2 * rank * b + rank, :] = in_down[b]
        out[at + 2 * rank * b + rank : at + 2 * rank * (b + 1), :] = out_up[b]
    at += 2 * rank * count
    for b in range(count):
        out[at + 2 * rank * b : at + 2 * rank * b + rank, :] = in_up[b].astype(f32).T.astype(bf16)
        flipped = out_down[b].astype(f32).T
        out[at + 2 * rank * b + rank : at + 2 * rank * (b + 1), :] = jnp.concatenate(
            [flipped, jnp.zeros_like(flipped)], axis=1
        ).astype(bf16)
    at += 2 * rank * count
    wide = jnp.concatenate([dt_weight[...].astype(f32), jnp.zeros((16 - part, rows), f32)], axis=0)
    out[at : at + 16, :] = wide.astype(bf16)
    out[at + 16 : at + 32, :] = jnp.zeros((16, lanes), bf16) + pick[0].astype(f32).astype(bf16)


def proj_kernel(left, *refs, weights):
    refs, ws = refs[weights:], refs[:weights]
    ranks, a_up, params, masks, tables, ex, b_t, u_out, sc_out, f_out, xs, moved = refs

    def body(parts):
        xs[...] = times(lambda at: left[:, at], parts) + dot(ranks[...], a_up[...])

    with_weight(ws, body, pl.program_id(0) // 2)
    own, width = u_out.shape
    step = min(width, 256)
    for c in range(own // chunk):
        rows = rows_of(c)
        for n in range(width // step):
            cols = slice(n * step, (n + 1) * step)
            cur = xs[edge + c * chunk - 8 : edge + (c + 1) * chunk, cols]
            total = params[0, 3:4, cols] * cur[8:] + params[0, 4:5, cols]
            for k in range(1, 4):
                shifted = pltpu.roll(cur, k, 0)[8:]
                total = total + params[0, 3 - k : 4 - k, cols] * (
                    shifted * tile_lanes(masks[k - 1, rows, :], step)
                )
            u_out[rows, cols] = total
            value = silu(total)
            scaled = (dot(tables[rows, :lanes], ex[:, cols]) * value).astype(bf16)
            sc_out[rows, cols] = scaled
            moved[rows, cols] = (dot(tables[rows, lanes:], ex[:, cols]) * scaled.astype(f32)).astype(bf16)
    f_out[...] = dot(b_t[...], moved[...]).astype(bf16)

def pair_parts(lcol, cums_t, p):
    lc = lcol[:, p * 2 * lanes : (p + 1) * 2 * lanes]
    lr = jnp.concatenate([cums_t[2 * p : 2 * p + 1, :], cums_t[2 * p + 1 : 2 * p + 2, :]], axis=1)
    return jnp.exp2(jnp.minimum(lc - lr, 0.0))


def two_heads(v, head_size):
    lane = lax.broadcasted_iota(jnp.int32, v.shape, 1)
    zero = jnp.zeros_like(v)
    return jnp.concatenate([jnp.where(lane < head_size, v, zero), jnp.where(lane < head_size, zero, v)], 0)


def within_kernel(sc, cums3, cums_t, scores, exl, y_out):
    own, width = y_out.shape
    for c in range(own // chunk):
        rows = rows_of(c)
        lcol = dot(cums3[rows, :], exl[...])
        allowed = tile_lanes(scores[0, c], 2 * lanes)
        for p in range(width // lanes):
            e = pair_parts(lcol, cums_t[0, c], p)
            m = (e * allowed).astype(bf16)
            cols = slice(p * lanes, (p + 1) * lanes)
            y_out[rows, cols] = dot(m, two_heads(sc[rows, cols], lanes // 2))


def row_scale_of(sumsq, inner):
    return lax.rsqrt(jnp.sum(sumsq, axis=1, keepdims=True) / inner + epsilon)


def put_width_parts(sent, value):
    rank = value.shape[0]
    dp, tp, _, _ = sent.shape
    size = value.shape[1] // dp
    for d in range(dp):
        piece = value[:, d * size : (d + 1) * size].astype(bf16)
        for t in range(tp):
            sent[d, t, :rank, :size] = piece


def put_inner_parts(sent, to, value, order, offset):
    rank = value.shape[0]
    dp = sent.shape[0]
    hp = value.shape[1] // dp
    moved = dot(value.astype(bf16), order[...]).astype(bf16)
    for d in range(dp):
        sent[d, to, rank : 2 * rank, offset : offset + hp] = moved[:, d * hp : (d + 1) * hp]


def middle_kernel(sel, left, *refs, weights, hops, inner):
    zs, outs, refs = refs[:weights], refs[weights : 2 * weights], refs[2 * weights :]
    s_ins, refs = refs[:hops], refs[hops:]
    (ranks, a_up, params, yw, u, sc, tables, own_in, keep, ex, b_t, c_t, in_c, cot, tokens, b_up, b_down, order, red,
     states, mixed, sent, gh_out, lz_out, g_out, ahead,
     ys, heads, gate_z, gated, gg, sumsq, dots, acc, cots, g_rank, rank, low) = refs
    phase, g = pl.program_id(0), pl.program_id(1)
    last = pl.num_programs(1) - 1
    half = g // 2
    own, width = gh_out.shape
    step = min(width, 256)
    blocks = own // chunk

    @pl.when((phase == 0) & (g == 0))
    def _():
        ahead[...] = jnp.zeros_like(ahead)
        sumsq[...] = jnp.zeros_like(sumsq)
        acc[...] = jnp.zeros_like(acc)
        rank[...] = jnp.zeros_like(rank)
        dots[...] = jnp.zeros_like(dots)
        sent[...] = jnp.zeros_like(sent)
        for j in range(8):
            at = pl.ds(pl.multiple_of(sel[korder[j]] * lanes, lanes), lanes)
            cots[:, j * lanes : (j + 1) * lanes] = cot[:, at]
        g_rank[...] = dot_nt(cot[...], b_up[...])

    @pl.when(phase == 0)
    def _():
        def body(parts):
            first = left.shape[0] - own
            gate_z[g] = times(lambda at: left[first:, at], parts) + dot(ranks[...], a_up[...])

        with_weight(zs, body, half)
        for n in range(width // step):
            cols = slice(n * step, (n + 1) * step)
            new = []
            for c in range(blocks):
                rows = rows_of(c)
                moved = (dot(tables[rows, lanes:], ex[:, cols]) * sc[rows, cols].astype(f32)).astype(bf16)
                new.append(dot(b_t[:, rows], moved))
            s = sum(r[:, cols].astype(f32) for r in s_ins)
            for c in range(blocks):
                states[c, :, cols] = s.astype(bf16)
                s = s * keep[c : c + 1, cols] + new[c]
            for c in range(blocks):
                rows = rows_of(c)
                y = yw[rows, cols] + dot(tables[rows, :lanes], ex[:, cols]) * dot(in_c[rows, :], states[c, :, cols])
                ys[g, rows, cols] = y
                head = y + params[0, 6:7, cols] * silu(u[rows, cols])
                heads[g, rows, cols] = head
                gd = head * silu(gate_z[g, rows, cols])
                gated[g, rows, cols] = gd
                sq = gd * gd
                total = sumsq[rows, :]
                for i in range(step // lanes):
                    total = total + sq[:, i * lanes : (i + 1) * lanes]
                sumsq[rows, :] = total

    @pl.when(phase == 1)
    def _():
        scale = row_scale_of(sumsq[...], inner)
        normed_inner = gated[g] * scale * params[0, 5:6, :]
        high, rest = halves(normed_inner)
        low[...] = high
        rank[...] += dot_nt(high, b_down[...]) + dot_nt(rest, b_down[...])
        r_high, r_low = halves(g_rank[...])
        p_down = dot_tn(r_high, high) + dot_tn(r_low, high) + dot_tn(r_high, rest)
        put_inner_parts(sent, sel[8 + g], p_down, order, 0)

        def body(parts):
            value = (times(lambda at: cots[:, at], parts) + dot2(g_rank[...], b_down[...])) * params[0, 5:6, :]
            gg[g] = value
            prod = value * gated[g]
            total = dots[...]
            for i in range(width // lanes):
                total = total + prod[:, i * lanes : (i + 1) * lanes]
            dots[...] = total
            add_times_transposed(acc, low[...], parts)

        with_weight(outs, body, half)

    @pl.when((phase == 1) & (g == last))
    def _():
        put_width_parts(sent, dot2_tn(rank[...], cot[...]))
        mixed[...] = tokens[...].astype(f32) + dot2(rank[...], b_up[...])
        for j in range(8):
            at = pl.ds(pl.multiple_of(sel[korder[j]] * lanes, lanes), lanes)
            mixed[:, at] += acc[:, j * lanes : (j + 1) * lanes]

    @pl.when(phase == 2)
    def _():
        scale = row_scale_of(sumsq[...], inner)
        coef = scale * scale * scale * (jnp.sum(dots[...], axis=1, keepdims=True) / inner)
        for c in range(blocks):
            rows = rows_of(c)
            sc_rows, co_rows = scale[rows], coef[rows]
            for n in range(width // step):
                cols = slice(n * step, (n + 1) * step)
                g_gated = gg[g, rows, cols] * sc_rows - gated[g, rows, cols] * co_rows
                gate, slope = silu_parts(gate_z[g, rows, cols])
                lz_out[rows, cols] = (g_gated * heads[g, rows, cols] * slope).astype(bf16)
                gh = g_gated * gate
                gh_out[rows, cols] = gh
                low[rows, cols] = (dot(own_in[rows, :], ex[:, cols]) * gh).astype(bf16)
                ahead[rows, :] += dot2(ys[g, rows, cols] * gh, red[cols, :])
        g_out[...] = dot(c_t[...], low[...]).astype(bf16)


def back_within_kernel(gh, ahead_in, sc, cums3, cums_t, scores, exl, red, dv_out, ds_out, ahead, prod):
    g = pl.program_id(0)

    @pl.when(g == 0)
    def _():
        ds_out[...] = jnp.zeros_like(ds_out)
        ahead[...] = ahead_in[...]

    own, width = dv_out.shape
    for c in range(own // chunk):
        rows = rows_of(c)
        lcol = dot(cums3[rows, :], exl[...])
        allowed = tile_lanes(scores[0, c], 2 * lanes)
        ds = jnp.zeros((chunk, lanes), f32)
        for p in range(width // lanes):
            cols = slice(p * lanes, (p + 1) * lanes)
            e = pair_parts(lcol, cums_t[0, c], p)
            m = (e * allowed).astype(bf16)
            v = sc[rows, cols]
            dy = gh[rows, cols]
            high, low = halves(dy)
            both = two_heads(v, lanes // 2)
            parts = jnp.concatenate([high, low], axis=1)
            dm = dot_nt(parts, jnp.concatenate([both, both], axis=1))
            eds = e * dm
            ds = ds + eds[:, :lanes] + eds[:, lanes:]
            dvb = dot_tn(m, high) + dot_tn(m, low)
            lane = lax.broadcasted_iota(jnp.int32, (chunk, lanes), 1)
            dv = jnp.where(lane < lanes // 2, dvb[:chunk], dvb[chunk:])
            dv_out[rows, cols] = dv
            prod[:, cols] = v.astype(f32) * dv
        ds_out[c] += ds
        ahead[rows, :] -= dot2(prod[...], red[...])


def conv_back(cur, params, masks, rows, width):
    total = params[3:4, :] * cur[:chunk]
    for k in range(1, 4):
        shifted = pltpu.roll(cur, cur.shape[0] - k, 0)[:chunk]
        total = total + params[3 - k : 4 - k, :] * (shifted * tile_lanes(masks[k - 1, rows, :], width))
    return total


def back_state_kernel(*refs, hops):
    grads_in, refs = refs[:hops], refs[hops:]
    (states, gh, sc, dv, u, params, bc, c_t, tables, keep, decays, ex, red, ds, ahead, allowed, rows_in, masks, lx_out, gbc_out,
     ldt_out, edges, tail, db, dc, behind, direct, carry) = refs
    state = c_t.shape[0]
    g = pl.program_id(0)

    @pl.when(g == 0)
    def _():
        for ref in (db, dc, behind, direct, carry):
            ref[...] = jnp.zeros_like(ref)

    own, width = lx_out.shape
    step = min(width, 256)
    blocks = own // chunk
    for n in range(width // step):
        cols = slice(n * step, (n + 1) * step)
        gs = sum(r[:, cols].astype(f32) for r in grads_in)
        following = jnp.zeros((8, step), f32)
        for c in reversed(range(blocks)):
            rows = rows_of(c)
            low_g = gs.astype(bf16)
            kept = keep[c : c + 1, cols]
            low_s = states[c, :, cols]
            scaled = sc[rows, cols].astype(f32)
            eo = dot(tables[rows, 3 * lanes :], ex[:, cols])
            dvs = eo * dot(bc[rows, :state], low_g)
            db[rows, :] += dot_nt((eo * scaled).astype(bf16), low_g)
            dy = gh[rows, cols]
            moved = (dot(tables[rows, 2 * lanes : 3 * lanes], ex[:, cols]) * dy).astype(bf16)
            dc[rows, :] += dot_nt(moved, low_s)
            carried = jnp.sum(low_s.astype(f32) * gs, axis=0, keepdims=True) * kept
            carry[c : c + 1, :] += dot2(jnp.broadcast_to(carried, (8, step)), red[cols, :])[:1]
            gs = gs * kept + dot(c_t[:, rows], moved)
            g_sc = dv[rows, cols] + dvs
            v, slope = silu_parts(u[rows, cols])
            behind[rows, :] += dot2(scaled * dvs, red[cols, :])
            direct[rows, :] += dot2(v * g_sc, red[cols, :])
            g_v = dot(tables[rows, :lanes], ex[:, cols]) * g_sc + params[0, 6:7, cols] * dy
            g_u = g_v * slope
            g_x = conv_back(jnp.concatenate([g_u, following], axis=0), params[0, :, cols], masks, rows, step)
            lx_out[rows, cols] = g_x.astype(bf16)
            following = g_u[:8]
            if c == blocks - 1:
                tail[:, cols] = g_x[-edge:]
            if c == 0:
                at = pl.ds(pl.multiple_of(g * width + n * step, lanes), step)
                edges[:, at] = g_u[:edge].astype(bf16)

    @pl.when(g == pl.num_programs(0) - 1)
    def _():
        i = lax.broadcasted_iota(jnp.int32, (chunk, chunk), 0)
        j = lax.broadcasted_iota(jnp.int32, (chunk, chunk), 1)
        at_most = jnp.where(i <= j, 1.0, 0.0).astype(bf16)
        below = jnp.where(j < i, 1.0, 0.0).astype(bf16)
        decay_row = decays[6:7, :]
        for c in range(blocks):
            rows = rows_of(c)

            g_logs = sums3(at_most, ahead[rows, :]) + sums3(below, behind[rows, :]) + carry[c : c + 1, :]
            heads = ldt_out.shape[1]
            g_dt = (direct[rows, :] + g_logs * decay_row) * rows_in[rows, 2 * state :]
            ldt_out[rows, :] = g_dt[:, :heads].astype(bf16)
            g_scores = ds[c] * allowed[0, c]
            low_ds = g_scores.astype(bf16)
            gc = dc[rows, :] + dot(low_ds, bc[rows, :state])
            gb = db[rows, :] + dot_tn(low_ds, bc[rows, state:])
            g_bc = jnp.concatenate([gb, gc], axis=1)
            _, slope = silu_parts(rows_in[rows, : 2 * state])
            gbc_out[rows, :] = g_bc * slope
            if c == 0:
                edges[:, edges.shape[1] - g_bc.shape[1] :] = (g_bc * slope)[:edge].astype(bf16)


def in_z_kernel(lz, *refs, weights):
    ws, refs = refs[:weights], refs[weights:]
    a_up, ranks, acc, g_rank, p_up = refs

    @pl.when(pl.program_id(0) == 0)
    def _():
        acc[...] = jnp.zeros_like(acc)
        g_rank[...] = jnp.zeros_like(g_rank)

    size = g_rank.shape[1]
    g_rank[...] += dot_nt(lz[...], a_up[...])
    both = dot_tn(ranks[...], lz[...])
    p_up[0] = both[:size] + both[size:]
    with_weight(ws, lambda parts: add_times_transposed(acc, lz[...], parts), pl.program_id(0) // 2)


def in_x_kernel(sel, lx, tail, halo, a_up, ranks, params, masks, g_rank_z, p_up_z, order, normed,
                fixed, g_rank, sent, low):
    g = pl.program_id(0)

    @pl.when(g == 0)
    def _():
        g_rank[...] = g_rank_z[...]
        sent[...] = jnp.zeros_like(sent)

    own, width = low.shape
    beyond = jnp.concatenate([jnp.zeros((edge, width), f32), halo[...].astype(f32)[:8]], axis=0)
    total = tail[...]
    for k in range(1, 4):
        shifted = pltpu.roll(beyond, beyond.shape[0] - k, 0)[:edge]
        total = total + params[0, 3 - k : 4 - k, :] * (
            shifted * tile_lanes(masks[k - 1, own - edge :, :], width)
        )
    fixed[...] = total.astype(bf16)
    low[: own - edge, :] = lx[: own - edge, :]
    low[own - edge :, :] = total.astype(bf16)
    size = g_rank.shape[1]
    g_rank[...] += dot_nt(low[...], a_up[...])
    both = dot_tn(ranks[...], low[...])
    to = sel[8 + g]
    put_inner_parts(sent, to, p_up_z[0], order, 0)
    put_inner_parts(sent, to, both[:size] + both[size:], order, width // sent.shape[0])

    @pl.when(g == pl.num_programs(0) - 1)
    def _():
        put_width_parts(sent, dot2_tn(g_rank[...], normed[...]))


def tokens_kernel(sel, lx, *refs, weights):
    ws, refs = refs[:weights], refs[weights:]
    (acc_z, g_rank, gbc, halo_bc, params_bc, w_bc, ldt, dt_t, ad, masks, tokens, cot, norm_gain, grad, acc, lbc,
     g_norm) = refs
    g = pl.program_id(0)

    @pl.when(g == 0)
    def _():
        acc[...] = acc_z[...]

    with_weight(ws, lambda parts: add_times_transposed(acc, lx[...], parts), pl.program_id(0) // 2)

    @pl.when(g == pl.num_programs(0) - 1)
    def _():
        own, width = grad.shape
        blocks = own // chunk
        for c in range(blocks):
            rows = rows_of(c)
            if c < blocks - 1:
                cur = gbc[c * chunk : (c + 1) * chunk + 8, :]
            else:
                cur = jnp.concatenate([gbc[rows, :], halo_bc[...].astype(f32)[:8]], axis=0)
            lbc[rows, :] = conv_back(cur, params_bc[...], masks, rows, gbc.shape[1]).astype(bf16)
        g_norm[...] = (
            dot_nt(lbc[...], w_bc[...]) + dot(ldt[...], dt_t[...]) + dot2(g_rank[...], ad[...])
        )
        for j in range(8):
            at = pl.ds(pl.multiple_of(sel[korder[j]] * lanes, lanes), lanes)
            g_norm[:, at] += acc[:, j * lanes : (j + 1) * lanes]
        for c in range(blocks):
            rows = rows_of(c)
            wide = tokens[rows, :].astype(f32)
            scale = lax.rsqrt(jnp.sum(wide * wide, axis=1, keepdims=True) / width + epsilon)
            gn = g_norm[rows, :] * norm_gain[...]
            row_dot = jnp.sum(gn * wide, axis=1, keepdims=True)
            grad[rows, :] = (
                cot[rows, :].astype(f32) + gn * scale - wide * (scale * scale * scale * row_dot / width)
            )


def collect_kernel(picks, arrived, up_out, down_out, down_in, up_in):
    dp, tp, rows, _ = arrived.shape
    rank = rows // 4
    for b in range(up_out.shape[0]):
        total = jnp.zeros(arrived.shape[2:], f32)
        for d in range(dp):
            one = arrived[d, 0].astype(f32)
            for t in range(1, tp):
                one = one + arrived[d, t].astype(f32)
            total = total + jnp.where(picks[d] == b, one, 0.0)
        up_out[b] = total[:rank, : up_out.shape[2]]
        down_out[b] = total[rank : 2 * rank].T[: down_out.shape[1]]
        down_in[b] = total[2 * rank : 3 * rank, : down_in.shape[2]]
        up_in[b] = total[3 * rank :].T[: up_in.shape[1]]


def up(x):
    n = lax.axis_size("tensor")
    return lax.ppermute(x, "tensor", [(i, i + 1) for i in range(n - 1)])


def down(x):
    n = lax.axis_size("tensor")
    return lax.ppermute(x, "tensor", [(i + 1, i) for i in range(n - 1)])


def around_tensor(x):
    n = lax.axis_size("tensor")
    return [x] + [lax.ppermute(x, "tensor", [(i, (i + s) % n) for i in range(n)]) for s in range(1, n)]


def swap(x, bit):
    n = lax.axis_size("dp")
    return lax.ppermute(x, "dp", [(i, i ^ (1 << bit)) for i in range(n)])


def all_dp(x):
    count = lax.axis_size("dp").bit_length() - 1
    cur = x.reshape((1,) * count + x.shape)
    for bit in list(range(1, count)) + [0]:
        cur = jnp.concatenate([cur, swap(cur, bit)], axis=count - 1 - bit)
    return cur.reshape((-1,) + x.shape)


def joined_with(x, axis, bit):
    n = lax.axis_size(axis)
    return jnp.concatenate([x, lax.ppermute(x, axis, [(i, i ^ (1 << bit)) for i in range(n)])])


def after(x, *events):
    return lax.optimization_barrier((x, events))[0]


def spread_dp(rotated, events):
    out = []
    curs = [after(jnp.stack(rotated[2 * j : 2 * j + 2]), *events) for j in range(2)]
    firsts = [swap(cur, 1 + j) for j, cur in enumerate(curs)]
    pairs = [jnp.stack([cur, first]) for cur, first in zip(curs, firsts)]
    fars = [swap(pair, 2 - j) for j, pair in enumerate(pairs)]
    for pair, far in zip(pairs, fars):
        out += [pair, far, swap(pair, 0), swap(far, 0)]
    return out, firsts


def gather_plain(x):
    n, tp = lax.axis_size("dp"), lax.axis_size("tensor")
    whole = lax.all_gather(x, ("dp", "tensor")).reshape((n, tp) + x.shape)
    return [whole.transpose(1, 0, 2, 3).reshape(tp, n * x.shape[0], x.shape[1])]


def pad_lanes(x):
    return jnp.pad(x, ((0, 0), (0, lanes - x.shape[1])))


def shards(
    tokens,
    cotangent,
    doc_ids,
    adapter_pick,
    norm_gain,
    gate_x_weight,
    bc_weight,
    dt_weight,
    conv_x_weight,
    conv_bc_weight,
    conv_x_bias,
    conv_bc_bias,
    dt_bias,
    a_log,
    skip_gain,
    inner_gain,
    out_weight,
    in_down,
    in_up,
    out_down,
    out_up,
):
    dp_size, tp_size = lax.axis_size("dp"), lax.axis_size("tensor")
    both = ("dp", "tensor")
    seq_count, own, width = tokens.shape
    assert seq_count == 1 and width == 8 * lanes
    group = gate_x_weight.shape[2]
    inner = group * tp_size
    part = dt_weight.shape[1]
    heads = part * tp_size
    head_size = inner // heads
    assert head_size * 2 == lanes
    state = bc_weight.shape[1] // 2
    rank = in_down.shape[2]
    adapters = in_down.shape[0]
    hops = min(1 + (doc_most - 2) // own, tp_size - 1)
    blocks = own // chunk
    d_rows = gate_x_weight.shape[0]
    p_part = in_up.shape[4]
    hp = part * p_part
    mine, place_at = lax.axis_index("dp"), lax.axis_index("tensor")
    by_exchange = dp_size == 8 and tp_size == 4 and d_rows == lanes
    cot, tok = cotangent[0], tokens[0]

    local_x, local_z, local_out = gate_x_weight[:, 1], gate_x_weight[:, 0], out_weight.T
    if by_exchange:
        ring_x = around_tensor(local_x)

    cuts = [d_rows, d_rows, adapters * 2 * rank, adapters * 2 * rank, 16, 16]
    starts = [sum(cuts[:n]) for n in range(len(cuts))]
    if by_exchange:
        small_in = [
            bc_weight, dt_weight.T, in_down.transpose(0, 2, 1), out_up,
            in_up.transpose(0, 2, 3, 4, 1).reshape(adapters, 2 * hp, rank), out_down.reshape(adapters, hp, rank),
        ]
        vmem = pl.BlockSpec(memory_space=pltpu.VMEM)
        small = pl.pallas_call(
            pack_kernel,
            name="pack_kernel",
            out_shape=jax.ShapeDtypeStruct((sum(cuts), lanes), bf16),
            in_specs=[vmem] * 6 + [pl.BlockSpec(memory_space=pltpu.SMEM)],
            out_specs=vmem,
        )(*small_in, adapter_pick)
    else:
        small = [
            bc_weight[:, :state],
            bc_weight[:, state:],
            jnp.concatenate([in_down.transpose(0, 2, 1), out_up], axis=1).reshape(-1, d_rows),
            jnp.concatenate(
                [in_up.reshape(adapters, rank, 2 * hp),
                 jnp.pad(out_down.reshape(adapters, hp, rank).transpose(0, 2, 1), ((0, 0), (0, 0), (0, hp)))],
                axis=1,
            ).reshape(-1, 2 * hp),
            jnp.pad(dt_weight.T, ((0, 16 - part), (0, 0))),
            jnp.broadcast_to(adapter_pick.astype(bf16)[:, None], (16, lanes)),
        ]
        small = lax.all_gather(jnp.concatenate([pad_lanes(x) for x in small]), "dp")
    if by_exchange:
        natural = jnp.arange(8) ^ mine
    else:
        natural, small_at = jnp.asarray(np.argsort(korder)), jnp.arange(8)

    last = tok[-edge:].astype(f32)
    last_scale = lax.rsqrt(jnp.mean(last * last, axis=1, keepdims=True) + epsilon)
    halo_in = up((last * last_scale * norm_gain).astype(bf16))

    heads_row = jnp.pad(jnp.concatenate([dt_bias, a_log])[None], ((0, 0), (0, group - 2 * part)))
    params = jnp.concatenate(
        [conv_x_weight, conv_x_bias[None], inner_gain[None], jnp.repeat(skip_gain, head_size)[None], heads_row]
    )

    if by_exchange:
        small = joined_with(joined_with(small[None], "dp", 1), "dp", 2)
        params = jnp.stack(around_tensor(after(params, small)))
        small = jnp.concatenate([small, swap(small, 0)])
        w_x, near_x = spread_dp(ring_x, [])
        ring_z = around_tensor(after(local_z, *ring_x[1:]))
        w_z, near_z = spread_dp(ring_z, near_x)
        small_at = jnp.asarray(np.argsort(korder))[natural]
    else:
        w_x, w_z, w_out = gather_plain(local_x), gather_plain(local_z), gather_plain(local_out)
        params = jnp.stack(around_tensor(params))
    pick = adapter_pick[0]
    taken = [small[:, a : a + c] for a, c in zip(starts, cuts)]
    picks = taken[5][:, 0, 0].astype(jnp.int32)
    inner_t = lax.dynamic_slice_in_dim(taken[3], pick * 2 * rank, 2 * rank, 1)
    dt_own = taken[4][:, :part]
    if by_exchange:
        picks, dt_own = picks[small_at], dt_own[small_at]
    if d_rows != lanes:
        fold = lanes // d_rows

        def rows_first(x):
            return x.reshape(8, fold * d_rows, lanes)

        def lanes_last(x):
            x = x[:, :, :d_rows].reshape(8, fold, x.shape[1], d_rows)
            return x.transpose(0, 2, 1, 3).reshape(8, -1, lanes)

        small = jnp.concatenate([rows_first(taken[0]), rows_first(taken[1]), lanes_last(taken[2])], 1)
        dt_own = lanes_last(dt_own)
    dt_own = dt_own.transpose(1, 0, 2).reshape(part, width)
    inner_rows = inner_t.reshape(-1, lanes)
    dt_rows = dt_own.reshape(-1, lanes)
    ring = jnp.concatenate([inner_rows, dt_rows])
    ring = around_tensor(ring)
    if by_exchange:
        ring_out = around_tensor(after(local_out, *ring[1:], *ring_z[1:]))
        w_out, _ = spread_dp(ring_out, near_z)
    ring = jnp.stack(ring)
    inner_t = ring[:, : inner_rows.shape[0]].reshape(tp_size, dp_size, 2 * rank, lanes)
    dt_t = ring[:, inner_rows.shape[0] :]
    dt_t = dt_t.reshape(heads, width)

    docs = doc_ids[0]
    padded = jnp.concatenate([jnp.full((4,), -1, jnp.int32), docs, jnp.full((4,), -2, jnp.int32)])
    near = lax.dynamic_slice_in_dim(padded, place_at * own, own + 8)
    segs = jnp.stack([near[1 + k : 1 + k + own] for k in range(7)]).astype(f32).reshape(7, blocks, chunk)
    bounds = jnp.stack([near[3 : 3 + own : chunk], near[3 + chunk :: chunk][:blocks]], axis=1).reshape(-1)
    groups = (place_at - jnp.arange(tp_size)) % tp_size
    sel = jnp.concatenate([natural, groups, jnp.arange(tp_size), pick[None], bounds, small_at]).astype(jnp.int32)

    def spread(width_each, copies):
        out = np.zeros((lanes, heads * width_each), np.float32)
        at = np.arange(heads * width_each)
        for n in range(copies):
            out[n * heads + at // width_each, at] = 1.0
        return jnp.asarray(out, bf16)

    ex, exl = spread(head_size, 2), spread(lanes, 3)
    red = jnp.asarray(np.arange(inner)[:, None] // head_size == np.arange(lanes)[None, :], bf16)
    at = np.arange(group)
    place = np.zeros((dp_size, hp, group), np.float32)
    place[at % head_size // p_part, at // head_size * p_part + at % p_part, at] = 1.0
    order = jnp.asarray(place.reshape(group, group).T, bf16)
    place = jnp.asarray(place, bf16)

    def full(*shape):
        return pl.BlockSpec(shape, lambda *s: (0,) * len(shape))

    def cols(rows, size=group, turn=0):
        return pl.BlockSpec((rows, size), lambda g, *s: (0, (g + turn) % tp_size))

    def stacked(*shape, base=0):
        return pl.BlockSpec((1,) + shape, lambda g, *s: (g + base,) + (0,) * len(shape))

    def params_at(base=0):
        return stacked(8, group, base=base)

    def weight_specs(ws, half=None):
        if len(ws) == 1:
            base = (half or 0) * tp_size // 2
            return [pl.BlockSpec((1,) + ws[0].shape[1:], lambda g, s: (s[8 + base + g], 0, 0))]
        shape = (2, 1) + ws[0].shape[2:]
        if half is not None:
            return [pl.BlockSpec(shape, lambda g, *s: (0, g, 0, 0))] * 4
        first = pl.BlockSpec(shape, lambda g, *s: (0, jnp.minimum(g, 1), 0, 0))
        second = pl.BlockSpec(shape, lambda g, *s: (0, jnp.maximum(g - 2, 0), 0, 0))
        return [first] * 4 + [second] * 4

    def call(kernel, out, in_specs, out_specs, scratch, flops, moved, steps=tp_size, grant=vmem_bytes, in_place=None):
        kernel, kernel_takes_sel, name = kernel

        def body(sel_ref, *refs):
            return kernel(sel_ref, *refs) if kernel_takes_sel else kernel(*refs)

        return pl.pallas_call(
            body,
            name=name,
            input_output_aliases={1 + i: to for i, to in (in_place or {}).items()},
            out_shape=[jax.ShapeDtypeStruct(s, d) for s, d in out],
            grid_spec=pltpu.PrefetchScalarGridSpec(
                num_scalar_prefetch=1,
                grid=steps if isinstance(steps, tuple) else (steps,),
                in_specs=in_specs,
                out_specs=out_specs,
                scratch_shapes=scratch,
            ),
            compiler_params=pltpu.CompilerParams(
                dimension_semantics=("arbitrary",) * (len(steps) if isinstance(steps, tuple) else 1),
                vmem_limit_bytes=grant,
            ),
            cost_estimate=pl.CostEstimate(flops=flops, bytes_accessed=moved, transcendentals=0),
        )

    def plain(kernel, **static):
        return (lambda *refs: kernel(*refs, **static)), False, kernel.__name__

    def selecting(kernel, **static):
        return (lambda *refs: kernel(*refs, **static)), True, kernel.__name__

    n_w = len(w_x)
    big = (own, inner)
    ext = own + edge
    mat = 2 * own * width * inner
    mega = 1 << 20
    params_bc = jnp.concatenate([conv_bc_weight, conv_bc_bias[None], jnp.zeros((3, 2 * state), f32)])
    prep_out = [
        ((ext, width), bf16), ((own, width), bf16), ((ext, 2 * rank), bf16), ((own, 2 * rank), bf16),
        ((own, 6 * lanes), bf16), ((own, 2 * state), bf16),
        ((2 * state, own), bf16), ((2, blocks, chunk, chunk), f32), ((own, 2 * state + lanes), f32),
        ((tp_size, blocks, part, chunk), f32), ((8, inner), f32), ((5 * rank, inner), bf16),
        ((2 * rank, width), bf16), ((width, 2 * state), bf16), ((6, own, lanes), f32),
    ]
    prep_in = [tok, halo_in, norm_gain[None], small, dt_t, inner_t, place, params, params_bc, segs, ex]
    normed_moved, normed, ranks, ranks_own, tables, bc, bc_t, scores, rows_f32, cums_t, keep, ups, wides, w_bc, masks = call(
        selecting(prep_kernel, rank=rank, state=state, moved_blocks=by_exchange),
        prep_out,
        [full(*x.shape) for x in prep_in],
        [full(*s) for s, _ in prep_out],
        [pltpu.VMEM((ext, width), bf16)],
        mat // 4, 6 * mega, 1, grant=vmem_bytes * 5 // 4,
    )(sel, *prep_in)

    def part_at(row, col, *shape):
        return pl.BlockSpec(shape, lambda *s: (row, col))

    def up_at(row, rows, base=0):
        return pl.BlockSpec((rows, group), lambda g, *s: (row, g + base))

    def first_at(row, *shape):
        return pl.BlockSpec(shape, lambda g, *s: (row,) + (0,) * (len(shape) - 1))

    scores_spec, allowed_spec = (first_at(n, 1, blocks, chunk, chunk) for n in range(2))
    b_t_spec, c_t_spec = part_at(0, 0, state, own), part_at(1, 0, state, own)
    masks_spec, masks_after_spec = first_at(0, 3, own, lanes), first_at(1, 3, own, lanes)
    ad_spec, b_up_spec = part_at(0, 0, rank, width), part_at(1, 0, rank, width)
    chunk_rows = stacked(blocks, part, chunk)
    z_specs = weight_specs(w_z)
    p_spec = params_at()
    order_spec = full(group, group)
    u, scaled, sent_state = call(
        plain(proj_kernel, weights=n_w),
        [(big, f32), (big, bf16), ((state, inner), bf16)],
        [full(ext, width)] + weight_specs(w_x)
        + [full(ext, 2 * rank), up_at(1, 2 * rank), p_spec, masks_spec, part_at(0, 0, own, 2 * lanes), cols(lanes),
           b_t_spec],
        [cols(own), cols(own), cols(state)],
        [pltpu.VMEM((ext, group), f32), pltpu.VMEM((own, group), bf16)],
        mat, 12 * mega, grant=vmem_bytes * 5 // 4,
    )(sel, normed_moved, *w_x, ranks, ups, params, masks, tables, ex, bc_t)

    def chain(x, step, sign, *events):
        out, moved = [step(x)], x
        for hop in range(1, hops):
            kept = jnp.roll(keep[7:8], sign * hop * group, axis=1)
            moved = (after(out[-1], *events).astype(f32) * kept).astype(bf16)
            out.append(step(moved))
        return out, moved

    within_specs = [cols(own), part_at(0, 5, own, lanes), chunk_rows, scores_spec, cols(lanes, part * lanes)]
    states_in, moved_state = chain(sent_state, up, -1)
    (y_within,) = call(
        plain(within_kernel), [(big, f32)], within_specs, [cols(own)], [], mat, 6 * mega
    )(sel, after(scaled, moved_state), tables, cums_t, scores, exl)

    states_spec = pl.BlockSpec((blocks, state, group), lambda g, *s: (0, 0, g))
    def steps_in(phase, first, then):
        return lambda p, g: jnp.where(p == phase, g, jnp.where(p < phase, first, then))

    def moving(phase, make):
        at = steps_in(phase, 0, tp_size - 1)
        return lambda p, g, s: make(at(p, g), s)

    def cols_in(phase, rows, size=group, turn=0):
        return pl.BlockSpec((rows, size), moving(phase, lambda i, s: (0, (i + turn) % tp_size)))

    def up_in(phase, row, rows):
        return pl.BlockSpec((rows, group), moving(phase, lambda i, s: (row, i)))

    def weights_in(phase, ws):
        if len(ws) == 1:
            return [pl.BlockSpec((1,) + ws[0].shape[1:], moving(phase, lambda i, s: (s[8 + i], 0, 0)))]
        shape = (2, 1) + ws[0].shape[2:]
        first = pl.BlockSpec(shape, moving(phase, lambda i, s: (0, jnp.minimum(i, 1), 0, 0)))
        second = pl.BlockSpec(shape, moving(phase, lambda i, s: (0, jnp.maximum(i - 2, 0), 0, 0)))
        return [first] * 4 + [second] * 4

    def cols_always(rows, size):
        return pl.BlockSpec((rows, size), lambda p, g, s: (0, g))

    sent_shape = (dp_size, tp_size, 2 * rank, max(d_rows, 2 * hp))
    cot = cotangent[0]
    big3 = (tp_size, own, group)
    states, mixed, sent_out, g_heads, low_z, sent_grad, ahead_sums = call(
        selecting(middle_kernel, weights=n_w, hops=hops, inner=inner),
        [((blocks, state, inner), bf16), ((own, width), f32), (sent_shape, bf16), (big, f32), (big, bf16),
         ((state, inner), bf16), ((own, lanes), f32)],
        [full(ext, width)] + weights_in(0, w_z) + weights_in(1, w_out)
        + [cols_in(0, state, group, -h) for h in range(1, hops + 1)]
        + [full(own, 2 * rank), up_in(0, 0, 2 * rank), pl.BlockSpec((1, 8, group), lambda p, g, s: (g, 0, 0)),
           cols_in(0, own), cols_in(0, own), cols_in(0, own), part_at(0, 1, own, 2 * lanes),
           part_at(0, 4, own, lanes), cols_in(0, 8), cols_always(lanes, group), b_t_spec, c_t_spec,
           part_at(0, 1, own, state), full(own, width), full(own, width), b_up_spec, up_in(1, 4, rank), order_spec,
           pl.BlockSpec((group, lanes), moving(2, lambda i, s: (i, 0)))],
        [pl.BlockSpec((blocks, state, group), moving(0, lambda i, s: (0, 0, i))), full(own, width),
         full(*sent_shape), cols_in(2, own), cols_in(2, own), cols_in(2, state), full(own, lanes)],
        [pltpu.VMEM(big3, f32), pltpu.VMEM(big3, f32), pltpu.VMEM(big3, f32), pltpu.VMEM(big3, f32),
         pltpu.VMEM(big3, f32),
         pltpu.VMEM((own, lanes), f32), pltpu.VMEM((own, lanes), f32), pltpu.VMEM((own, width), f32),
         pltpu.VMEM((own, width), bf16), pltpu.VMEM((own, rank), f32), pltpu.VMEM((own, rank), f32),
         pltpu.VMEM((own, group), bf16)],
        4 * mat, 40 * mega, (3, tp_size), grant=vmem_bytes * 5 // 4,
    )(sel, normed_moved, *w_z, *w_out, *states_in, ranks_own, ups, params, y_within, u, scaled, tables, tables, keep,
      ex, bc_t, bc_t, bc, cot, tok, wides, ups, order, red)
    red_spec = pl.BlockSpec((group, lanes), lambda g, *s: (g, 0))
    d_within, d_scores, ahead = call(
        plain(back_within_kernel),
        [(big, f32), ((blocks, chunk, chunk), f32), ((own, lanes), f32)],
        [cols(own), full(own, lanes)] + within_specs + [red_spec],
        [cols(own), full(blocks, chunk, chunk), full(own, lanes)],
        [pltpu.VMEM((chunk, group), f32)],
        2 * mat, 14 * mega, grant=vmem_bytes * 5 // 4,
    )(sel, g_heads, ahead_sums, scaled, tables, cums_t, scores, exl, red)
    grads_in, moved_grad = chain(sent_grad, down, 1, ahead)
    low_z = after(low_z, moved_grad)

    acc_z, g_rank_z, p_up_z = call(
        plain(in_z_kernel, weights=n_w),
        [((own, width), f32), ((own, rank), f32), ((tp_size, rank, group), f32)],
        [cols(own)] + z_specs + [up_at(0, rank), full(own, 2 * rank)],
        [full(own, width), full(own, rank), stacked(rank, group)],
        [],
        mat, 8 * mega,
    )(sel, low_z, *w_z, ups, ranks_own)

    grads_in = [after(x, acc_z) for x in grads_in]
    edges_shape = (edge, inner + 2 * state)
    low_x, g_u_bc, low_dt, edges, tail = call(
        plain(back_state_kernel, hops=hops),
        [(big, bf16), ((own, 2 * state), f32), ((own, heads), bf16), (edges_shape, bf16), ((edge, inner), f32)],
        [cols(state, group, h) for h in range(1, hops + 1)]
        + [states_spec, cols(own), cols(own), cols(own), cols(own), p_spec, full(own, 2 * state), c_t_spec,
           part_at(0, 0, own, 4 * lanes), cols(8), part_at(0, 0, 8, lanes), cols(lanes), red_spec,
           full(blocks, chunk, chunk), full(own, lanes), allowed_spec, full(own, 2 * state + lanes),
           masks_after_spec],
        [cols(own), full(own, 2 * state), full(own, heads), full(*edges_shape), cols(edge)],
        [pltpu.VMEM((own, state), f32), pltpu.VMEM((own, state), f32), pltpu.VMEM((own, lanes), f32),
         pltpu.VMEM((own, lanes), f32), pltpu.VMEM((8, lanes), f32)],
        mat, 24 * mega,
    )(sel, *grads_in, states, g_heads, scaled, d_within, u, params, bc, bc_t, tables, keep, keep, ex, red, d_scores,
      ahead, scores, rows_f32, masks)

    halo = down(edges)
    low_x, g_rank, sent_in = call(
        selecting(in_x_kernel),
        [(big, bf16), ((own, rank), f32), (sent_shape, bf16)],
        [cols(own), cols(edge), cols(edge, group, 1), up_at(2, rank), full(own, 2 * rank), p_spec, masks_after_spec,
         full(own, rank), stacked(rank, group), order_spec, full(own, width)],
        [pl.BlockSpec((edge, group), lambda g, *s: (own // edge - 1, g)), full(own, rank), full(*sent_shape)],
        [pltpu.VMEM((own, group), bf16)],
        mat // 8, 8 * mega, in_place={0: 0},
    )(sel, low_x, tail, halo, ups, ranks_own, params, masks, g_rank_z, p_up_z, order, normed)

    (tokens_grad,) = call(
        selecting(tokens_kernel, weights=n_w),
        [((own, width), f32)],
        [cols(own)] + weight_specs(w_x)
        + [full(own, width), full(own, rank), full(own, 2 * state),
           pl.BlockSpec((edge, 2 * state), lambda g, *s: (0, inner // (2 * state))),
           full(8, 2 * state), full(width, 2 * state), full(own, heads), full(heads, width), ad_spec,
           masks_after_spec, full(own, width), full(own, width), full(1, width)],
        [full(own, width)],
        [pltpu.VMEM((own, width), f32), pltpu.VMEM((own, 2 * state), bf16), pltpu.VMEM((own, width), f32)],
        mat, 14 * mega, grant=vmem_bytes * 5 // 4,
    )(sel, low_x, *w_x, acc_z, g_rank, g_u_bc, halo, params_bc, w_bc, low_dt, dt_t, wides, masks, tok, cot,
      norm_gain[None])

    sent = jnp.concatenate([sent_out, sent_in], axis=2)
    arrived = lax.all_to_all(sent.reshape((-1,) + sent.shape[2:]), both, 0, 0, tiled=True)
    arrived = arrived.reshape(sent.shape)
    shapes = [(adapters, rank, d_rows), (adapters, hp, rank), (adapters, rank, d_rows), (adapters, 2 * hp, rank)]
    grad_out_up, grad_out_down, grad_in_down, grad_in_up = call(
        selecting(collect_kernel), [(s, f32) for s in shapes], [full(*sent.shape)],
        [full(*s) for s in shapes], [], mega, mega, 1,
    )(picks, arrived)

    grad_out_down = grad_out_down.reshape(out_down.shape)
    grad_in_down = grad_in_down.transpose(0, 2, 1)
    grad_in_up = grad_in_up.reshape(adapters, 2, part, p_part, rank).transpose(0, 4, 1, 2, 3)
    return (mixed[None], tokens_grad[None], grad_in_down, grad_in_up, grad_out_down, grad_out_up)


def solution(mesh):
    placed = (
        P("dp", "tensor", None),
        P("dp", "tensor", None),
        P("dp", None),
        P("dp"),
        P(),
        P("dp", None, "tensor"),
        P("dp", None),
        P("dp", "tensor"),
        P(None, "tensor"),
        P(),
        P("tensor"),
        P(),
        P("tensor"),
        P("tensor"),
        P("tensor"),
        P("tensor"),
        P("tensor", "dp"),
        P(None, "dp", None),
        P(None, None, None, "tensor", "dp"),
        P(None, "tensor", "dp", None),
        P(None, None, "dp"),
    )
    return jax.shard_map(
        shards,
        mesh=mesh,
        in_specs=placed,
        out_specs=(
            P("dp", "tensor", None),
            P("dp", "tensor", None),
            P(None, "dp", None),
            P(None, None, None, "tensor", "dp"),
            P(None, "tensor", "dp", None),
            P(None, None, "dp"),
        ),
        check_vma=False,
    )
```

```python
import math

import jax
import jax.numpy as jnp
import numpy as np
from jax import lax
from jax.experimental import pallas as pl
from jax.experimental.pallas import tpu as pltpu
from jax.sharding import PartitionSpec as P

epsilon = 1e-05
chunk = 128
lanes = 128
doc_most = 800
edge = 16
f32, bf16 = jnp.float32, jnp.bfloat16
exact = lax.Precision.HIGHEST
vmem_bytes = 48 * 1024 * 1024


def dot(a, b):
    return jnp.dot(a, b, preferred_element_type=f32)


def dot_nt(a, b):
    return lax.dot_general(a, b, (((1,), (1,)), ((), ())), preferred_element_type=f32)


def dot_tn(a, b):
    return lax.dot_general(a, b, (((0,), (0,)), ((), ())), preferred_element_type=f32)


def halves(x):
    high = x.astype(bf16)
    return high, (x - high.astype(f32)).astype(bf16)


def pieces(x, count):
    out = []
    for _ in range(count):
        part = lax.reduce_precision(x, 8, 7)
        out.append(part.astype(bf16))
        x = x - part
    return jnp.concatenate(out, axis=-1)


def dot2(x, w):
    high, low = halves(x)
    return dot(high, w) + dot(low, w)


def dot2_nt(x, w):
    high, low = halves(x)
    return dot_nt(high, w) + dot_nt(low, w)


def dot2_tn(x, w):
    high, low = halves(x)
    return dot_tn(high, w) + dot_tn(low, w)


def tile_lanes(m, width):
    return m if width == lanes else jnp.concatenate([m] * (width // lanes), axis=1)


def sigmoid(u):
    return 0.5 + 0.5 * jnp.tanh(0.5 * u)


def silu(u):
    return u * sigmoid(u)


def silu_parts(u):
    s = sigmoid(u)
    v = u * s
    return v, s + v * (1.0 - s)


korder = (0, 2, 4, 6, 1, 3, 5, 7)


def weight_pieces(refs, at=0):
    if len(refs) == 1:
        return [(refs[0][...].reshape(-1, refs[0].shape[-1]), None)]
    pairs = ((0, 1), (2, 3), (4, 5), (6, 7)) if at == 0 else ((0, 2), (1, 3), (4, 6), (5, 7))
    return [
        (ref[...].reshape(2 * lanes, ref.shape[-1]), pair) for ref, pair in zip(refs[4 * at : 4 * at + 4], pairs)
    ]


def block_at(n):
    return slice(n * lanes, (n + 1) * lanes)


def with_weight(refs, body, half):
    if len(refs) == 1:
        body(weight_pieces(refs))
        return
    if isinstance(half, int):
        body(weight_pieces(refs * 2, half))
        return

    @pl.when(half == 0)
    def _():
        body(weight_pieces(refs, 0))

    @pl.when(half == 1)
    def _():
        body(weight_pieces(refs, 1))


def times(left, parts):
    total = None
    for w, pair in parts:
        if pair is None:
            value = left(slice(None))
        elif pair[1] == pair[0] + 1:
            value = left(slice(pair[0] * lanes, (pair[1] + 1) * lanes))
        else:
            value = jnp.concatenate([left(block_at(n)) for n in pair], axis=1)
        term = dot(value, w)
        total = term if total is None else total + term
    return total


def add_times_transposed(acc, low, parts):
    for w, pair in parts:
        term = dot_nt(low, w)
        if pair is None:
            acc[...] += term
        elif pair[1] == pair[0] + 1:
            acc[:, pair[0] * lanes : (pair[1] + 1) * lanes] += term
        else:
            for i, n in enumerate(pair):
                acc[:, block_at(n)] += term[:, block_at(i)]


def rows_of(c):
    return slice(c * chunk, (c + 1) * chunk)


def sums3(tri, x):
    high, mid = halves(x)
    low = (x - high.astype(f32) - mid.astype(f32)).astype(bf16)
    return dot(tri, high) + dot(tri, mid) + dot(tri, low)


def parts_of(x, count):
    out = []
    for _ in range(count):
        part = x.astype(bf16)
        out.append(part)
        x = x - part.astype(f32)
    return jnp.concatenate(out, axis=1)


def table_of(x, count):
    parts = parts_of(x, count)
    return jnp.concatenate([parts, jnp.zeros((x.shape[0], lanes - parts.shape[1]), bf16)], axis=1)


def column(row):
    return jnp.broadcast_to(row, (lanes, lanes)).T


def prep_kernel(sel, tokens, halo, norm_gain, small, dt_t, inner_t, place, params, params_bc, segs, ex, no_out,
                normed, ranks, ranks_own, tables, bc_out, bct_out, scores, rows_out, cums_t, keep, ups, wides, w_bc,
                masks, ext, *, rank, state, moved_blocks):
    own, width = tokens.shape
    blocks = own // chunk
    tp, _, group = params.shape
    heads = dt_t.shape[0]
    part = heads // tp
    bc_rows = 2 * lanes
    turn, pick, bound, small_at = 8 + tp, sel[8 + 2 * tp], 9 + 2 * tp, 9 + 2 * tp + 2 * blocks

    for c in range(blocks):
        wide = tokens[rows_of(c), :].astype(f32)
        scale = lax.rsqrt(jnp.sum(wide * wide, axis=1, keepdims=True) / width + epsilon)
        ext[edge + c * chunk : edge + (c + 1) * chunk, :] = (wide * scale * norm_gain[...]).astype(bf16)
    ext[:edge, :] = halo[...]
    for j in range(8):
        k = korder[j]
        at = pl.ds(pl.multiple_of(sel[k] * lanes, lanes), lanes)
        cols = slice(j * lanes, (j + 1) * lanes)
        no_out[:, cols] = ext[:, at]
        at = sel[small_at + j]
        wides[:, cols] = small[at, pl.ds(pl.multiple_of(bc_rows + pick * 2 * rank, 2 * rank), 2 * rank), :]
        w_bc[j * lanes : (j + 1) * lanes, :state] = small[at, :lanes, :]
        w_bc[j * lanes : (j + 1) * lanes, state:] = small[at, lanes : 2 * lanes, :]
    normed[...] = ext[edge:, :]
    ranks[...] = parts_of(dot_nt(ext[...], wides[:rank, :]), 2)
    ranks_own[...] = ranks[edge:, :]
    bc = dot(ext[...], w_bc[...])

    hp = place.shape[1]
    for s in range(tp):
        cols = slice(s * group, (s + 1) * group)
        z = x = d = None
        for k in range(inner_t.shape[1]):
            where = place[sel[korder[k]]] if moved_blocks else place[k]
            piece = inner_t[sel[turn + s], k]
            terms = (dot(piece[:rank, :hp], where), dot(piece[:rank, hp : 2 * hp], where),
                     dot(piece[rank:, :hp], where))
            z, x, d = terms if z is None else (z + terms[0], x + terms[1], d + terms[2])
        z, x = z.astype(bf16), x.astype(bf16)
        ups[:, cols] = jnp.concatenate([z, z, x, x, d.astype(bf16)], axis=0)

    i = lax.broadcasted_iota(jnp.int32, (chunk, chunk), 0)
    j = lax.broadcasted_iota(jnp.int32, (chunk, chunk), 1)
    tril = jnp.where(j <= i, 1.0, 0.0)
    segs_at = []
    for c in range(blocks):
        rows = rows_of(c)
        seg = column(segs[3, c : c + 1, :])
        segs_at.append(seg[:, :heads])
        for k in range(1, 4):
            masks[k - 1, rows, :] = jnp.where(column(segs[3 - k, c : c + 1, :]) == seg, 1.0, 0.0)
            masks[k + 2, rows, :] = jnp.where(column(segs[3 + k, c : c + 1, :]) == seg, 1.0, 0.0)
        cur = bc[edge + c * chunk - 8 : edge + (c + 1) * chunk]
        total = params_bc[3:4, :] * cur[8:] + params_bc[4:5, :]
        for k in range(1, 4):
            shifted = pltpu.roll(cur, k, 0)[8:]
            total = total + params_bc[3 - k : 4 - k, :] * (
                shifted * tile_lanes(masks[k - 1, rows, :], 2 * state)
            )
        rows_out[rows, : 2 * state] = total
        value = silu(total)
        inb, inc = value[:, :state], value[:, state:]
        bc_out[rows, :] = value.astype(bf16)
        bct_out[:state, rows] = inb.T.astype(bf16)
        bct_out[state:, rows] = inc.T.astype(bf16)
        okay = jnp.where(seg == segs[3, c : c + 1, :], tril, 0.0)
        scores[1, c] = okay
        scores[0, c] = dot_nt(inc.astype(bf16), inb.astype(bf16)) * okay

    bias = jnp.concatenate([params[sel[turn + s], 7:8, :part] for s in range(tp)], axis=1)
    a_log = jnp.concatenate([params[sel[turn + s], 7:8, part : 2 * part] for s in range(tp)], axis=1)
    decays = -jnp.exp(a_log)
    raw = dot_nt(ext[edge:, :], dt_t[...]) + bias
    dt = jnp.maximum(raw, 0.0) + jnp.log1p(jnp.exp(-jnp.abs(raw)))
    rows_out[:, 2 * state :] = jnp.concatenate([sigmoid(raw), jnp.zeros((own, lanes - heads), f32)], axis=1)
    tables[:, :lanes] = table_of(dt, 2)
    logs = dt * decays * math.log2(math.e)
    bounds = [sel[bound + n].astype(f32) for n in range(2 * blocks)]
    before_seg, last_seg = bounds[0], bounds[-1]
    prior = jnp.zeros((1, heads), f32)
    all_cums, keeps = [], []
    tri = tril.astype(bf16)
    for c in range(blocks):
        rows = rows_of(c)
        before_c, last_c = bounds[2 * c], bounds[2 * c + 1]
        cums = sums3(tri, logs[rows])
        end = cums[chunk - 1 : chunk]
        seg = segs_at[c]
        tables[rows, 5 * lanes :] = table_of(cums, 3)
        flipped = jnp.concatenate([cums, jnp.zeros((chunk, lanes - heads), f32)], axis=1).T
        for s in range(tp):
            cums_t[s, c] = flipped[s * part : (s + 1) * part]
        tables[rows, 2 * lanes : 3 * lanes] = table_of(jnp.where(seg == before_c, jnp.exp2(cums), 0.0), 2)
        tables[rows, 3 * lanes : 4 * lanes] = table_of(jnp.where(seg == last_c, jnp.exp2(end - cums), 0.0), 2)
        keeps.append(jnp.where(before_c == last_c, jnp.exp2(end), 0.0))
        all_cums.append(cums + prior)
        prior = prior + end
    for c in range(blocks):
        rows = rows_of(c)
        seg = segs_at[c]
        tables[rows, 4 * lanes : 5 * lanes] = table_of(jnp.where(seg == before_seg, jnp.exp2(all_cums[c]), 0.0), 2)
        tables[rows, lanes : 2 * lanes] = table_of(jnp.where(seg == last_seg, jnp.exp2(prior - all_cums[c]), 0.0), 2)
    whole = jnp.where(before_seg == last_seg, jnp.exp2(prior), 0.0)
    table = jnp.concatenate(keeps + [jnp.zeros((7 - blocks, heads), f32), whole], axis=0)
    high, mid = halves(table)
    low = (table - high.astype(f32) - mid.astype(f32)).astype(bf16)
    spread = ex[:heads, :]
    keep[...] = dot(high, spread) + dot(mid, spread) + dot(low, spread)
    keep[6:7, :lanes] = jnp.concatenate([decays, jnp.zeros((1, lanes - heads), f32)], axis=1)


def pack_kernel(bc, dt_weight, in_down, out_up, in_up, out_down, pick, out):
    rows, two = bc.shape
    part = dt_weight.shape[0]
    count, rank, _ = in_down.shape
    at = 2 * rows
    out[:rows, :] = bc[:, : two // 2]
    out[rows:at, :] = bc[:, two // 2 :]
    for b in range(count):
        out[at + 2 * rank * b : at + 2 * rank * b + rank, :] = in_down[b]
        out[at + 2 * rank * b + rank : at + 2 * rank * (b + 1), :] = out_up[b]
    at += 2 * rank * count
    for b in range(count):
        out[at + 2 * rank * b : at + 2 * rank * b + rank, :] = in_up[b].astype(f32).T.astype(bf16)
        flipped = out_down[b].astype(f32).T
        out[at + 2 * rank * b + rank : at + 2 * rank * (b + 1), :] = jnp.concatenate(
            [flipped, jnp.zeros_like(flipped)], axis=1
        ).astype(bf16)
    at += 2 * rank * count
    wide = jnp.concatenate([dt_weight[...].astype(f32), jnp.zeros((16 - part, rows), f32)], axis=0)
    out[at : at + 16, :] = wide.astype(bf16)
    out[at + 16 : at + 32, :] = jnp.zeros((16, lanes), bf16) + pick[0].astype(f32).astype(bf16)


def proj_kernel(left, *refs, weights):
    refs, ws = refs[weights:], refs[:weights]
    ranks, a_up, params, masks, tables, ex, b_t, u_out, sc_out, f_out, xs, moved = refs

    def body(parts):
        xs[...] = times(lambda at: left[:, at], parts) + dot(ranks[...], a_up[...])

    with_weight(ws, body, pl.program_id(0) // 2)
    own, width = u_out.shape
    step = min(width, 256)
    dt_wide, out_wide = dot(tables[:, :lanes], ex[...]), dot(tables[:, lanes:], ex[...])
    for c in range(own // chunk):
        rows = rows_of(c)
        for n in range(width // step):
            cols = slice(n * step, (n + 1) * step)
            cur = xs[edge + c * chunk - 8 : edge + (c + 1) * chunk, cols]
            total = params[0, 3:4, cols] * cur[8:] + params[0, 4:5, cols]
            for k in range(1, 4):
                shifted = pltpu.roll(cur, k, 0)[8:]
                total = total + params[0, 3 - k : 4 - k, cols] * (
                    shifted * tile_lanes(masks[k - 1, rows, :], step)
                )
            u_out[rows, cols] = total
            value = silu(total)
            scaled = (dt_wide[rows, cols] * value).astype(bf16)
            sc_out[rows, cols] = scaled
            moved[rows, cols] = (out_wide[rows, cols] * scaled.astype(f32)).astype(bf16)
    f_out[...] = dot(b_t[...], moved[...]).astype(bf16)

def pair_parts(lcol, cums_t, p):
    lc = lcol[:, p * 2 * lanes : (p + 1) * 2 * lanes]
    lr = jnp.concatenate([cums_t[2 * p : 2 * p + 1, :], cums_t[2 * p + 1 : 2 * p + 2, :]], axis=1)
    return jnp.exp2(jnp.minimum(lc - lr, 0.0))


def two_heads(v, head_size):
    lane = lax.broadcasted_iota(jnp.int32, v.shape, 1)
    zero = jnp.zeros_like(v)
    return jnp.concatenate([jnp.where(lane < head_size, v, zero), jnp.where(lane < head_size, zero, v)], 0)


def within_kernel(sc, cums3, cums_t, scores, exl, y_out):
    own, width = y_out.shape
    wide = dot(cums3[...], exl[...])
    for c in range(own // chunk):
        rows = rows_of(c)
        lcol = wide[rows]
        allowed = tile_lanes(scores[0, c], 2 * lanes)
        for p in range(width // lanes):
            e = pair_parts(lcol, cums_t[0, c], p)
            m = (e * allowed).astype(bf16)
            cols = slice(p * lanes, (p + 1) * lanes)
            y_out[rows, cols] = dot(m, two_heads(sc[rows, cols], lanes // 2))


def row_scale_of(sumsq, inner):
    return lax.rsqrt(jnp.sum(sumsq, axis=1, keepdims=True) / inner + epsilon)


def put_width_parts(sent, value):
    rank = value.shape[0]
    dp, tp, _, _ = sent.shape
    size = value.shape[1] // dp
    for d in range(dp):
        piece = value[:, d * size : (d + 1) * size].astype(bf16)
        for t in range(tp):
            sent[d, t, :rank, :size] = piece


def put_inner_parts(sent, to, value, order, offset):
    rank = value.shape[0]
    dp = sent.shape[0]
    hp = value.shape[1] // dp
    moved = dot(value.astype(bf16), order[...]).astype(bf16)
    for d in range(dp):
        sent[d, to, rank : 2 * rank, offset : offset + hp] = moved[:, d * hp : (d + 1) * hp]


def middle_kernel(sel, left, *refs, weights, hops, inner):
    zs, outs, refs = refs[:weights], refs[weights : 2 * weights], refs[2 * weights :]
    s_ins, refs = refs[:hops], refs[hops:]
    (ranks, a_up, params, yw, u, sc, tables, own_in, keep, ex, b_t, c_t, in_c, cot, tokens, b_up, b_down, order, red,
     states, mixed, sent, gh_out, lz_out, g_out, ahead,
     ys, heads, gate_z, gated, gg, sumsq, dots, acc, cots, g_rank, rank, low) = refs
    phase, g = pl.program_id(0), pl.program_id(1)
    last = pl.num_programs(1) - 1
    half = g // 2
    own, width = gh_out.shape
    step = min(width, 256)
    blocks = own // chunk

    @pl.when((phase == 0) & (g == 0))
    def _():
        ahead[...] = jnp.zeros_like(ahead)
        sumsq[...] = jnp.zeros_like(sumsq)
        acc[...] = jnp.zeros_like(acc)
        rank[...] = jnp.zeros_like(rank)
        dots[...] = jnp.zeros_like(dots)
        sent[...] = jnp.zeros_like(sent)
        for j in range(8):
            at = pl.ds(pl.multiple_of(sel[korder[j]] * lanes, lanes), lanes)
            cots[:, j * lanes : (j + 1) * lanes] = cot[:, at]
        g_rank[...] = parts_of(dot_nt(cot[...], b_up[...]), 2)

    @pl.when(phase == 0)
    def _():
        def body(parts):
            first = left.shape[0] - own
            gate_z[g] = times(lambda at: left[first:, at], parts) + dot(ranks[...], a_up[...])

        with_weight(zs, body, half)
        in_wide, out_wide = dot(tables[:, :lanes], ex[...]), dot(tables[:, lanes:], ex[...])
        for n in range(width // step):
            cols = slice(n * step, (n + 1) * step)
            new = []
            for c in range(blocks):
                rows = rows_of(c)
                moved = (out_wide[rows, cols] * sc[rows, cols].astype(f32)).astype(bf16)
                new.append(dot(b_t[:, rows], moved))
            s = sum(r[:, cols].astype(f32) for r in s_ins)
            for c in range(blocks):
                states[c, :, cols] = s.astype(bf16)
                s = s * keep[c : c + 1, cols] + new[c]
            for c in range(blocks):
                rows = rows_of(c)
                y = yw[rows, cols] + in_wide[rows, cols] * dot(in_c[rows, :], states[c, :, cols])
                ys[g, rows, cols] = y
                head = y + params[0, 6:7, cols] * silu(u[rows, cols])
                heads[g, rows, cols] = head
                gd = head * silu(gate_z[g, rows, cols])
                gated[g, rows, cols] = gd
                sq = gd * gd
                total = sumsq[rows, :]
                for i in range(step // lanes):
                    total = total + sq[:, i * lanes : (i + 1) * lanes]
                sumsq[rows, :] = total

    @pl.when(phase == 1)
    def _():
        scale = row_scale_of(sumsq[...], inner)
        normed_inner = gated[g] * scale * params[0, 5:6, :]
        high, rest = halves(normed_inner)
        low[...] = high
        rank[...] += dot_nt(high, b_down[...]) + dot_nt(rest, b_down[...])
        size = rank.shape[1]
        both = dot_tn(g_rank[...], high)
        put_inner_parts(sent, sel[8 + g], both[:size] + both[size:], order, 0)

        def body(parts):
            twice = jnp.concatenate([b_down[...], b_down[...]], axis=0)
            value = (times(lambda at: cots[:, at], parts) + dot(g_rank[...], twice)) * params[0, 5:6, :]
            gg[g] = value
            prod = value * gated[g]
            total = dots[...]
            for i in range(width // lanes):
                total = total + prod[:, i * lanes : (i + 1) * lanes]
            dots[...] = total
            add_times_transposed(acc, low[...], parts)

        with_weight(outs, body, half)

    @pl.when((phase == 1) & (g == last))
    def _():
        put_width_parts(sent, dot2_tn(rank[...], cot[...]))
        mixed[...] = tokens[...].astype(f32) + dot2(rank[...], b_up[...])
        for j in range(8):
            at = pl.ds(pl.multiple_of(sel[korder[j]] * lanes, lanes), lanes)
            mixed[:, at] += acc[:, j * lanes : (j + 1) * lanes]

    @pl.when(phase == 2)
    def _():
        scale = row_scale_of(sumsq[...], inner)
        coef = scale * scale * scale * (jnp.sum(dots[...], axis=1, keepdims=True) / inner)
        own_wide = dot(own_in[...], ex[...])
        for c in range(blocks):
            rows = rows_of(c)
            sc_rows, co_rows = scale[rows], coef[rows]
            for n in range(width // step):
                cols = slice(n * step, (n + 1) * step)
                g_gated = gg[g, rows, cols] * sc_rows - gated[g, rows, cols] * co_rows
                gate, slope = silu_parts(gate_z[g, rows, cols])
                lz_out[rows, cols] = (g_gated * heads[g, rows, cols] * slope).astype(bf16)
                gh = g_gated * gate
                gh_out[rows, cols] = gh
                low[rows, cols] = (own_wide[rows, cols] * gh).astype(bf16)
                ys[g, rows, cols] = ys[g, rows, cols] * gh
        ahead[...] += dot2(ys[g], red[...])
        g_out[...] = dot(c_t[...], low[...]).astype(bf16)


def back_within_kernel(gh, ahead_in, sc, cums3, cums_t, scores, exl, red, dv_out, ds_out, ahead, prod):
    g = pl.program_id(0)

    @pl.when(g == 0)
    def _():
        ds_out[...] = jnp.zeros_like(ds_out)
        ahead[...] = ahead_in[...]

    own, width = dv_out.shape
    wide = dot(cums3[...], exl[...])
    for c in range(own // chunk):
        rows = rows_of(c)
        lcol = wide[rows]
        allowed = tile_lanes(scores[0, c], 2 * lanes)
        ds = jnp.zeros((chunk, lanes), f32)
        for p in range(width // lanes):
            cols = slice(p * lanes, (p + 1) * lanes)
            e = pair_parts(lcol, cums_t[0, c], p)
            m = (e * allowed).astype(bf16)
            v = sc[rows, cols]
            dy = gh[rows, cols]
            high, low = halves(dy)
            both = two_heads(v, lanes // 2)
            parts = jnp.concatenate([high, low], axis=1)
            dm = dot_nt(parts, jnp.concatenate([both, both], axis=1))
            eds = e * dm
            ds = ds + eds[:, :lanes] + eds[:, lanes:]
            dvb = dot_tn(m, high) + dot_tn(m, low)
            lane = lax.broadcasted_iota(jnp.int32, (chunk, lanes), 1)
            dv = jnp.where(lane < lanes // 2, dvb[:chunk], dvb[chunk:])
            dv_out[rows, cols] = dv
            prod[rows, cols] = v.astype(f32) * dv
        ds_out[c] += ds
    ahead[...] -= dot2(prod[...], red[...])


def conv_back(cur, params, masks, rows, width):
    total = params[3:4, :] * cur[:chunk]
    for k in range(1, 4):
        shifted = pltpu.roll(cur, cur.shape[0] - k, 0)[:chunk]
        total = total + params[3 - k : 4 - k, :] * (shifted * tile_lanes(masks[k - 1, rows, :], width))
    return total


def back_state_kernel(*refs, hops):
    grads_in, refs = refs[:hops], refs[hops:]
    (states, gh, sc, dv, u, params, bc, c_t, tables, keep, decays, ex, red, ds, ahead, allowed, rows_in, masks, lx_out, gbc_out,
     ldt_out, edges, tail, db, dc, behind, direct, carry, prods, carries) = refs
    state = c_t.shape[0]
    g = pl.program_id(0)

    @pl.when(g == 0)
    def _():
        for ref in (db, dc, behind, direct, carry, carries):
            ref[...] = jnp.zeros_like(ref)

    own, width = lx_out.shape
    step = min(width, 256)
    blocks = own // chunk
    dt_wide, in_wide = dot(tables[:, :lanes], ex[...]), dot(tables[:, 2 * lanes : 3 * lanes], ex[...])
    out_wide = dot(tables[:, 3 * lanes :], ex[...])
    for n in range(width // step):
        cols = slice(n * step, (n + 1) * step)
        gs = sum(r[:, cols].astype(f32) for r in grads_in)
        following = jnp.zeros((8, step), f32)
        for c in reversed(range(blocks)):
            rows = rows_of(c)
            low_g = gs.astype(bf16)
            kept = keep[c : c + 1, cols]
            low_s = states[c, :, cols]
            scaled = sc[rows, cols].astype(f32)
            eo = out_wide[rows, cols]
            dvs = eo * dot(bc[rows, :state], low_g)
            db[rows, :] += dot_nt((eo * scaled).astype(bf16), low_g)
            dy = gh[rows, cols]
            moved = (in_wide[rows, cols] * dy).astype(bf16)
            dc[rows, :] += dot_nt(moved, low_s)
            carried = jnp.sum(low_s.astype(f32) * gs, axis=0, keepdims=True) * kept
            carries[c : c + 1, cols] = carried
            gs = gs * kept + dot(c_t[:, rows], moved)
            g_sc = dv[rows, cols] + dvs
            v, slope = silu_parts(u[rows, cols])
            prods[0, rows, cols] = scaled * dvs
            prods[1, rows, cols] = v * g_sc
            g_v = dt_wide[rows, cols] * g_sc + params[0, 6:7, cols] * dy
            g_u = g_v * slope
            g_x = conv_back(jnp.concatenate([g_u, following], axis=0), params[0, :, cols], masks, rows, step)
            lx_out[rows, cols] = g_x.astype(bf16)
            following = g_u[:8]
            if c == blocks - 1:
                tail[:, cols] = g_x[-edge:]
            if c == 0:
                at = pl.ds(pl.multiple_of(g * width + n * step, lanes), step)
                edges[:, at] = g_u[:edge].astype(bf16)
    behind[...] += dot2(prods[0], red[...])
    direct[...] += dot2(prods[1], red[...])
    carry[...] += dot2(carries[...], red[...])

    @pl.when(g == pl.num_programs(0) - 1)
    def _():
        i = lax.broadcasted_iota(jnp.int32, (chunk, chunk), 0)
        j = lax.broadcasted_iota(jnp.int32, (chunk, chunk), 1)
        at_most = jnp.where(i <= j, 1.0, 0.0).astype(bf16)
        below = jnp.where(j < i, 1.0, 0.0).astype(bf16)
        decay_row = decays[6:7, :]
        for c in range(blocks):
            rows = rows_of(c)

            g_logs = sums3(at_most, ahead[rows, :]) + sums3(below, behind[rows, :]) + carry[c : c + 1, :]
            heads = ldt_out.shape[1]
            g_dt = (direct[rows, :] + g_logs * decay_row) * rows_in[rows, 2 * state :]
            ldt_out[rows, :] = g_dt[:, :heads].astype(bf16)
            g_scores = ds[c] * allowed[0, c]
            low_ds = g_scores.astype(bf16)
            gc = dc[rows, :] + dot(low_ds, bc[rows, :state])
            gb = db[rows, :] + dot_tn(low_ds, bc[rows, state:])
            g_bc = jnp.concatenate([gb, gc], axis=1)
            _, slope = silu_parts(rows_in[rows, : 2 * state])
            gbc_out[rows, :] = g_bc * slope
            if c == 0:
                edges[:, edges.shape[1] - g_bc.shape[1] :] = (g_bc * slope)[:edge].astype(bf16)


def in_z_kernel(lz, *refs, weights):
    ws, refs = refs[:weights], refs[weights:]
    a_up, ranks, acc, g_rank, p_up = refs

    @pl.when(pl.program_id(0) == 0)
    def _():
        acc[...] = jnp.zeros_like(acc)
        g_rank[...] = jnp.zeros_like(g_rank)

    size = g_rank.shape[1]
    g_rank[...] += dot_nt(lz[...], a_up[...])
    both = dot_tn(ranks[...], lz[...])
    p_up[0] = both[:size] + both[size:]
    with_weight(ws, lambda parts: add_times_transposed(acc, lz[...], parts), pl.program_id(0) // 2)


def in_x_kernel(sel, lx, tail, halo, a_up, ranks, params, masks, g_rank_z, p_up_z, order, normed,
                fixed, g_rank, sent, low):
    g = pl.program_id(0)

    @pl.when(g == 0)
    def _():
        g_rank[...] = g_rank_z[...]
        sent[...] = jnp.zeros_like(sent)

    own, width = low.shape
    beyond = jnp.concatenate([jnp.zeros((edge, width), f32), halo[...].astype(f32)[:8]], axis=0)
    total = tail[...]
    for k in range(1, 4):
        shifted = pltpu.roll(beyond, beyond.shape[0] - k, 0)[:edge]
        total = total + params[0, 3 - k : 4 - k, :] * (
            shifted * tile_lanes(masks[k - 1, own - edge :, :], width)
        )
    fixed[...] = total.astype(bf16)
    low[: own - edge, :] = lx[: own - edge, :]
    low[own - edge :, :] = total.astype(bf16)
    size = g_rank.shape[1]
    g_rank[...] += dot_nt(low[...], a_up[...])
    both = dot_tn(ranks[...], low[...])
    to = sel[8 + g]
    put_inner_parts(sent, to, p_up_z[0], order, 0)
    put_inner_parts(sent, to, both[:size] + both[size:], order, width // sent.shape[0])

    @pl.when(g == pl.num_programs(0) - 1)
    def _():
        put_width_parts(sent, dot2_tn(g_rank[...], normed[...]))


def tokens_kernel(sel, lx, *refs, weights):
    ws, refs = refs[:weights], refs[weights:]
    (acc_z, g_rank, gbc, halo_bc, params_bc, w_bc, ldt, dt_t, ad, masks, tokens, cot, norm_gain, grad, acc, lbc,
     g_norm) = refs
    g = pl.program_id(0)

    @pl.when(g == 0)
    def _():
        acc[...] = acc_z[...]

    with_weight(ws, lambda parts: add_times_transposed(acc, lx[...], parts), pl.program_id(0) // 2)

    @pl.when(g == pl.num_programs(0) - 1)
    def _():
        own, width = grad.shape
        blocks = own // chunk
        for c in range(blocks):
            rows = rows_of(c)
            if c < blocks - 1:
                cur = gbc[c * chunk : (c + 1) * chunk + 8, :]
            else:
                cur = jnp.concatenate([gbc[rows, :], halo_bc[...].astype(f32)[:8]], axis=0)
            lbc[rows, :] = conv_back(cur, params_bc[...], masks, rows, gbc.shape[1]).astype(bf16)
        g_norm[...] = (
            dot_nt(lbc[...], w_bc[...]) + dot(ldt[...], dt_t[...]) + dot2(g_rank[...], ad[...])
        )
        for j in range(8):
            at = pl.ds(pl.multiple_of(sel[korder[j]] * lanes, lanes), lanes)
            g_norm[:, at] += acc[:, j * lanes : (j + 1) * lanes]
        for c in range(blocks):
            rows = rows_of(c)
            wide = tokens[rows, :].astype(f32)
            scale = lax.rsqrt(jnp.sum(wide * wide, axis=1, keepdims=True) / width + epsilon)
            gn = g_norm[rows, :] * norm_gain[...]
            row_dot = jnp.sum(gn * wide, axis=1, keepdims=True)
            grad[rows, :] = (
                cot[rows, :].astype(f32) + gn * scale - wide * (scale * scale * scale * row_dot / width)
            )


def collect_kernel(picks, arrived, up_out, down_out, down_in, up_in, sums):
    dp, tp, rows, _ = arrived.shape
    rank = rows // 4
    for d in range(dp):
        one = arrived[d, 0].astype(f32)
        for t in range(1, tp):
            one = one + arrived[d, t].astype(f32)
        sums[d] = one
    for b in range(up_out.shape[0]):
        total = jnp.zeros(arrived.shape[2:], f32)
        for d in range(dp):
            total = total + jnp.where(picks[d] == b, sums[d], 0.0)
        up_out[b] = total[:rank, : up_out.shape[2]]
        down_out[b] = total[rank : 2 * rank].T[: down_out.shape[1]]
        down_in[b] = total[2 * rank : 3 * rank, : down_in.shape[2]]
        up_in[b] = total[3 * rank :].T[: up_in.shape[1]]


def up(x):
    n = lax.axis_size("tensor")
    return lax.ppermute(x, "tensor", [(i, i + 1) for i in range(n - 1)])


def down(x):
    n = lax.axis_size("tensor")
    return lax.ppermute(x, "tensor", [(i + 1, i) for i in range(n - 1)])


def around_tensor(x):
    n = lax.axis_size("tensor")
    return [x] + [lax.ppermute(x, "tensor", [(i, (i + s) % n) for i in range(n)]) for s in range(1, n)]


def swap(x, bit):
    n = lax.axis_size("dp")
    return lax.ppermute(x, "dp", [(i, i ^ (1 << bit)) for i in range(n)])


def all_dp(x):
    count = lax.axis_size("dp").bit_length() - 1
    cur = x.reshape((1,) * count + x.shape)
    for bit in list(range(1, count)) + [0]:
        cur = jnp.concatenate([cur, swap(cur, bit)], axis=count - 1 - bit)
    return cur.reshape((-1,) + x.shape)


def joined_with(x, axis, bit):
    n = lax.axis_size(axis)
    return jnp.concatenate([x, lax.ppermute(x, axis, [(i, i ^ (1 << bit)) for i in range(n)])])


def after(x, *events):
    return lax.optimization_barrier((x, events))[0]


def spread_dp(rotated, events):
    out = []
    curs = [after(jnp.stack(rotated[2 * j : 2 * j + 2]), *events) for j in range(2)]
    firsts = [swap(cur, 1 + j) for j, cur in enumerate(curs)]
    pairs = [jnp.stack([cur, first]) for cur, first in zip(curs, firsts)]
    fars = [swap(pair, 2 - j) for j, pair in enumerate(pairs)]
    for pair, far in zip(pairs, fars):
        out += [pair, far, swap(pair, 0), swap(far, 0)]
    return out, firsts


def gather_plain(x):
    n, tp = lax.axis_size("dp"), lax.axis_size("tensor")
    whole = lax.all_gather(x, ("dp", "tensor")).reshape((n, tp) + x.shape)
    return [whole.transpose(1, 0, 2, 3).reshape(tp, n * x.shape[0], x.shape[1])]


def pad_lanes(x):
    return jnp.pad(x, ((0, 0), (0, lanes - x.shape[1])))


def shards(
    tokens,
    cotangent,
    doc_ids,
    adapter_pick,
    norm_gain,
    gate_x_weight,
    bc_weight,
    dt_weight,
    conv_x_weight,
    conv_bc_weight,
    conv_x_bias,
    conv_bc_bias,
    dt_bias,
    a_log,
    skip_gain,
    inner_gain,
    out_weight,
    in_down,
    in_up,
    out_down,
    out_up,
):
    dp_size, tp_size = lax.axis_size("dp"), lax.axis_size("tensor")
    both = ("dp", "tensor")
    seq_count, own, width = tokens.shape
    assert seq_count == 1 and width == 8 * lanes
    group = gate_x_weight.shape[2]
    inner = group * tp_size
    part = dt_weight.shape[1]
    heads = part * tp_size
    head_size = inner // heads
    assert head_size * 2 == lanes
    state = bc_weight.shape[1] // 2
    rank = in_down.shape[2]
    adapters = in_down.shape[0]
    hops = min(1 + (doc_most - 2) // own, tp_size - 1)
    blocks = own // chunk
    d_rows = gate_x_weight.shape[0]
    p_part = in_up.shape[4]
    hp = part * p_part
    mine, place_at = lax.axis_index("dp"), lax.axis_index("tensor")
    by_exchange = dp_size == 8 and tp_size == 4 and d_rows == lanes
    cot, tok = cotangent[0], tokens[0]

    local_x, local_z, local_out = gate_x_weight[:, 1], gate_x_weight[:, 0], out_weight.T
    if by_exchange:
        ring_x = around_tensor(local_x)

    cuts = [d_rows, d_rows, adapters * 2 * rank, adapters * 2 * rank, 16, 16]
    starts = [sum(cuts[:n]) for n in range(len(cuts))]
    if by_exchange:
        small_in = [
            bc_weight, dt_weight.T, in_down.transpose(0, 2, 1), out_up,
            in_up.transpose(0, 2, 3, 4, 1).reshape(adapters, 2 * hp, rank), out_down.reshape(adapters, hp, rank),
        ]
        vmem = pl.BlockSpec(memory_space=pltpu.VMEM)
        small = pl.pallas_call(
            pack_kernel,
            name="pack_kernel",
            out_shape=jax.ShapeDtypeStruct((sum(cuts), lanes), bf16),
            in_specs=[vmem] * 6 + [pl.BlockSpec(memory_space=pltpu.SMEM)],
            out_specs=vmem,
        )(*small_in, adapter_pick)
    else:
        small = [
            bc_weight[:, :state],
            bc_weight[:, state:],
            jnp.concatenate([in_down.transpose(0, 2, 1), out_up], axis=1).reshape(-1, d_rows),
            jnp.concatenate(
                [in_up.reshape(adapters, rank, 2 * hp),
                 jnp.pad(out_down.reshape(adapters, hp, rank).transpose(0, 2, 1), ((0, 0), (0, 0), (0, hp)))],
                axis=1,
            ).reshape(-1, 2 * hp),
            jnp.pad(dt_weight.T, ((0, 16 - part), (0, 0))),
            jnp.broadcast_to(adapter_pick.astype(bf16)[:, None], (16, lanes)),
        ]
        small = lax.all_gather(jnp.concatenate([pad_lanes(x) for x in small]), "dp")
    if by_exchange:
        natural = jnp.arange(8) ^ mine
    else:
        natural, small_at = jnp.asarray(np.argsort(korder)), jnp.arange(8)

    last = tok[-edge:].astype(f32)
    last_scale = lax.rsqrt(jnp.mean(last * last, axis=1, keepdims=True) + epsilon)
    halo_in = up((last * last_scale * norm_gain).astype(bf16))

    heads_row = jnp.pad(jnp.concatenate([dt_bias, a_log])[None], ((0, 0), (0, group - 2 * part)))
    params = jnp.concatenate(
        [conv_x_weight, conv_x_bias[None], inner_gain[None], jnp.repeat(skip_gain, head_size)[None], heads_row]
    )

    if by_exchange:
        small = joined_with(joined_with(small[None], "dp", 1), "dp", 2)
        params = jnp.stack(around_tensor(after(params, small)))
        small = jnp.concatenate([small, swap(small, 0)])
        w_x, near_x = spread_dp(ring_x, [])
        ring_z = around_tensor(after(local_z, *ring_x[1:]))
        w_z, near_z = spread_dp(ring_z, near_x)
        small_at = jnp.asarray(np.argsort(korder))[natural]
    else:
        w_x, w_z, w_out = gather_plain(local_x), gather_plain(local_z), gather_plain(local_out)
        params = jnp.stack(around_tensor(params))
    pick = adapter_pick[0]
    taken = [small[:, a : a + c] for a, c in zip(starts, cuts)]
    picks = taken[5][:, 0, 0].astype(jnp.int32)
    inner_t = lax.dynamic_slice_in_dim(taken[3], pick * 2 * rank, 2 * rank, 1)
    dt_own = taken[4][:, :part]
    if by_exchange:
        picks, dt_own = picks[small_at], dt_own[small_at]
    if d_rows != lanes:
        fold = lanes // d_rows

        def rows_first(x):
            return x.reshape(8, fold * d_rows, lanes)

        def lanes_last(x):
            x = x[:, :, :d_rows].reshape(8, fold, x.shape[1], d_rows)
            return x.transpose(0, 2, 1, 3).reshape(8, -1, lanes)

        small = jnp.concatenate([rows_first(taken[0]), rows_first(taken[1]), lanes_last(taken[2])], 1)
        dt_own = lanes_last(dt_own)
    dt_own = dt_own.transpose(1, 0, 2).reshape(part, width)
    inner_rows = inner_t.reshape(-1, lanes)
    dt_rows = dt_own.reshape(-1, lanes)
    ring = jnp.concatenate([inner_rows, dt_rows])
    ring = around_tensor(ring)
    if by_exchange:
        ring_out = around_tensor(after(local_out, *ring[1:], *ring_z[1:]))
        w_out, _ = spread_dp(ring_out, near_z)
    ring = jnp.stack(ring)
    inner_t = ring[:, : inner_rows.shape[0]].reshape(tp_size, dp_size, 2 * rank, lanes)
    dt_t = ring[:, inner_rows.shape[0] :]
    dt_t = dt_t.reshape(heads, width)

    docs = doc_ids[0]
    padded = jnp.concatenate([jnp.full((4,), -1, jnp.int32), docs, jnp.full((4,), -2, jnp.int32)])
    near = lax.dynamic_slice_in_dim(padded, place_at * own, own + 8)
    segs = jnp.stack([near[1 + k : 1 + k + own] for k in range(7)]).astype(f32).reshape(7, blocks, chunk)
    bounds = jnp.stack([near[3 : 3 + own : chunk], near[3 + chunk :: chunk][:blocks]], axis=1).reshape(-1)
    groups = (place_at - jnp.arange(tp_size)) % tp_size
    sel = jnp.concatenate([natural, groups, jnp.arange(tp_size), pick[None], bounds, small_at]).astype(jnp.int32)

    def spread(width_each, copies):
        out = np.zeros((lanes, heads * width_each), np.float32)
        at = np.arange(heads * width_each)
        for n in range(copies):
            out[n * heads + at // width_each, at] = 1.0
        return jnp.asarray(out, bf16)

    ex, exl = spread(head_size, 2), spread(lanes, 3)
    red = jnp.asarray(np.arange(inner)[:, None] // head_size == np.arange(lanes)[None, :], bf16)
    at = np.arange(group)
    place = np.zeros((dp_size, hp, group), np.float32)
    place[at % head_size // p_part, at // head_size * p_part + at % p_part, at] = 1.0
    order = jnp.asarray(place.reshape(group, group).T, bf16)
    place = jnp.asarray(place, bf16)

    def full(*shape):
        return pl.BlockSpec(shape, lambda *s: (0,) * len(shape))

    def cols(rows, size=group, turn=0):
        return pl.BlockSpec((rows, size), lambda g, *s: (0, (g + turn) % tp_size))

    def stacked(*shape, base=0):
        return pl.BlockSpec((1,) + shape, lambda g, *s: (g + base,) + (0,) * len(shape))

    def params_at(base=0):
        return stacked(8, group, base=base)

    def weight_specs(ws, half=None):
        if len(ws) == 1:
            base = (half or 0) * tp_size // 2
            return [pl.BlockSpec((1,) + ws[0].shape[1:], lambda g, s: (s[8 + base + g], 0, 0))]
        shape = (2, 1) + ws[0].shape[2:]
        if half is not None:
            return [pl.BlockSpec(shape, lambda g, *s: (0, g, 0, 0))] * 4
        first = pl.BlockSpec(shape, lambda g, *s: (0, jnp.minimum(g, 1), 0, 0))
        second = pl.BlockSpec(shape, lambda g, *s: (0, jnp.maximum(g - 2, 0), 0, 0))
        return [first] * 4 + [second] * 4

    def call(kernel, out, in_specs, out_specs, scratch, flops, moved, steps=tp_size, grant=vmem_bytes, in_place=None):
        kernel, kernel_takes_sel, name = kernel

        def body(sel_ref, *refs):
            return kernel(sel_ref, *refs) if kernel_takes_sel else kernel(*refs)

        return pl.pallas_call(
            body,
            name=name,
            input_output_aliases={1 + i: to for i, to in (in_place or {}).items()},
            out_shape=[jax.ShapeDtypeStruct(s, d) for s, d in out],
            grid_spec=pltpu.PrefetchScalarGridSpec(
                num_scalar_prefetch=1,
                grid=steps if isinstance(steps, tuple) else (steps,),
                in_specs=in_specs,
                out_specs=out_specs,
                scratch_shapes=scratch,
            ),
            compiler_params=pltpu.CompilerParams(
                dimension_semantics=("arbitrary",) * (len(steps) if isinstance(steps, tuple) else 1),
                vmem_limit_bytes=grant,
            ),
            cost_estimate=pl.CostEstimate(flops=flops, bytes_accessed=moved, transcendentals=0),
        )

    def plain(kernel, **static):
        return (lambda *refs: kernel(*refs, **static)), False, kernel.__name__

    def selecting(kernel, **static):
        return (lambda *refs: kernel(*refs, **static)), True, kernel.__name__

    n_w = len(w_x)
    big = (own, inner)
    ext = own + edge
    mat = 2 * own * width * inner
    mega = 1 << 20
    params_bc = jnp.concatenate([conv_bc_weight, conv_bc_bias[None], jnp.zeros((3, 2 * state), f32)])
    prep_out = [
        ((ext, width), bf16), ((own, width), bf16), ((ext, 2 * rank), bf16), ((own, 2 * rank), bf16),
        ((own, 6 * lanes), bf16), ((own, 2 * state), bf16),
        ((2 * state, own), bf16), ((2, blocks, chunk, chunk), f32), ((own, 2 * state + lanes), f32),
        ((tp_size, blocks, part, chunk), f32), ((8, inner), f32), ((5 * rank, inner), bf16),
        ((2 * rank, width), bf16), ((width, 2 * state), bf16), ((6, own, lanes), f32),
    ]
    prep_in = [tok, halo_in, norm_gain[None], small, dt_t, inner_t, place, params, params_bc, segs, ex]
    normed_moved, normed, ranks, ranks_own, tables, bc, bc_t, scores, rows_f32, cums_t, keep, ups, wides, w_bc, masks = call(
        selecting(prep_kernel, rank=rank, state=state, moved_blocks=by_exchange),
        prep_out,
        [full(*x.shape) for x in prep_in],
        [full(*s) for s, _ in prep_out],
        [pltpu.VMEM((ext, width), bf16)],
        mat // 4, 6 * mega, 1, grant=vmem_bytes * 5 // 4,
    )(sel, *prep_in)

    def part_at(row, col, *shape):
        return pl.BlockSpec(shape, lambda *s: (row, col))

    def up_at(row, rows, base=0):
        return pl.BlockSpec((rows, group), lambda g, *s: (row, g + base))

    def first_at(row, *shape):
        return pl.BlockSpec(shape, lambda g, *s: (row,) + (0,) * (len(shape) - 1))

    scores_spec, allowed_spec = (first_at(n, 1, blocks, chunk, chunk) for n in range(2))
    b_t_spec, c_t_spec = part_at(0, 0, state, own), part_at(1, 0, state, own)
    masks_spec, masks_after_spec = first_at(0, 3, own, lanes), first_at(1, 3, own, lanes)
    ad_spec, b_up_spec = part_at(0, 0, rank, width), part_at(1, 0, rank, width)
    chunk_rows = stacked(blocks, part, chunk)
    z_specs = weight_specs(w_z)
    p_spec = params_at()
    order_spec = full(group, group)
    u, scaled, sent_state = call(
        plain(proj_kernel, weights=n_w),
        [(big, f32), (big, bf16), ((state, inner), bf16)],
        [full(ext, width)] + weight_specs(w_x)
        + [full(ext, 2 * rank), up_at(1, 2 * rank), p_spec, masks_spec, part_at(0, 0, own, 2 * lanes), cols(lanes),
           b_t_spec],
        [cols(own), cols(own), cols(state)],
        [pltpu.VMEM((ext, group), f32), pltpu.VMEM((own, group), bf16)],
        mat, 12 * mega, grant=vmem_bytes * 5 // 4,
    )(sel, normed_moved, *w_x, ranks, ups, params, masks, tables, ex, bc_t)

    def chain(x, step, sign, *events):
        out, moved = [step(x)], x
        for hop in range(1, hops):
            kept = jnp.roll(keep[7:8], sign * hop * group, axis=1)
            moved = (after(out[-1], *events).astype(f32) * kept).astype(bf16)
            out.append(step(moved))
        return out, moved

    within_specs = [cols(own), part_at(0, 5, own, lanes), chunk_rows, scores_spec, cols(lanes, part * lanes)]
    states_in, moved_state = chain(sent_state, up, -1)
    (y_within,) = call(
        plain(within_kernel), [(big, f32)], within_specs, [cols(own)], [], mat, 6 * mega
    )(sel, after(scaled, moved_state), tables, cums_t, scores, exl)

    states_spec = pl.BlockSpec((blocks, state, group), lambda g, *s: (0, 0, g))
    def steps_in(phase, first, then):
        return lambda p, g: jnp.where(p == phase, g, jnp.where(p < phase, first, then))

    def moving(phase, make):
        at = steps_in(phase, 0, tp_size - 1)
        return lambda p, g, s: make(at(p, g), s)

    def cols_in(phase, rows, size=group, turn=0):
        return pl.BlockSpec((rows, size), moving(phase, lambda i, s: (0, (i + turn) % tp_size)))

    def up_in(phase, row, rows):
        return pl.BlockSpec((rows, group), moving(phase, lambda i, s: (row, i)))

    def weights_in(phase, ws):
        if len(ws) == 1:
            return [pl.BlockSpec((1,) + ws[0].shape[1:], moving(phase, lambda i, s: (s[8 + i], 0, 0)))]
        shape = (2, 1) + ws[0].shape[2:]
        first = pl.BlockSpec(shape, moving(phase, lambda i, s: (0, jnp.minimum(i, 1), 0, 0)))
        second = pl.BlockSpec(shape, moving(phase, lambda i, s: (0, jnp.maximum(i - 2, 0), 0, 0)))
        return [first] * 4 + [second] * 4

    def cols_always(rows, size):
        return pl.BlockSpec((rows, size), lambda p, g, s: (0, g))

    sent_shape = (dp_size, tp_size, 2 * rank, max(d_rows, 2 * hp))
    cot = cotangent[0]
    big3 = (tp_size, own, group)
    states, mixed, sent_out, g_heads, low_z, sent_grad, ahead_sums = call(
        selecting(middle_kernel, weights=n_w, hops=hops, inner=inner),
        [((blocks, state, inner), bf16), ((own, width), f32), (sent_shape, bf16), (big, f32), (big, bf16),
         ((state, inner), bf16), ((own, lanes), f32)],
        [full(ext, width)] + weights_in(0, w_z) + weights_in(1, w_out)
        + [cols_in(0, state, group, -h) for h in range(1, hops + 1)]
        + [full(own, 2 * rank), up_in(0, 0, 2 * rank), pl.BlockSpec((1, 8, group), lambda p, g, s: (g, 0, 0)),
           cols_in(0, own), cols_in(0, own), cols_in(0, own), part_at(0, 1, own, 2 * lanes),
           part_at(0, 4, own, lanes), cols_in(0, 8), cols_always(lanes, group), b_t_spec, c_t_spec,
           part_at(0, 1, own, state), full(own, width), full(own, width), b_up_spec, up_in(1, 4, rank), order_spec,
           pl.BlockSpec((group, lanes), moving(2, lambda i, s: (i, 0)))],
        [pl.BlockSpec((blocks, state, group), moving(0, lambda i, s: (0, 0, i))), full(own, width),
         full(*sent_shape), cols_in(2, own), cols_in(2, own), cols_in(2, state), full(own, lanes)],
        [pltpu.VMEM(big3, f32), pltpu.VMEM(big3, f32), pltpu.VMEM(big3, f32), pltpu.VMEM(big3, f32),
         pltpu.VMEM(big3, f32),
         pltpu.VMEM((own, lanes), f32), pltpu.VMEM((own, lanes), f32), pltpu.VMEM((own, width), f32),
         pltpu.VMEM((own, width), bf16), pltpu.VMEM((own, 2 * rank), bf16), pltpu.VMEM((own, rank), f32),
         pltpu.VMEM((own, group), bf16)],
        4 * mat, 40 * mega, (3, tp_size), grant=vmem_bytes * 5 // 4,
    )(sel, normed_moved, *w_z, *w_out, *states_in, ranks_own, ups, params, y_within, u, scaled, tables, tables, keep,
      ex, bc_t, bc_t, bc, cot, tok, wides, ups, order, red)
    red_spec = pl.BlockSpec((group, lanes), lambda g, *s: (g, 0))
    d_within, d_scores, ahead = call(
        plain(back_within_kernel),
        [(big, f32), ((blocks, chunk, chunk), f32), ((own, lanes), f32)],
        [cols(own), full(own, lanes)] + within_specs + [red_spec],
        [cols(own), full(blocks, chunk, chunk), full(own, lanes)],
        [pltpu.VMEM((own, group), f32)],
        2 * mat, 14 * mega, grant=vmem_bytes * 5 // 4,
    )(sel, g_heads, ahead_sums, scaled, tables, cums_t, scores, exl, red)
    grads_in, moved_grad = chain(sent_grad, down, 1, ahead)
    low_z = after(low_z, moved_grad)

    acc_z, g_rank_z, p_up_z = call(
        plain(in_z_kernel, weights=n_w),
        [((own, width), f32), ((own, rank), f32), ((tp_size, rank, group), f32)],
        [cols(own)] + z_specs + [up_at(0, rank), full(own, 2 * rank)],
        [full(own, width), full(own, rank), stacked(rank, group)],
        [],
        mat, 8 * mega,
    )(sel, low_z, *w_z, ups, ranks_own)

    grads_in = [after(x, acc_z) for x in grads_in]
    edges_shape = (edge, inner + 2 * state)
    low_x, g_u_bc, low_dt, edges, tail = call(
        plain(back_state_kernel, hops=hops),
        [(big, bf16), ((own, 2 * state), f32), ((own, heads), bf16), (edges_shape, bf16), ((edge, inner), f32)],
        [cols(state, group, h) for h in range(1, hops + 1)]
        + [states_spec, cols(own), cols(own), cols(own), cols(own), p_spec, full(own, 2 * state), c_t_spec,
           part_at(0, 0, own, 4 * lanes), cols(8), part_at(0, 0, 8, lanes), cols(lanes), red_spec,
           full(blocks, chunk, chunk), full(own, lanes), allowed_spec, full(own, 2 * state + lanes),
           masks_after_spec],
        [cols(own), full(own, 2 * state), full(own, heads), full(*edges_shape), cols(edge)],
        [pltpu.VMEM((own, state), f32), pltpu.VMEM((own, state), f32), pltpu.VMEM((own, lanes), f32),
         pltpu.VMEM((own, lanes), f32), pltpu.VMEM((8, lanes), f32), pltpu.VMEM((2, own, group), f32),
         pltpu.VMEM((8, group), f32)],
        mat, 24 * mega,
    )(sel, *grads_in, states, g_heads, scaled, d_within, u, params, bc, bc_t, tables, keep, keep, ex, red, d_scores,
      ahead, scores, rows_f32, masks)

    halo = down(edges)
    low_x, g_rank, sent_in = call(
        selecting(in_x_kernel),
        [(big, bf16), ((own, rank), f32), (sent_shape, bf16)],
        [cols(own), cols(edge), cols(edge, group, 1), up_at(2, rank), full(own, 2 * rank), p_spec, masks_after_spec,
         full(own, rank), stacked(rank, group), order_spec, full(own, width)],
        [pl.BlockSpec((edge, group), lambda g, *s: (own // edge - 1, g)), full(own, rank), full(*sent_shape)],
        [pltpu.VMEM((own, group), bf16)],
        mat // 8, 8 * mega, in_place={0: 0},
    )(sel, low_x, tail, halo, ups, ranks_own, params, masks, g_rank_z, p_up_z, order, normed)

    (tokens_grad,) = call(
        selecting(tokens_kernel, weights=n_w),
        [((own, width), f32)],
        [cols(own)] + weight_specs(w_x)
        + [full(own, width), full(own, rank), full(own, 2 * state),
           pl.BlockSpec((edge, 2 * state), lambda g, *s: (0, inner // (2 * state))),
           full(8, 2 * state), full(width, 2 * state), full(own, heads), full(heads, width), ad_spec,
           masks_after_spec, full(own, width), full(own, width), full(1, width)],
        [full(own, width)],
        [pltpu.VMEM((own, width), f32), pltpu.VMEM((own, 2 * state), bf16), pltpu.VMEM((own, width), f32)],
        mat, 14 * mega, grant=vmem_bytes * 5 // 4,
    )(sel, low_x, *w_x, acc_z, g_rank, g_u_bc, halo, params_bc, w_bc, low_dt, dt_t, wides, masks, tok, cot,
      norm_gain[None])

    sent = jnp.concatenate([sent_out, sent_in], axis=2)
    arrived = lax.all_to_all(sent.reshape((-1,) + sent.shape[2:]), both, 0, 0, tiled=True)
    arrived = arrived.reshape(sent.shape)
    shapes = [(adapters, rank, d_rows), (adapters, hp, rank), (adapters, rank, d_rows), (adapters, 2 * hp, rank)]
    grad_out_up, grad_out_down, grad_in_down, grad_in_up = call(
        selecting(collect_kernel), [(s, f32) for s in shapes], [full(*sent.shape)],
        [full(*s) for s in shapes], [pltpu.VMEM((dp_size,) + sent.shape[2:], f32)], mega, mega, 1,
    )(picks, arrived)

    grad_out_down = grad_out_down.reshape(out_down.shape)
    grad_in_down = grad_in_down.transpose(0, 2, 1)
    grad_in_up = grad_in_up.reshape(adapters, 2, part, p_part, rank).transpose(0, 4, 1, 2, 3)
    return (mixed[None], tokens_grad[None], grad_in_down, grad_in_up, grad_out_down, grad_out_up)


def solution(mesh):
    placed = (
        P("dp", "tensor", None),
        P("dp", "tensor", None),
        P("dp", None),
        P("dp"),
        P(),
        P("dp", None, "tensor"),
        P("dp", None),
        P("dp", "tensor"),
        P(None, "tensor"),
        P(),
        P("tensor"),
        P(),
        P("tensor"),
        P("tensor"),
        P("tensor"),
        P("tensor"),
        P("tensor", "dp"),
        P(None, "dp", None),
        P(None, None, None, "tensor", "dp"),
        P(None, "tensor", "dp", None),
        P(None, None, "dp"),
    )
    return jax.shard_map(
        shards,
        mesh=mesh,
        in_specs=placed,
        out_specs=(
            P("dp", "tensor", None),
            P("dp", "tensor", None),
            P(None, "dp", None),
            P(None, None, None, "tensor", "dp"),
            P(None, "tensor", "dp", None),
            P(None, None, "dp"),
        ),
        check_vma=False,
    )
```

```python
import math

import jax
import jax.numpy as jnp
import numpy as np
from jax import lax
from jax.experimental import pallas as pl
from jax.experimental.pallas import tpu as pltpu
from jax.sharding import PartitionSpec as P

epsilon = 1e-05
chunk = 128
lanes = 128
doc_most = 800
edge = 16
f32, bf16 = jnp.float32, jnp.bfloat16
exact = lax.Precision.HIGHEST
vmem_bytes = 48 * 1024 * 1024


def dot(a, b):
    return jnp.dot(a, b, preferred_element_type=f32)


def dot_nt(a, b):
    return lax.dot_general(a, b, (((1,), (1,)), ((), ())), preferred_element_type=f32)


def dot_tn(a, b):
    return lax.dot_general(a, b, (((0,), (0,)), ((), ())), preferred_element_type=f32)


def halves(x):
    high = x.astype(bf16)
    return high, (x - high.astype(f32)).astype(bf16)


def pieces(x, count):
    out = []
    for _ in range(count):
        part = lax.reduce_precision(x, 8, 7)
        out.append(part.astype(bf16))
        x = x - part
    return jnp.concatenate(out, axis=-1)


def dot2(x, w):
    high, low = halves(x)
    return dot(high, w) + dot(low, w)


def dot2_nt(x, w):
    high, low = halves(x)
    return dot_nt(high, w) + dot_nt(low, w)


def dot2_tn(x, w):
    high, low = halves(x)
    return dot_tn(high, w) + dot_tn(low, w)


def tile_lanes(m, width):
    return m if width == lanes else jnp.concatenate([m] * (width // lanes), axis=1)


def sigmoid(u):
    return 0.5 + 0.5 * jnp.tanh(0.5 * u)


def silu(u):
    return u * sigmoid(u)


def silu_parts(u):
    s = sigmoid(u)
    v = u * s
    return v, s + v * (1.0 - s)


korder = (0, 2, 4, 6, 1, 3, 5, 7)


def weight_pieces(refs, at=0):
    if len(refs) == 1:
        return [(refs[0][...].reshape(-1, refs[0].shape[-1]), None)]
    pairs = ((0, 1), (2, 3), (4, 5), (6, 7)) if at == 0 else ((0, 2), (1, 3), (4, 6), (5, 7))
    return [
        (ref[...].reshape(2 * lanes, ref.shape[-1]), pair) for ref, pair in zip(refs[4 * at : 4 * at + 4], pairs)
    ]


def block_at(n):
    return slice(n * lanes, (n + 1) * lanes)


def with_weight(refs, body, half):
    if len(refs) == 1:
        body(weight_pieces(refs))
        return
    if isinstance(half, int):
        body(weight_pieces(refs * 2, half))
        return

    @pl.when(half == 0)
    def _():
        body(weight_pieces(refs, 0))

    @pl.when(half == 1)
    def _():
        body(weight_pieces(refs, 1))


def times(left, parts):
    total = None
    for w, pair in parts:
        if pair is None:
            value = left(slice(None))
        elif pair[1] == pair[0] + 1:
            value = left(slice(pair[0] * lanes, (pair[1] + 1) * lanes))
        else:
            value = jnp.concatenate([left(block_at(n)) for n in pair], axis=1)
        term = dot(value, w)
        total = term if total is None else total + term
    return total


def add_times_transposed(acc, low, parts):
    for w, pair in parts:
        term = dot_nt(low, w)
        if pair is None:
            acc[...] += term
        elif pair[1] == pair[0] + 1:
            acc[:, pair[0] * lanes : (pair[1] + 1) * lanes] += term
        else:
            for i, n in enumerate(pair):
                acc[:, block_at(n)] += term[:, block_at(i)]


def rows_of(c):
    return slice(c * chunk, (c + 1) * chunk)


def sums3(tri, x):
    high, mid = halves(x)
    low = (x - high.astype(f32) - mid.astype(f32)).astype(bf16)
    return dot(tri, high) + dot(tri, mid) + dot(tri, low)


def parts_of(x, count):
    out = []
    for _ in range(count):
        part = x.astype(bf16)
        out.append(part)
        x = x - part.astype(f32)
    return jnp.concatenate(out, axis=1)


def table_of(x, count):
    parts = parts_of(x, count)
    return jnp.concatenate([parts, jnp.zeros((x.shape[0], lanes - parts.shape[1]), bf16)], axis=1)


def column(row):
    return jnp.broadcast_to(row, (lanes, lanes)).T


def prep_kernel(sel, tokens, halo, norm_gain, small, picked, dt_t, inner_t, place, params, params_bc, segs, ex, no_out,
                normed, ranks, ranks_own, tables, bc_out, bct_out, scores, rows_out, cums_t, keep, ups, wides, w_bc,
                masks, ext, *, rank, state, moved_blocks):
    own, width = tokens.shape
    blocks = own // chunk
    tp, _, group = params.shape
    heads = dt_t.shape[0]
    part = heads // tp
    turn, pick, bound, small_at = 8 + tp, sel[8 + 2 * tp], 9 + 2 * tp, 9 + 2 * tp + 2 * blocks

    for c in range(blocks):
        wide = tokens[rows_of(c), :].astype(f32)
        scale = lax.rsqrt(jnp.sum(wide * wide, axis=1, keepdims=True) / width + epsilon)
        ext[edge + c * chunk : edge + (c + 1) * chunk, :] = (wide * scale * norm_gain[...]).astype(bf16)
    ext[:edge, :] = halo[...]
    for j in range(8):
        k = korder[j]
        at = pl.ds(pl.multiple_of(sel[k] * lanes, lanes), lanes)
        cols = slice(j * lanes, (j + 1) * lanes)
        no_out[:, cols] = ext[:, at]
        at = sel[small_at + j]
        wides[:, cols] = picked[at]
        w_bc[j * lanes : (j + 1) * lanes, :state] = small[at, :lanes, :]
        w_bc[j * lanes : (j + 1) * lanes, state:] = small[at, lanes : 2 * lanes, :]
    normed[...] = ext[edge:, :]
    ranks[...] = parts_of(dot_nt(ext[...], wides[:rank, :]), 2)
    ranks_own[...] = ranks[edge:, :]
    bc = dot(ext[...], w_bc[...])

    hp = place.shape[1]
    for s in range(tp):
        cols = slice(s * group, (s + 1) * group)
        z = x = d = None
        for k in range(inner_t.shape[1]):
            where = place[sel[korder[k]]] if moved_blocks else place[k]
            piece = inner_t[sel[turn + s], k]
            terms = (dot(piece[:rank, :hp], where), dot(piece[:rank, hp : 2 * hp], where),
                     dot(piece[rank:, :hp], where))
            z, x, d = terms if z is None else (z + terms[0], x + terms[1], d + terms[2])
        z, x = z.astype(bf16), x.astype(bf16)
        ups[:, cols] = jnp.concatenate([z, z, x, x, d.astype(bf16)], axis=0)

    i = lax.broadcasted_iota(jnp.int32, (chunk, chunk), 0)
    j = lax.broadcasted_iota(jnp.int32, (chunk, chunk), 1)
    tril = jnp.where(j <= i, 1.0, 0.0)
    segs_at = []
    for c in range(blocks):
        rows = rows_of(c)
        seg = column(segs[3, c : c + 1, :])
        segs_at.append(seg[:, :heads])
        for k in range(1, 4):
            masks[k - 1, rows, :] = jnp.where(column(segs[3 - k, c : c + 1, :]) == seg, 1.0, 0.0)
            masks[k + 2, rows, :] = jnp.where(column(segs[3 + k, c : c + 1, :]) == seg, 1.0, 0.0)
        cur = bc[edge + c * chunk - 8 : edge + (c + 1) * chunk]
        total = params_bc[3:4, :] * cur[8:] + params_bc[4:5, :]
        for k in range(1, 4):
            shifted = pltpu.roll(cur, k, 0)[8:]
            total = total + params_bc[3 - k : 4 - k, :] * (
                shifted * tile_lanes(masks[k - 1, rows, :], 2 * state)
            )
        rows_out[rows, : 2 * state] = total
        value = silu(total)
        inb, inc = value[:, :state], value[:, state:]
        bc_out[rows, :] = value.astype(bf16)
        bct_out[:state, rows] = inb.T.astype(bf16)
        bct_out[state:, rows] = inc.T.astype(bf16)
        okay = jnp.where(seg == segs[3, c : c + 1, :], tril, 0.0)
        scores[1, c] = okay
        scores[0, c] = dot_nt(inc.astype(bf16), inb.astype(bf16)) * okay

    bias = jnp.concatenate([params[sel[turn + s], 7:8, :part] for s in range(tp)], axis=1)
    a_log = jnp.concatenate([params[sel[turn + s], 7:8, part : 2 * part] for s in range(tp)], axis=1)
    decays = -jnp.exp(a_log)
    raw = dot_nt(ext[edge:, :], dt_t[...]) + bias
    dt = jnp.maximum(raw, 0.0) + jnp.log1p(jnp.exp(-jnp.abs(raw)))
    rows_out[:, 2 * state :] = jnp.concatenate([sigmoid(raw), jnp.zeros((own, lanes - heads), f32)], axis=1)
    tables[:, :lanes] = table_of(dt, 2)
    logs = dt * decays * math.log2(math.e)
    bounds = [sel[bound + n].astype(f32) for n in range(2 * blocks)]
    before_seg, last_seg = bounds[0], bounds[-1]
    prior = jnp.zeros((1, heads), f32)
    all_cums, keeps = [], []
    tri = tril.astype(bf16)
    for c in range(blocks):
        rows = rows_of(c)
        before_c, last_c = bounds[2 * c], bounds[2 * c + 1]
        cums = sums3(tri, logs[rows])
        end = cums[chunk - 1 : chunk]
        seg = segs_at[c]
        tables[rows, 5 * lanes :] = table_of(cums, 3)
        flipped = jnp.concatenate([cums, jnp.zeros((chunk, lanes - heads), f32)], axis=1).T
        for s in range(tp):
            cums_t[s, c] = flipped[s * part : (s + 1) * part]
        tables[rows, 2 * lanes : 3 * lanes] = table_of(jnp.where(seg == before_c, jnp.exp2(cums), 0.0), 2)
        tables[rows, 3 * lanes : 4 * lanes] = table_of(jnp.where(seg == last_c, jnp.exp2(end - cums), 0.0), 2)
        keeps.append(jnp.where(before_c == last_c, jnp.exp2(end), 0.0))
        all_cums.append(cums + prior)
        prior = prior + end
    for c in range(blocks):
        rows = rows_of(c)
        seg = segs_at[c]
        tables[rows, 4 * lanes : 5 * lanes] = table_of(jnp.where(seg == before_seg, jnp.exp2(all_cums[c]), 0.0), 2)
        tables[rows, lanes : 2 * lanes] = table_of(jnp.where(seg == last_seg, jnp.exp2(prior - all_cums[c]), 0.0), 2)
    whole = jnp.where(before_seg == last_seg, jnp.exp2(prior), 0.0)
    table = jnp.concatenate(keeps + [jnp.zeros((7 - blocks, heads), f32), whole], axis=0)
    high, mid = halves(table)
    low = (table - high.astype(f32) - mid.astype(f32)).astype(bf16)
    spread = ex[:heads, :]
    keep[...] = dot(high, spread) + dot(mid, spread) + dot(low, spread)
    keep[6:7, :lanes] = jnp.concatenate([decays, jnp.zeros((1, lanes - heads), f32)], axis=1)


def pack_kernel(bc, dt_weight, in_down, out_up, in_up, out_down, pick, out):
    rows, two = bc.shape
    part = dt_weight.shape[0]
    count, rank, _ = in_down.shape
    at = 2 * rows
    out[:rows, :] = bc[:, : two // 2]
    out[rows:at, :] = bc[:, two // 2 :]
    for b in range(count):
        out[at + 2 * rank * b : at + 2 * rank * b + rank, :] = in_down[b]
        out[at + 2 * rank * b + rank : at + 2 * rank * (b + 1), :] = out_up[b]
    at += 2 * rank * count
    for b in range(count):
        out[at + 2 * rank * b : at + 2 * rank * b + rank, :] = in_up[b].astype(f32).T.astype(bf16)
        flipped = out_down[b].astype(f32).T
        out[at + 2 * rank * b + rank : at + 2 * rank * (b + 1), :] = jnp.concatenate(
            [flipped, jnp.zeros_like(flipped)], axis=1
        ).astype(bf16)
    at += 2 * rank * count
    wide = jnp.concatenate([dt_weight[...].astype(f32), jnp.zeros((16 - part, rows), f32)], axis=0)
    out[at : at + 16, :] = wide.astype(bf16)
    out[at + 16 : at + 32, :] = jnp.zeros((16, lanes), bf16) + pick[0].astype(f32).astype(bf16)


def proj_kernel(left, *refs, weights):
    refs, ws = refs[weights:], refs[:weights]
    ranks, a_up, params, masks, tables, ex, b_t, u_out, sc_out, f_out, xs, moved = refs

    def body(parts):
        xs[...] = times(lambda at: left[:, at], parts) + dot(ranks[...], a_up[...])

    with_weight(ws, body, pl.program_id(0) // 2)
    own, width = u_out.shape
    step = min(width, 256)
    dt_wide, out_wide = dot(tables[:, :lanes], ex[...]), dot(tables[:, lanes:], ex[...])
    for c in range(own // chunk):
        rows = rows_of(c)
        for n in range(width // step):
            cols = slice(n * step, (n + 1) * step)
            cur = xs[edge + c * chunk - 8 : edge + (c + 1) * chunk, cols]
            total = params[0, 3:4, cols] * cur[8:] + params[0, 4:5, cols]
            for k in range(1, 4):
                shifted = pltpu.roll(cur, k, 0)[8:]
                total = total + params[0, 3 - k : 4 - k, cols] * (
                    shifted * tile_lanes(masks[k - 1, rows, :], step)
                )
            u_out[rows, cols] = total
            value = silu(total)
            scaled = (dt_wide[rows, cols] * value).astype(bf16)
            sc_out[rows, cols] = scaled
            moved[rows, cols] = (out_wide[rows, cols] * scaled.astype(f32)).astype(bf16)
    f_out[...] = dot(b_t[...], moved[...]).astype(bf16)

def pair_parts(lcol, cums_t, p):
    lc = lcol[:, p * 2 * lanes : (p + 1) * 2 * lanes]
    lr = jnp.concatenate([cums_t[2 * p : 2 * p + 1, :], cums_t[2 * p + 1 : 2 * p + 2, :]], axis=1)
    return jnp.exp2(jnp.minimum(lc - lr, 0.0))


def two_heads(v, head_size):
    lane = lax.broadcasted_iota(jnp.int32, v.shape, 1)
    zero = jnp.zeros_like(v)
    return jnp.concatenate([jnp.where(lane < head_size, v, zero), jnp.where(lane < head_size, zero, v)], 0)


def within_kernel(sc, cums3, cums_t, scores, exl, y_out):
    own, width = y_out.shape
    wide = dot(cums3[...], exl[...])
    for c in range(own // chunk):
        rows = rows_of(c)
        lcol = wide[rows]
        allowed = tile_lanes(scores[0, c], 2 * lanes)
        for p in range(width // lanes):
            e = pair_parts(lcol, cums_t[0, c], p)
            m = (e * allowed).astype(bf16)
            cols = slice(p * lanes, (p + 1) * lanes)
            y_out[rows, cols] = dot(m, two_heads(sc[rows, cols], lanes // 2))


def row_scale_of(sumsq, inner):
    return lax.rsqrt(jnp.sum(sumsq, axis=1, keepdims=True) / inner + epsilon)


def put_width_parts(sent, value):
    rank = value.shape[0]
    dp, tp, _, _ = sent.shape
    size = value.shape[1] // dp
    for d in range(dp):
        piece = value[:, d * size : (d + 1) * size].astype(bf16)
        for t in range(tp):
            sent[d, t, :rank, :size] = piece


def put_inner_parts(sent, to, value, order, offset):
    rank = value.shape[0]
    dp = sent.shape[0]
    hp = value.shape[1] // dp
    moved = dot(value.astype(bf16), order[...]).astype(bf16)
    for d in range(dp):
        sent[d, to, rank : 2 * rank, offset : offset + hp] = moved[:, d * hp : (d + 1) * hp]


def middle_kernel(sel, left, *refs, weights, hops, inner):
    zs, outs, refs = refs[:weights], refs[weights : 2 * weights], refs[2 * weights :]
    s_ins, refs = refs[:hops], refs[hops:]
    (ranks, a_up, params, yw, u, sc, tables, own_in, keep, ex, b_t, c_t, in_c, cot, tokens, b_up, b_down, order, red,
     states, mixed, sent, gh_out, lz_out, g_out, ahead,
     ys, heads, gate_z, gated, gg, sumsq, dots, acc, cots, g_rank, rank, low) = refs
    phase, g = pl.program_id(0), pl.program_id(1)
    last = pl.num_programs(1) - 1
    half = g // 2
    own, width = gh_out.shape
    step = min(width, 256)
    blocks = own // chunk

    @pl.when((phase == 0) & (g == 0))
    def _():
        ahead[...] = jnp.zeros_like(ahead)
        sumsq[...] = jnp.zeros_like(sumsq)
        acc[...] = jnp.zeros_like(acc)
        rank[...] = jnp.zeros_like(rank)
        dots[...] = jnp.zeros_like(dots)
        sent[...] = jnp.zeros_like(sent)
        for j in range(8):
            at = pl.ds(pl.multiple_of(sel[korder[j]] * lanes, lanes), lanes)
            cots[:, j * lanes : (j + 1) * lanes] = cot[:, at]
        g_rank[...] = parts_of(dot_nt(cot[...], b_up[...]), 2)

    @pl.when(phase == 0)
    def _():
        def body(parts):
            first = left.shape[0] - own
            gate_z[g] = times(lambda at: left[first:, at], parts) + dot(ranks[...], a_up[...])

        with_weight(zs, body, half)
        in_wide, out_wide = dot(tables[:, :lanes], ex[...]), dot(tables[:, lanes:], ex[...])
        for n in range(width // step):
            cols = slice(n * step, (n + 1) * step)
            new = []
            for c in range(blocks):
                rows = rows_of(c)
                moved = (out_wide[rows, cols] * sc[rows, cols].astype(f32)).astype(bf16)
                new.append(dot(b_t[:, rows], moved))
            s = sum(r[:, cols].astype(f32) for r in s_ins)
            for c in range(blocks):
                states[c, :, cols] = s.astype(bf16)
                s = s * keep[c : c + 1, cols] + new[c]
            for c in range(blocks):
                rows = rows_of(c)
                y = yw[rows, cols] + in_wide[rows, cols] * dot(in_c[rows, :], states[c, :, cols])
                ys[g, rows, cols] = y
                head = y + params[0, 6:7, cols] * silu(u[rows, cols])
                heads[g, rows, cols] = head
                gd = head * silu(gate_z[g, rows, cols])
                gated[g, rows, cols] = gd
                sq = gd * gd
                total = sumsq[rows, :]
                for i in range(step // lanes):
                    total = total + sq[:, i * lanes : (i + 1) * lanes]
                sumsq[rows, :] = total

    @pl.when(phase == 1)
    def _():
        scale = row_scale_of(sumsq[...], inner)
        normed_inner = gated[g] * scale * params[0, 5:6, :]
        high, rest = halves(normed_inner)
        low[...] = high
        rank[...] += dot_nt(high, b_down[...]) + dot_nt(rest, b_down[...])
        size = rank.shape[1]
        both = dot_tn(g_rank[...], high)
        put_inner_parts(sent, sel[8 + g], both[:size] + both[size:], order, 0)

        def body(parts):
            twice = jnp.concatenate([b_down[...], b_down[...]], axis=0)
            value = (times(lambda at: cots[:, at], parts) + dot(g_rank[...], twice)) * params[0, 5:6, :]
            gg[g] = value
            prod = value * gated[g]
            total = dots[...]
            for i in range(width // lanes):
                total = total + prod[:, i * lanes : (i + 1) * lanes]
            dots[...] = total
            add_times_transposed(acc, low[...], parts)

        with_weight(outs, body, half)

    @pl.when((phase == 1) & (g == last))
    def _():
        put_width_parts(sent, dot2_tn(rank[...], cot[...]))
        mixed[...] = tokens[...].astype(f32) + dot2(rank[...], b_up[...])
        for j in range(8):
            at = pl.ds(pl.multiple_of(sel[korder[j]] * lanes, lanes), lanes)
            mixed[:, at] += acc[:, j * lanes : (j + 1) * lanes]

    @pl.when(phase == 2)
    def _():
        scale = row_scale_of(sumsq[...], inner)
        coef = scale * scale * scale * (jnp.sum(dots[...], axis=1, keepdims=True) / inner)
        own_wide = dot(own_in[...], ex[...])
        for c in range(blocks):
            rows = rows_of(c)
            sc_rows, co_rows = scale[rows], coef[rows]
            for n in range(width // step):
                cols = slice(n * step, (n + 1) * step)
                g_gated = gg[g, rows, cols] * sc_rows - gated[g, rows, cols] * co_rows
                gate, slope = silu_parts(gate_z[g, rows, cols])
                lz_out[rows, cols] = (g_gated * heads[g, rows, cols] * slope).astype(bf16)
                gh = g_gated * gate
                gh_out[rows, cols] = gh
                low[rows, cols] = (own_wide[rows, cols] * gh).astype(bf16)
                ys[g, rows, cols] = ys[g, rows, cols] * gh
        ahead[...] += dot2(ys[g], red[...])
        g_out[...] = dot(c_t[...], low[...]).astype(bf16)


def back_within_kernel(gh, ahead_in, sc, cums3, cums_t, scores, exl, red, dv_out, ds_out, ahead, prod):
    g = pl.program_id(0)

    @pl.when(g == 0)
    def _():
        ds_out[...] = jnp.zeros_like(ds_out)
        ahead[...] = ahead_in[...]

    own, width = dv_out.shape
    wide = dot(cums3[...], exl[...])
    for c in range(own // chunk):
        rows = rows_of(c)
        lcol = wide[rows]
        allowed = tile_lanes(scores[0, c], 2 * lanes)
        ds = jnp.zeros((chunk, lanes), f32)
        for p in range(width // lanes):
            cols = slice(p * lanes, (p + 1) * lanes)
            e = pair_parts(lcol, cums_t[0, c], p)
            m = (e * allowed).astype(bf16)
            v = sc[rows, cols]
            dy = gh[rows, cols]
            high, low = halves(dy)
            both = two_heads(v, lanes // 2)
            parts = jnp.concatenate([high, low], axis=1)
            dm = dot_nt(parts, jnp.concatenate([both, both], axis=1))
            eds = e * dm
            ds = ds + eds[:, :lanes] + eds[:, lanes:]
            dvb = dot_tn(m, high) + dot_tn(m, low)
            lane = lax.broadcasted_iota(jnp.int32, (chunk, lanes), 1)
            dv = jnp.where(lane < lanes // 2, dvb[:chunk], dvb[chunk:])
            dv_out[rows, cols] = dv
            prod[rows, cols] = v.astype(f32) * dv
        ds_out[c] += ds
    ahead[...] -= dot2(prod[...], red[...])


def conv_back(cur, params, masks, rows, width):
    total = params[3:4, :] * cur[:chunk]
    for k in range(1, 4):
        shifted = pltpu.roll(cur, cur.shape[0] - k, 0)[:chunk]
        total = total + params[3 - k : 4 - k, :] * (shifted * tile_lanes(masks[k - 1, rows, :], width))
    return total


def back_state_kernel(*refs, hops):
    grads_in, refs = refs[:hops], refs[hops:]
    (states, gh, sc, dv, u, params, bc, c_t, tables, keep, decays, ex, red, ds, ahead, allowed, rows_in, masks, lx_out, gbc_out,
     ldt_out, edges, tail, db, dc, behind, direct, carry, prods, carries) = refs
    state = c_t.shape[0]
    g = pl.program_id(0)

    @pl.when(g == 0)
    def _():
        for ref in (db, dc, behind, direct, carry, carries):
            ref[...] = jnp.zeros_like(ref)

    own, width = lx_out.shape
    step = min(width, 256)
    blocks = own // chunk
    dt_wide, in_wide = dot(tables[:, :lanes], ex[...]), dot(tables[:, 2 * lanes : 3 * lanes], ex[...])
    out_wide = dot(tables[:, 3 * lanes :], ex[...])
    for n in range(width // step):
        cols = slice(n * step, (n + 1) * step)
        gs = sum(r[:, cols].astype(f32) for r in grads_in)
        following = jnp.zeros((8, step), f32)
        for c in reversed(range(blocks)):
            rows = rows_of(c)
            low_g = gs.astype(bf16)
            kept = keep[c : c + 1, cols]
            low_s = states[c, :, cols]
            scaled = sc[rows, cols].astype(f32)
            eo = out_wide[rows, cols]
            dvs = eo * dot(bc[rows, :state], low_g)
            db[rows, :] += dot_nt((eo * scaled).astype(bf16), low_g)
            dy = gh[rows, cols]
            moved = (in_wide[rows, cols] * dy).astype(bf16)
            dc[rows, :] += dot_nt(moved, low_s)
            carried = jnp.sum(low_s.astype(f32) * gs, axis=0, keepdims=True) * kept
            carries[c : c + 1, cols] = carried
            gs = gs * kept + dot(c_t[:, rows], moved)
            g_sc = dv[rows, cols] + dvs
            v, slope = silu_parts(u[rows, cols])
            prods[0, rows, cols] = (scaled * dvs).astype(bf16)
            prods[1, rows, cols] = (v * g_sc).astype(bf16)
            g_v = dt_wide[rows, cols] * g_sc + params[0, 6:7, cols] * dy
            g_u = g_v * slope
            g_x = conv_back(jnp.concatenate([g_u, following], axis=0), params[0, :, cols], masks, rows, step)
            lx_out[rows, cols] = g_x.astype(bf16)
            following = g_u[:8]
            if c == blocks - 1:
                tail[:, cols] = g_x[-edge:]
            if c == 0:
                at = pl.ds(pl.multiple_of(g * width + n * step, lanes), step)
                edges[:, at] = g_u[:edge].astype(bf16)
    behind[...] += dot(prods[0], red[...])
    direct[...] += dot(prods[1], red[...])
    carry[...] += dot2(carries[...], red[...])

    @pl.when(g == pl.num_programs(0) - 1)
    def _():
        i = lax.broadcasted_iota(jnp.int32, (chunk, chunk), 0)
        j = lax.broadcasted_iota(jnp.int32, (chunk, chunk), 1)
        at_most = jnp.where(i <= j, 1.0, 0.0).astype(bf16)
        below = jnp.where(j < i, 1.0, 0.0).astype(bf16)
        decay_row = decays[6:7, :]
        for c in range(blocks):
            rows = rows_of(c)

            g_logs = sums3(at_most, ahead[rows, :]) + sums3(below, behind[rows, :]) + carry[c : c + 1, :]
            heads = ldt_out.shape[1]
            g_dt = (direct[rows, :] + g_logs * decay_row) * rows_in[rows, 2 * state :]
            ldt_out[rows, :] = g_dt[:, :heads].astype(bf16)
            g_scores = ds[c] * allowed[0, c]
            low_ds = g_scores.astype(bf16)
            gc = dc[rows, :] + dot(low_ds, bc[rows, :state])
            gb = db[rows, :] + dot_tn(low_ds, bc[rows, state:])
            g_bc = jnp.concatenate([gb, gc], axis=1)
            _, slope = silu_parts(rows_in[rows, : 2 * state])
            gbc_out[rows, :] = g_bc * slope
            if c == 0:
                edges[:, edges.shape[1] - g_bc.shape[1] :] = (g_bc * slope)[:edge].astype(bf16)


def in_z_kernel(lz, *refs, weights):
    ws, refs = refs[:weights], refs[weights:]
    a_up, ranks, acc, g_rank, p_up = refs

    @pl.when(pl.program_id(0) == 0)
    def _():
        acc[...] = jnp.zeros_like(acc)
        g_rank[...] = jnp.zeros_like(g_rank)

    size = g_rank.shape[1]
    g_rank[...] += dot_nt(lz[...], a_up[...])
    both = dot_tn(ranks[...], lz[...])
    p_up[0] = both[:size] + both[size:]
    with_weight(ws, lambda parts: add_times_transposed(acc, lz[...], parts), pl.program_id(0) // 2)


def in_x_kernel(sel, lx, tail, halo, a_up, ranks, params, masks, g_rank_z, p_up_z, order, normed,
                fixed, g_rank, sent, low):
    g = pl.program_id(0)

    @pl.when(g == 0)
    def _():
        g_rank[...] = g_rank_z[...]
        sent[...] = jnp.zeros_like(sent)

    own, width = low.shape
    beyond = jnp.concatenate([jnp.zeros((edge, width), f32), halo[...].astype(f32)[:8]], axis=0)
    total = tail[...]
    for k in range(1, 4):
        shifted = pltpu.roll(beyond, beyond.shape[0] - k, 0)[:edge]
        total = total + params[0, 3 - k : 4 - k, :] * (
            shifted * tile_lanes(masks[k - 1, own - edge :, :], width)
        )
    fixed[...] = total.astype(bf16)
    low[: own - edge, :] = lx[: own - edge, :]
    low[own - edge :, :] = total.astype(bf16)
    size = g_rank.shape[1]
    g_rank[...] += dot_nt(low[...], a_up[...])
    both = dot_tn(ranks[...], low[...])
    to = sel[8 + g]
    put_inner_parts(sent, to, p_up_z[0], order, 0)
    put_inner_parts(sent, to, both[:size] + both[size:], order, width // sent.shape[0])

    @pl.when(g == pl.num_programs(0) - 1)
    def _():
        put_width_parts(sent, dot2_tn(g_rank[...], normed[...]))


def tokens_kernel(sel, lx, *refs, weights):
    ws, refs = refs[:weights], refs[weights:]
    (acc_z, g_rank, gbc, halo_bc, params_bc, w_bc, ldt, dt_t, ad, masks, tokens, cot, norm_gain, grad, acc, lbc,
     g_norm) = refs
    g = pl.program_id(0)

    @pl.when(g == 0)
    def _():
        acc[...] = acc_z[...]

    with_weight(ws, lambda parts: add_times_transposed(acc, lx[...], parts), pl.program_id(0) // 2)

    @pl.when(g == pl.num_programs(0) - 1)
    def _():
        own, width = grad.shape
        blocks = own // chunk
        for c in range(blocks):
            rows = rows_of(c)
            if c < blocks - 1:
                cur = gbc[c * chunk : (c + 1) * chunk + 8, :]
            else:
                cur = jnp.concatenate([gbc[rows, :], halo_bc[...].astype(f32)[:8]], axis=0)
            lbc[rows, :] = conv_back(cur, params_bc[...], masks, rows, gbc.shape[1]).astype(bf16)
        g_norm[...] = (
            dot_nt(lbc[...], w_bc[...]) + dot(ldt[...], dt_t[...])
            + dot(parts_of(g_rank[...], 2), jnp.concatenate([ad[...], ad[...]], axis=0))
        )
        for j in range(8):
            at = pl.ds(pl.multiple_of(sel[korder[j]] * lanes, lanes), lanes)
            g_norm[:, at] += acc[:, j * lanes : (j + 1) * lanes]
        for c in range(blocks):
            rows = rows_of(c)
            wide = tokens[rows, :].astype(f32)
            scale = lax.rsqrt(jnp.sum(wide * wide, axis=1, keepdims=True) / width + epsilon)
            gn = g_norm[rows, :] * norm_gain[...]
            row_dot = jnp.sum(gn * wide, axis=1, keepdims=True)
            grad[rows, :] = (
                cot[rows, :].astype(f32) + gn * scale - wide * (scale * scale * scale * row_dot / width)
            )


def collect_kernel(picks, arrived, up_out, down_out, down_in, up_in, sums):
    dp, tp, rows, _ = arrived.shape
    rank = rows // 4
    for d in range(dp):
        one = arrived[d, 0].astype(f32)
        for t in range(1, tp):
            one = one + arrived[d, t].astype(f32)
        sums[d] = one
    for b in range(up_out.shape[0]):
        total = jnp.zeros(arrived.shape[2:], f32)
        for d in range(dp):
            total = total + jnp.where(picks[d] == b, sums[d], 0.0)
        up_out[b] = total[:rank, : up_out.shape[2]]
        down_out[b] = total[rank : 2 * rank].T[: down_out.shape[1]]
        down_in[b] = total[2 * rank : 3 * rank, : down_in.shape[2]]
        up_in[b] = total[3 * rank :].T[: up_in.shape[1]]


def up(x):
    n = lax.axis_size("tensor")
    return lax.ppermute(x, "tensor", [(i, i + 1) for i in range(n - 1)])


def down(x):
    n = lax.axis_size("tensor")
    return lax.ppermute(x, "tensor", [(i + 1, i) for i in range(n - 1)])


def around_tensor(x):
    n = lax.axis_size("tensor")
    return [x] + [lax.ppermute(x, "tensor", [(i, (i + s) % n) for i in range(n)]) for s in range(1, n)]


def swap(x, bit):
    n = lax.axis_size("dp")
    return lax.ppermute(x, "dp", [(i, i ^ (1 << bit)) for i in range(n)])


def all_dp(x):
    count = lax.axis_size("dp").bit_length() - 1
    cur = x.reshape((1,) * count + x.shape)
    for bit in list(range(1, count)) + [0]:
        cur = jnp.concatenate([cur, swap(cur, bit)], axis=count - 1 - bit)
    return cur.reshape((-1,) + x.shape)


def joined_with(x, axis, bit):
    n = lax.axis_size(axis)
    return jnp.concatenate([x, lax.ppermute(x, axis, [(i, i ^ (1 << bit)) for i in range(n)])])


def after(x, *events):
    return lax.optimization_barrier((x, events))[0]


def spread_dp(rotated, events):
    out = []
    curs = [after(jnp.stack(rotated[2 * j : 2 * j + 2]), *events) for j in range(2)]
    firsts = [swap(cur, 1 + j) for j, cur in enumerate(curs)]
    pairs = [jnp.stack([cur, first]) for cur, first in zip(curs, firsts)]
    fars = [swap(pair, 2 - j) for j, pair in enumerate(pairs)]
    for pair, far in zip(pairs, fars):
        out += [pair, far, swap(pair, 0), swap(far, 0)]
    return out, firsts


def gather_plain(x):
    n, tp = lax.axis_size("dp"), lax.axis_size("tensor")
    whole = lax.all_gather(x, ("dp", "tensor")).reshape((n, tp) + x.shape)
    return [whole.transpose(1, 0, 2, 3).reshape(tp, n * x.shape[0], x.shape[1])]


def pad_lanes(x):
    return jnp.pad(x, ((0, 0), (0, lanes - x.shape[1])))


def shards(
    tokens,
    cotangent,
    doc_ids,
    adapter_pick,
    norm_gain,
    gate_x_weight,
    bc_weight,
    dt_weight,
    conv_x_weight,
    conv_bc_weight,
    conv_x_bias,
    conv_bc_bias,
    dt_bias,
    a_log,
    skip_gain,
    inner_gain,
    out_weight,
    in_down,
    in_up,
    out_down,
    out_up,
):
    dp_size, tp_size = lax.axis_size("dp"), lax.axis_size("tensor")
    both = ("dp", "tensor")
    seq_count, own, width = tokens.shape
    assert seq_count == 1 and width == 8 * lanes
    group = gate_x_weight.shape[2]
    inner = group * tp_size
    part = dt_weight.shape[1]
    heads = part * tp_size
    head_size = inner // heads
    assert head_size * 2 == lanes
    state = bc_weight.shape[1] // 2
    rank = in_down.shape[2]
    adapters = in_down.shape[0]
    hops = min(1 + (doc_most - 2) // own, tp_size - 1)
    blocks = own // chunk
    d_rows = gate_x_weight.shape[0]
    p_part = in_up.shape[4]
    hp = part * p_part
    mine, place_at = lax.axis_index("dp"), lax.axis_index("tensor")
    by_exchange = dp_size == 8 and tp_size == 4 and d_rows == lanes
    cot, tok = cotangent[0], tokens[0]

    local_x, local_z, local_out = gate_x_weight[:, 1], gate_x_weight[:, 0], out_weight.T
    if by_exchange:
        ring_x = around_tensor(local_x)

    cuts = [d_rows, d_rows, adapters * 2 * rank, adapters * 2 * rank, 16, 16]
    starts = [sum(cuts[:n]) for n in range(len(cuts))]
    if by_exchange:
        small_in = [
            bc_weight, dt_weight.T, in_down.transpose(0, 2, 1), out_up,
            in_up.transpose(0, 2, 3, 4, 1).reshape(adapters, 2 * hp, rank), out_down.reshape(adapters, hp, rank),
        ]
        vmem = pl.BlockSpec(memory_space=pltpu.VMEM)
        small = pl.pallas_call(
            pack_kernel,
            name="pack_kernel",
            out_shape=jax.ShapeDtypeStruct((sum(cuts), lanes), bf16),
            in_specs=[vmem] * 6 + [pl.BlockSpec(memory_space=pltpu.SMEM)],
            out_specs=vmem,
        )(*small_in, adapter_pick)
    else:
        small = [
            bc_weight[:, :state],
            bc_weight[:, state:],
            jnp.concatenate([in_down.transpose(0, 2, 1), out_up], axis=1).reshape(-1, d_rows),
            jnp.concatenate(
                [in_up.reshape(adapters, rank, 2 * hp),
                 jnp.pad(out_down.reshape(adapters, hp, rank).transpose(0, 2, 1), ((0, 0), (0, 0), (0, hp)))],
                axis=1,
            ).reshape(-1, 2 * hp),
            jnp.pad(dt_weight.T, ((0, 16 - part), (0, 0))),
            jnp.broadcast_to(adapter_pick.astype(bf16)[:, None], (16, lanes)),
        ]
        small = lax.all_gather(jnp.concatenate([pad_lanes(x) for x in small]), "dp")
    if by_exchange:
        natural = jnp.arange(8) ^ mine
    else:
        natural, small_at = jnp.asarray(np.argsort(korder)), jnp.arange(8)

    last = tok[-edge:].astype(f32)
    last_scale = lax.rsqrt(jnp.mean(last * last, axis=1, keepdims=True) + epsilon)
    halo_in = up((last * last_scale * norm_gain).astype(bf16))

    heads_row = jnp.pad(jnp.concatenate([dt_bias, a_log])[None], ((0, 0), (0, group - 2 * part)))
    params = jnp.concatenate(
        [conv_x_weight, conv_x_bias[None], inner_gain[None], jnp.repeat(skip_gain, head_size)[None], heads_row]
    )

    if by_exchange:
        small = joined_with(joined_with(small[None], "dp", 1), "dp", 2)
        params = jnp.stack(around_tensor(after(params, small)))
        small = jnp.concatenate([small, swap(small, 0)])
        w_x, near_x = spread_dp(ring_x, [])
        ring_z = around_tensor(after(local_z, *ring_x[1:]))
        w_z, near_z = spread_dp(ring_z, near_x)
        small_at = jnp.asarray(np.argsort(korder))[natural]
    else:
        w_x, w_z, w_out = gather_plain(local_x), gather_plain(local_z), gather_plain(local_out)
        params = jnp.stack(around_tensor(params))
    pick = adapter_pick[0]
    taken = [small[:, a : a + c] for a, c in zip(starts, cuts)]
    picks = taken[5][:, 0, 0].astype(jnp.int32)
    inner_t = lax.dynamic_slice_in_dim(taken[3], pick * 2 * rank, 2 * rank, 1)
    dt_own = taken[4][:, :part]
    if by_exchange:
        picks, dt_own = picks[small_at], dt_own[small_at]
    if d_rows != lanes:
        fold = lanes // d_rows

        def rows_first(x):
            return x.reshape(8, fold * d_rows, lanes)

        def lanes_last(x):
            x = x[:, :, :d_rows].reshape(8, fold, x.shape[1], d_rows)
            return x.transpose(0, 2, 1, 3).reshape(8, -1, lanes)

        small = jnp.concatenate([rows_first(taken[0]), rows_first(taken[1]), lanes_last(taken[2])], 1)
        dt_own = lanes_last(dt_own)
    dt_own = dt_own.transpose(1, 0, 2).reshape(part, width)
    inner_rows = inner_t.reshape(-1, lanes)
    dt_rows = dt_own.reshape(-1, lanes)
    ring = jnp.concatenate([inner_rows, dt_rows])
    ring = around_tensor(ring)
    if by_exchange:
        ring_out = around_tensor(after(local_out, *ring[1:], *ring_z[1:]))
        w_out, _ = spread_dp(ring_out, near_z)
    ring = jnp.stack(ring)
    inner_t = ring[:, : inner_rows.shape[0]].reshape(tp_size, dp_size, 2 * rank, lanes)
    dt_t = ring[:, inner_rows.shape[0] :]
    dt_t = dt_t.reshape(heads, width)

    docs = doc_ids[0]
    padded = jnp.concatenate([jnp.full((4,), -1, jnp.int32), docs, jnp.full((4,), -2, jnp.int32)])
    near = lax.dynamic_slice_in_dim(padded, place_at * own, own + 8)
    segs = jnp.stack([near[1 + k : 1 + k + own] for k in range(7)]).astype(f32).reshape(7, blocks, chunk)
    bounds = jnp.stack([near[3 : 3 + own : chunk], near[3 + chunk :: chunk][:blocks]], axis=1).reshape(-1)
    groups = (place_at - jnp.arange(tp_size)) % tp_size
    sel = jnp.concatenate([natural, groups, jnp.arange(tp_size), pick[None], bounds, small_at]).astype(jnp.int32)

    def spread(width_each, copies):
        out = np.zeros((lanes, heads * width_each), np.float32)
        at = np.arange(heads * width_each)
        for n in range(copies):
            out[n * heads + at // width_each, at] = 1.0
        return jnp.asarray(out, bf16)

    ex, exl = spread(head_size, 2), spread(lanes, 3)
    red = jnp.asarray(np.arange(inner)[:, None] // head_size == np.arange(lanes)[None, :], bf16)
    at = np.arange(group)
    place = np.zeros((dp_size, hp, group), np.float32)
    place[at % head_size // p_part, at // head_size * p_part + at % p_part, at] = 1.0
    order = jnp.asarray(place.reshape(group, group).T, bf16)
    place = jnp.asarray(place, bf16)

    def full(*shape):
        return pl.BlockSpec(shape, lambda *s: (0,) * len(shape))

    def cols(rows, size=group, turn=0):
        return pl.BlockSpec((rows, size), lambda g, *s: (0, (g + turn) % tp_size))

    def stacked(*shape, base=0):
        return pl.BlockSpec((1,) + shape, lambda g, *s: (g + base,) + (0,) * len(shape))

    def params_at(base=0):
        return stacked(8, group, base=base)

    def weight_specs(ws, half=None):
        if len(ws) == 1:
            base = (half or 0) * tp_size // 2
            return [pl.BlockSpec((1,) + ws[0].shape[1:], lambda g, s: (s[8 + base + g], 0, 0))]
        shape = (2, 1) + ws[0].shape[2:]
        if half is not None:
            return [pl.BlockSpec(shape, lambda g, *s: (0, g, 0, 0))] * 4
        first = pl.BlockSpec(shape, lambda g, *s: (0, jnp.minimum(g, 1), 0, 0))
        second = pl.BlockSpec(shape, lambda g, *s: (0, jnp.maximum(g - 2, 0), 0, 0))
        return [first] * 4 + [second] * 4

    def call(kernel, out, in_specs, out_specs, scratch, flops, moved, steps=tp_size, grant=vmem_bytes, in_place=None):
        kernel, kernel_takes_sel, name = kernel

        def body(sel_ref, *refs):
            return kernel(sel_ref, *refs) if kernel_takes_sel else kernel(*refs)

        return pl.pallas_call(
            body,
            name=name,
            input_output_aliases={1 + i: to for i, to in (in_place or {}).items()},
            out_shape=[jax.ShapeDtypeStruct(s, d) for s, d in out],
            grid_spec=pltpu.PrefetchScalarGridSpec(
                num_scalar_prefetch=1,
                grid=steps if isinstance(steps, tuple) else (steps,),
                in_specs=in_specs,
                out_specs=out_specs,
                scratch_shapes=scratch,
            ),
            compiler_params=pltpu.CompilerParams(
                dimension_semantics=("arbitrary",) * (len(steps) if isinstance(steps, tuple) else 1),
                vmem_limit_bytes=grant,
            ),
            cost_estimate=pl.CostEstimate(flops=flops, bytes_accessed=moved, transcendentals=0),
        )

    def plain(kernel, **static):
        return (lambda *refs: kernel(*refs, **static)), False, kernel.__name__

    def selecting(kernel, **static):
        return (lambda *refs: kernel(*refs, **static)), True, kernel.__name__

    n_w = len(w_x)
    big = (own, inner)
    ext = own + edge
    mat = 2 * own * width * inner
    mega = 1 << 20
    params_bc = jnp.concatenate([conv_bc_weight, conv_bc_bias[None], jnp.zeros((3, 2 * state), f32)])
    prep_out = [
        ((ext, width), bf16), ((own, width), bf16), ((ext, 2 * rank), bf16), ((own, 2 * rank), bf16),
        ((own, 6 * lanes), bf16), ((own, 2 * state), bf16),
        ((2 * state, own), bf16), ((2, blocks, chunk, chunk), f32), ((own, 2 * state + lanes), f32),
        ((tp_size, blocks, part, chunk), f32), ((8, inner), f32), ((5 * rank, inner), bf16),
        ((2 * rank, width), bf16), ((width, 2 * state), bf16), ((6, own, lanes), f32),
    ]
    at_pick = 8 + 2 * tp_size
    prep_in = [tok, halo_in, norm_gain[None], small, small, dt_t, inner_t, place, params, params_bc, segs, ex]
    prep_specs = [full(*x.shape) for x in prep_in]
    prep_specs[3] = full(8, 2 * lanes, lanes)
    prep_specs[4] = pl.BlockSpec((8, 2 * rank, lanes), lambda g, s: (0, lanes // rank + s[at_pick], 0))
    normed_moved, normed, ranks, ranks_own, tables, bc, bc_t, scores, rows_f32, cums_t, keep, ups, wides, w_bc, masks = call(
        selecting(prep_kernel, rank=rank, state=state, moved_blocks=by_exchange),
        prep_out,
        prep_specs,
        [full(*s) for s, _ in prep_out],
        [pltpu.VMEM((ext, width), bf16)],
        mat // 4, 6 * mega, 1, grant=vmem_bytes * 5 // 4,
    )(sel, *prep_in)

    def part_at(row, col, *shape):
        return pl.BlockSpec(shape, lambda *s: (row, col))

    def up_at(row, rows, base=0):
        return pl.BlockSpec((rows, group), lambda g, *s: (row, g + base))

    def first_at(row, *shape):
        return pl.BlockSpec(shape, lambda g, *s: (row,) + (0,) * (len(shape) - 1))

    scores_spec, allowed_spec = (first_at(n, 1, blocks, chunk, chunk) for n in range(2))
    b_t_spec, c_t_spec = part_at(0, 0, state, own), part_at(1, 0, state, own)
    masks_spec, masks_after_spec = first_at(0, 3, own, lanes), first_at(1, 3, own, lanes)
    ad_spec, b_up_spec = part_at(0, 0, rank, width), part_at(1, 0, rank, width)
    chunk_rows = stacked(blocks, part, chunk)
    z_specs = weight_specs(w_z)
    p_spec = params_at()
    order_spec = full(group, group)
    u, scaled, sent_state = call(
        plain(proj_kernel, weights=n_w),
        [(big, f32), (big, bf16), ((state, inner), bf16)],
        [full(ext, width)] + weight_specs(w_x)
        + [full(ext, 2 * rank), up_at(1, 2 * rank), p_spec, masks_spec, part_at(0, 0, own, 2 * lanes), cols(lanes),
           b_t_spec],
        [cols(own), cols(own), cols(state)],
        [pltpu.VMEM((ext, group), f32), pltpu.VMEM((own, group), bf16)],
        mat, 12 * mega, grant=vmem_bytes * 5 // 4,
    )(sel, normed_moved, *w_x, ranks, ups, params, masks, tables, ex, bc_t)

    def chain(x, step, sign, *events):
        out, moved = [step(x)], x
        for hop in range(1, hops):
            kept = jnp.roll(keep[7:8], sign * hop * group, axis=1)
            moved = (after(out[-1], *events).astype(f32) * kept).astype(bf16)
            out.append(step(moved))
        return out, moved

    within_specs = [cols(own), part_at(0, 5, own, lanes), chunk_rows, scores_spec, cols(lanes, part * lanes)]
    states_in, moved_state = chain(sent_state, up, -1)
    (y_within,) = call(
        plain(within_kernel), [(big, f32)], within_specs, [cols(own)], [], mat, 6 * mega
    )(sel, after(scaled, moved_state), tables, cums_t, scores, exl)

    states_spec = pl.BlockSpec((blocks, state, group), lambda g, *s: (0, 0, g))
    def steps_in(phase, first, then):
        return lambda p, g: jnp.where(p == phase, g, jnp.where(p < phase, first, then))

    def moving(phase, make):
        at = steps_in(phase, 0, tp_size - 1)
        return lambda p, g, s: make(at(p, g), s)

    def cols_in(phase, rows, size=group, turn=0):
        return pl.BlockSpec((rows, size), moving(phase, lambda i, s: (0, (i + turn) % tp_size)))

    def up_in(phase, row, rows):
        return pl.BlockSpec((rows, group), moving(phase, lambda i, s: (row, i)))

    def weights_in(phase, ws):
        if len(ws) == 1:
            return [pl.BlockSpec((1,) + ws[0].shape[1:], moving(phase, lambda i, s: (s[8 + i], 0, 0)))]
        shape = (2, 1) + ws[0].shape[2:]
        first = pl.BlockSpec(shape, moving(phase, lambda i, s: (0, jnp.minimum(i, 1), 0, 0)))
        second = pl.BlockSpec(shape, moving(phase, lambda i, s: (0, jnp.maximum(i - 2, 0), 0, 0)))
        return [first] * 4 + [second] * 4

    def cols_always(rows, size):
        return pl.BlockSpec((rows, size), lambda p, g, s: (0, g))

    sent_shape = (dp_size, tp_size, 2 * rank, max(d_rows, 2 * hp))
    cot = cotangent[0]
    big3 = (tp_size, own, group)
    states, mixed, sent_out, g_heads, low_z, sent_grad, ahead_sums = call(
        selecting(middle_kernel, weights=n_w, hops=hops, inner=inner),
        [((blocks, state, inner), bf16), ((own, width), f32), (sent_shape, bf16), (big, f32), (big, bf16),
         ((state, inner), bf16), ((own, lanes), f32)],
        [full(ext, width)] + weights_in(0, w_z) + weights_in(1, w_out)
        + [cols_in(0, state, group, -h) for h in range(1, hops + 1)]
        + [full(own, 2 * rank), up_in(0, 0, 2 * rank), pl.BlockSpec((1, 8, group), lambda p, g, s: (g, 0, 0)),
           cols_in(0, own), cols_in(0, own), cols_in(0, own), part_at(0, 1, own, 2 * lanes),
           part_at(0, 4, own, lanes), cols_in(0, 8), cols_always(lanes, group), b_t_spec, c_t_spec,
           part_at(0, 1, own, state), full(own, width), full(own, width), b_up_spec, up_in(1, 4, rank), order_spec,
           pl.BlockSpec((group, lanes), moving(2, lambda i, s: (i, 0)))],
        [pl.BlockSpec((blocks, state, group), moving(0, lambda i, s: (0, 0, i))), full(own, width),
         full(*sent_shape), cols_in(2, own), cols_in(2, own), cols_in(2, state), full(own, lanes)],
        [pltpu.VMEM(big3, f32), pltpu.VMEM(big3, f32), pltpu.VMEM(big3, f32), pltpu.VMEM(big3, f32),
         pltpu.VMEM(big3, f32),
         pltpu.VMEM((own, lanes), f32), pltpu.VMEM((own, lanes), f32), pltpu.VMEM((own, width), f32),
         pltpu.VMEM((own, width), bf16), pltpu.VMEM((own, 2 * rank), bf16), pltpu.VMEM((own, rank), f32),
         pltpu.VMEM((own, group), bf16)],
        4 * mat, 40 * mega, (3, tp_size), grant=vmem_bytes * 5 // 4,
    )(sel, normed_moved, *w_z, *w_out, *states_in, ranks_own, ups, params, y_within, u, scaled, tables, tables, keep,
      ex, bc_t, bc_t, bc, cot, tok, wides, ups, order, red)
    red_spec = pl.BlockSpec((group, lanes), lambda g, *s: (g, 0))
    d_within, d_scores, ahead = call(
        plain(back_within_kernel),
        [(big, f32), ((blocks, chunk, chunk), f32), ((own, lanes), f32)],
        [cols(own), full(own, lanes)] + within_specs + [red_spec],
        [cols(own), full(blocks, chunk, chunk), full(own, lanes)],
        [pltpu.VMEM((own, group), f32)],
        2 * mat, 14 * mega, grant=vmem_bytes * 5 // 4,
    )(sel, g_heads, ahead_sums, scaled, tables, cums_t, scores, exl, red)
    grads_in, moved_grad = chain(sent_grad, down, 1, ahead)
    low_z = after(low_z, moved_grad)

    acc_z, g_rank_z, p_up_z = call(
        plain(in_z_kernel, weights=n_w),
        [((own, width), f32), ((own, rank), f32), ((tp_size, rank, group), f32)],
        [cols(own)] + z_specs + [up_at(0, rank), full(own, 2 * rank)],
        [full(own, width), full(own, rank), stacked(rank, group)],
        [],
        mat, 8 * mega,
    )(sel, low_z, *w_z, ups, ranks_own)

    grads_in = [after(x, acc_z) for x in grads_in]
    edges_shape = (edge, inner + 2 * state)
    low_x, g_u_bc, low_dt, edges, tail = call(
        plain(back_state_kernel, hops=hops),
        [(big, bf16), ((own, 2 * state), f32), ((own, heads), bf16), (edges_shape, bf16), ((edge, inner), f32)],
        [cols(state, group, h) for h in range(1, hops + 1)]
        + [states_spec, cols(own), cols(own), cols(own), cols(own), p_spec, full(own, 2 * state), c_t_spec,
           part_at(0, 0, own, 4 * lanes), cols(8), part_at(0, 0, 8, lanes), cols(lanes), red_spec,
           full(blocks, chunk, chunk), full(own, lanes), allowed_spec, full(own, 2 * state + lanes),
           masks_after_spec],
        [cols(own), full(own, 2 * state), full(own, heads), full(*edges_shape), cols(edge)],
        [pltpu.VMEM((own, state), f32), pltpu.VMEM((own, state), f32), pltpu.VMEM((own, lanes), f32),
         pltpu.VMEM((own, lanes), f32), pltpu.VMEM((8, lanes), f32), pltpu.VMEM((2, own, group), bf16),
         pltpu.VMEM((8, group), f32)],
        mat, 24 * mega,
    )(sel, *grads_in, states, g_heads, scaled, d_within, u, params, bc, bc_t, tables, keep, keep, ex, red, d_scores,
      ahead, scores, rows_f32, masks)

    halo = down(edges)
    low_x, g_rank, sent_in = call(
        selecting(in_x_kernel),
        [(big, bf16), ((own, rank), f32), (sent_shape, bf16)],
        [cols(own), cols(edge), cols(edge, group, 1), up_at(2, rank), full(own, 2 * rank), p_spec, masks_after_spec,
         full(own, rank), stacked(rank, group), order_spec, full(own, width)],
        [pl.BlockSpec((edge, group), lambda g, *s: (own // edge - 1, g)), full(own, rank), full(*sent_shape)],
        [pltpu.VMEM((own, group), bf16)],
        mat // 8, 8 * mega, in_place={0: 0},
    )(sel, low_x, tail, halo, ups, ranks_own, params, masks, g_rank_z, p_up_z, order, normed)

    (tokens_grad,) = call(
        selecting(tokens_kernel, weights=n_w),
        [((own, width), f32)],
        [cols(own)] + weight_specs(w_x)
        + [full(own, width), full(own, rank), full(own, 2 * state),
           pl.BlockSpec((edge, 2 * state), lambda g, *s: (0, inner // (2 * state))),
           full(8, 2 * state), full(width, 2 * state), full(own, heads), full(heads, width), ad_spec,
           masks_after_spec, full(own, width), full(own, width), full(1, width)],
        [full(own, width)],
        [pltpu.VMEM((own, width), f32), pltpu.VMEM((own, 2 * state), bf16), pltpu.VMEM((own, width), f32)],
        mat, 14 * mega, grant=vmem_bytes * 5 // 4,
    )(sel, low_x, *w_x, acc_z, g_rank, g_u_bc, halo, params_bc, w_bc, low_dt, dt_t, wides, masks, tok, cot,
      norm_gain[None])

    sent = jnp.concatenate([sent_out, sent_in], axis=2)
    arrived = lax.all_to_all(sent.reshape((-1,) + sent.shape[2:]), both, 0, 0, tiled=True)
    arrived = arrived.reshape(sent.shape)
    shapes = [(adapters, rank, d_rows), (adapters, hp, rank), (adapters, rank, d_rows), (adapters, 2 * hp, rank)]
    grad_out_up, grad_out_down, grad_in_down, grad_in_up = call(
        selecting(collect_kernel), [(s, f32) for s in shapes], [full(*sent.shape)],
        [full(*s) for s in shapes], [pltpu.VMEM((dp_size,) + sent.shape[2:], f32)], mega, mega, 1,
    )(picks, arrived)

    grad_out_down = grad_out_down.reshape(out_down.shape)
    grad_in_down = grad_in_down.transpose(0, 2, 1)
    grad_in_up = grad_in_up.reshape(adapters, 2, part, p_part, rank).transpose(0, 4, 1, 2, 3)
    return (mixed[None], tokens_grad[None], grad_in_down, grad_in_up, grad_out_down, grad_out_up)


def solution(mesh):
    placed = (
        P("dp", "tensor", None),
        P("dp", "tensor", None),
        P("dp", None),
        P("dp"),
        P(),
        P("dp", None, "tensor"),
        P("dp", None),
        P("dp", "tensor"),
        P(None, "tensor"),
        P(),
        P("tensor"),
        P(),
        P("tensor"),
        P("tensor"),
        P("tensor"),
        P("tensor"),
        P("tensor", "dp"),
        P(None, "dp", None),
        P(None, None, None, "tensor", "dp"),
        P(None, "tensor", "dp", None),
        P(None, None, "dp"),
    )
    return jax.shard_map(
        shards,
        mesh=mesh,
        in_specs=placed,
        out_specs=(
            P("dp", "tensor", None),
            P("dp", "tensor", None),
            P(None, "dp", None),
            P(None, None, None, "tensor", "dp"),
            P(None, "tensor", "dp", None),
            P(None, None, "dp"),
        ),
        check_vma=False,
    )
```

```python
import math

import jax
import jax.numpy as jnp
import numpy as np
from jax import lax
from jax.experimental import pallas as pl
from jax.experimental.pallas import tpu as pltpu
from jax.sharding import PartitionSpec as P

epsilon = 1e-05
chunk = 128
lanes = 128
doc_most = 800
edge = 16
f32, bf16 = jnp.float32, jnp.bfloat16
exact = lax.Precision.HIGHEST
vmem_bytes = 48 * 1024 * 1024


def dot(a, b):
    return jnp.dot(a, b, preferred_element_type=f32)


def dot_nt(a, b):
    return lax.dot_general(a, b, (((1,), (1,)), ((), ())), preferred_element_type=f32)


def dot_tn(a, b):
    return lax.dot_general(a, b, (((0,), (0,)), ((), ())), preferred_element_type=f32)


def halves(x):
    high = x.astype(bf16)
    return high, (x - high.astype(f32)).astype(bf16)


def pieces(x, count):
    out = []
    for _ in range(count):
        part = lax.reduce_precision(x, 8, 7)
        out.append(part.astype(bf16))
        x = x - part
    return jnp.concatenate(out, axis=-1)


def dot2(x, w):
    high, low = halves(x)
    return dot(high, w) + dot(low, w)


def dot2_nt(x, w):
    high, low = halves(x)
    return dot_nt(high, w) + dot_nt(low, w)


def dot2_tn(x, w):
    high, low = halves(x)
    return dot_tn(high, w) + dot_tn(low, w)


def tile_lanes(m, width):
    return m if width == lanes else jnp.concatenate([m] * (width // lanes), axis=1)


def sigmoid(u):
    return 0.5 + 0.5 * jnp.tanh(0.5 * u)


def silu(u):
    return u * sigmoid(u)


def silu_parts(u):
    s = sigmoid(u)
    v = u * s
    return v, s + v * (1.0 - s)


korder = (0, 2, 4, 6, 1, 3, 5, 7)


def weight_pieces(refs, at=0):
    if len(refs) == 1:
        return [(refs[0][...].reshape(-1, refs[0].shape[-1]), None)]
    pairs = ((0, 1), (2, 3), (4, 5), (6, 7)) if at == 0 else ((0, 2), (1, 3), (4, 6), (5, 7))
    return [
        (ref[...].reshape(2 * lanes, ref.shape[-1]), pair) for ref, pair in zip(refs[4 * at : 4 * at + 4], pairs)
    ]


def block_at(n):
    return slice(n * lanes, (n + 1) * lanes)


def with_weight(refs, body, half):
    if len(refs) == 1:
        body(weight_pieces(refs))
        return
    if isinstance(half, int):
        body(weight_pieces(refs * 2, half))
        return

    @pl.when(half == 0)
    def _():
        body(weight_pieces(refs, 0))

    @pl.when(half == 1)
    def _():
        body(weight_pieces(refs, 1))


def times(left, parts):
    total = None
    for w, pair in parts:
        if pair is None:
            value = left(slice(None))
        elif pair[1] == pair[0] + 1:
            value = left(slice(pair[0] * lanes, (pair[1] + 1) * lanes))
        else:
            value = jnp.concatenate([left(block_at(n)) for n in pair], axis=1)
        term = dot(value, w)
        total = term if total is None else total + term
    return total


def add_times_transposed(acc, low, parts):
    for w, pair in parts:
        term = dot_nt(low, w)
        if pair is None:
            acc[...] += term
        elif pair[1] == pair[0] + 1:
            acc[:, pair[0] * lanes : (pair[1] + 1) * lanes] += term
        else:
            for i, n in enumerate(pair):
                acc[:, block_at(n)] += term[:, block_at(i)]


def rows_of(c):
    return slice(c * chunk, (c + 1) * chunk)


def sums3(tri, x):
    high, mid = halves(x)
    low = (x - high.astype(f32) - mid.astype(f32)).astype(bf16)
    return dot(tri, high) + dot(tri, mid) + dot(tri, low)


def parts_of(x, count):
    out = []
    for _ in range(count):
        part = x.astype(bf16)
        out.append(part)
        x = x - part.astype(f32)
    return jnp.concatenate(out, axis=1)


def table_of(x, count):
    parts = parts_of(x, count)
    return jnp.concatenate([parts, jnp.zeros((x.shape[0], lanes - parts.shape[1]), bf16)], axis=1)


def column(row):
    return jnp.broadcast_to(row, (lanes, lanes)).T


def prep_kernel(sel, tokens, halo, norm_gain, small, picked, dt_t, inner_t, place, params, params_bc, segs, ex, no_out,
                normed, ranks, ranks_own, tables, bc_out, bct_out, scores, rows_out, cums_t, keep, ups, wides, w_bc,
                masks, ext, *, rank, state, moved_blocks):
    own, width = tokens.shape
    blocks = own // chunk
    tp, _, group = params.shape
    heads = dt_t.shape[0]
    part = heads // tp
    turn, pick, bound, small_at = 8 + tp, sel[8 + 2 * tp], 9 + 2 * tp, 9 + 2 * tp + 2 * blocks

    for c in range(blocks):
        wide = tokens[rows_of(c), :].astype(f32)
        scale = lax.rsqrt(jnp.sum(wide * wide, axis=1, keepdims=True) / width + epsilon)
        ext[edge + c * chunk : edge + (c + 1) * chunk, :] = (wide * scale * norm_gain[...]).astype(bf16)
    ext[:edge, :] = halo[...]
    for j in range(8):
        k = korder[j]
        at = pl.ds(pl.multiple_of(sel[k] * lanes, lanes), lanes)
        cols = slice(j * lanes, (j + 1) * lanes)
        no_out[:, cols] = ext[:, at]
        at = sel[small_at + j]
        wides[:, cols] = picked[at]
        w_bc[j * lanes : (j + 1) * lanes, :state] = small[at, :lanes, :]
        w_bc[j * lanes : (j + 1) * lanes, state:] = small[at, lanes : 2 * lanes, :]
    normed[...] = ext[edge:, :]
    ranks[...] = parts_of(dot_nt(ext[...], wides[:rank, :]), 2)
    ranks_own[...] = ranks[edge:, :]
    bc = dot(ext[...], w_bc[...])

    hp = place.shape[1]
    for s in range(tp):
        cols = slice(s * group, (s + 1) * group)
        z = x = d = None
        for k in range(inner_t.shape[1]):
            where = place[sel[korder[k]]] if moved_blocks else place[k]
            piece = inner_t[sel[turn + s], k]
            terms = (dot(piece[:rank, :hp], where), dot(piece[:rank, hp : 2 * hp], where),
                     dot(piece[rank:, :hp], where))
            z, x, d = terms if z is None else (z + terms[0], x + terms[1], d + terms[2])
        z, x = z.astype(bf16), x.astype(bf16)
        ups[:, cols] = jnp.concatenate([z, z, x, x, d.astype(bf16)], axis=0)

    i = lax.broadcasted_iota(jnp.int32, (chunk, chunk), 0)
    j = lax.broadcasted_iota(jnp.int32, (chunk, chunk), 1)
    tril = jnp.where(j <= i, 1.0, 0.0)
    segs_at = []
    for c in range(blocks):
        rows = rows_of(c)
        seg = column(segs[3, c : c + 1, :])
        segs_at.append(seg[:, :heads])
        for k in range(1, 4):
            masks[k - 1, rows, :] = jnp.where(column(segs[3 - k, c : c + 1, :]) == seg, 1.0, 0.0)
            masks[k + 2, rows, :] = jnp.where(column(segs[3 + k, c : c + 1, :]) == seg, 1.0, 0.0)
        cur = bc[edge + c * chunk - 8 : edge + (c + 1) * chunk]
        total = params_bc[3:4, :] * cur[8:] + params_bc[4:5, :]
        for k in range(1, 4):
            shifted = pltpu.roll(cur, k, 0)[8:]
            total = total + params_bc[3 - k : 4 - k, :] * (
                shifted * tile_lanes(masks[k - 1, rows, :], 2 * state)
            )
        rows_out[rows, : 2 * state] = total
        value = silu(total)
        inb, inc = value[:, :state], value[:, state:]
        bc_out[rows, :] = value.astype(bf16)
        bct_out[:state, rows] = inb.T.astype(bf16)
        bct_out[state:, rows] = inc.T.astype(bf16)
        okay = jnp.where(seg == segs[3, c : c + 1, :], tril, 0.0)
        scores[1, c] = okay
        scores[0, c] = dot_nt(inc.astype(bf16), inb.astype(bf16)) * okay

    bias = jnp.concatenate([params[sel[turn + s], 7:8, :part] for s in range(tp)], axis=1)
    a_log = jnp.concatenate([params[sel[turn + s], 7:8, part : 2 * part] for s in range(tp)], axis=1)
    decays = -jnp.exp(a_log)
    raw = dot_nt(ext[edge:, :], dt_t[...]) + bias
    dt = jnp.maximum(raw, 0.0) + jnp.log1p(jnp.exp(-jnp.abs(raw)))
    rows_out[:, 2 * state :] = jnp.concatenate([sigmoid(raw), jnp.zeros((own, lanes - heads), f32)], axis=1)
    tables[:, :lanes] = table_of(dt, 2)
    logs = dt * decays * math.log2(math.e)
    bounds = [sel[bound + n].astype(f32) for n in range(2 * blocks)]
    before_seg, last_seg = bounds[0], bounds[-1]
    prior = jnp.zeros((1, heads), f32)
    all_cums, keeps = [], []
    tri = tril.astype(bf16)
    for c in range(blocks):
        rows = rows_of(c)
        before_c, last_c = bounds[2 * c], bounds[2 * c + 1]
        cums = sums3(tri, logs[rows])
        end = cums[chunk - 1 : chunk]
        seg = segs_at[c]
        tables[rows, 5 * lanes :] = table_of(cums, 3)
        flipped = jnp.concatenate([cums, jnp.zeros((chunk, lanes - heads), f32)], axis=1).T
        for s in range(tp):
            cums_t[s, c] = flipped[s * part : (s + 1) * part]
        tables[rows, 2 * lanes : 3 * lanes] = table_of(jnp.where(seg == before_c, jnp.exp2(cums), 0.0), 2)
        tables[rows, 3 * lanes : 4 * lanes] = table_of(jnp.where(seg == last_c, jnp.exp2(end - cums), 0.0), 2)
        keeps.append(jnp.where(before_c == last_c, jnp.exp2(end), 0.0))
        all_cums.append(cums + prior)
        prior = prior + end
    for c in range(blocks):
        rows = rows_of(c)
        seg = segs_at[c]
        tables[rows, 4 * lanes : 5 * lanes] = table_of(jnp.where(seg == before_seg, jnp.exp2(all_cums[c]), 0.0), 2)
        tables[rows, lanes : 2 * lanes] = table_of(jnp.where(seg == last_seg, jnp.exp2(prior - all_cums[c]), 0.0), 2)
    whole = jnp.where(before_seg == last_seg, jnp.exp2(prior), 0.0)
    table = jnp.concatenate(keeps + [jnp.zeros((7 - blocks, heads), f32), whole], axis=0)
    high, mid = halves(table)
    low = (table - high.astype(f32) - mid.astype(f32)).astype(bf16)
    spread = ex[:heads, :]
    keep[...] = dot(high, spread) + dot(mid, spread) + dot(low, spread)
    keep[6:7, :lanes] = jnp.concatenate([decays, jnp.zeros((1, lanes - heads), f32)], axis=1)


def pack_kernel(bc, dt_weight, in_down, out_up, in_up, out_down, pick, out):
    rows, two = bc.shape
    part = dt_weight.shape[0]
    count, rank, _ = in_down.shape
    at = 2 * rows
    out[:rows, :] = bc[:, : two // 2]
    out[rows:at, :] = bc[:, two // 2 :]
    for b in range(count):
        out[at + 2 * rank * b : at + 2 * rank * b + rank, :] = in_down[b]
        out[at + 2 * rank * b + rank : at + 2 * rank * (b + 1), :] = out_up[b]
    at += 2 * rank * count
    for b in range(count):
        out[at + 2 * rank * b : at + 2 * rank * b + rank, :] = in_up[b].astype(f32).T.astype(bf16)
        flipped = out_down[b].astype(f32).T
        out[at + 2 * rank * b + rank : at + 2 * rank * (b + 1), :] = jnp.concatenate(
            [flipped, jnp.zeros_like(flipped)], axis=1
        ).astype(bf16)
    at += 2 * rank * count
    wide = jnp.concatenate([dt_weight[...].astype(f32), jnp.zeros((16 - part, rows), f32)], axis=0)
    out[at : at + 16, :] = wide.astype(bf16)
    out[at + 16 : at + 32, :] = jnp.zeros((16, lanes), bf16) + pick[0].astype(f32).astype(bf16)


def proj_kernel(left, *refs, weights):
    refs, ws = refs[weights:], refs[:weights]
    ranks, a_up, params, masks, tables, ex, b_t, u_out, sc_out, f_out, xs, moved = refs

    def body(parts):
        xs[...] = times(lambda at: left[:, at], parts) + dot(ranks[...], a_up[...])

    with_weight(ws, body, pl.program_id(0) // 2)
    own, width = u_out.shape
    step = min(width, 256)
    dt_wide, out_wide = dot(tables[:, :lanes], ex[...]), dot(tables[:, lanes:], ex[...])
    for c in range(own // chunk):
        rows = rows_of(c)
        for n in range(width // step):
            cols = slice(n * step, (n + 1) * step)
            cur = xs[edge + c * chunk - 8 : edge + (c + 1) * chunk, cols]
            total = params[0, 3:4, cols] * cur[8:] + params[0, 4:5, cols]
            for k in range(1, 4):
                shifted = pltpu.roll(cur, k, 0)[8:]
                total = total + params[0, 3 - k : 4 - k, cols] * (
                    shifted * tile_lanes(masks[k - 1, rows, :], step)
                )
            u_out[rows, cols] = total
            value = silu(total)
            scaled = (dt_wide[rows, cols] * value).astype(bf16)
            sc_out[rows, cols] = scaled
            moved[rows, cols] = (out_wide[rows, cols] * scaled.astype(f32)).astype(bf16)
    f_out[...] = dot(b_t[...], moved[...]).astype(bf16)

def pair_parts(lcol, cums_t, p):
    lc = lcol[:, p * 2 * lanes : (p + 1) * 2 * lanes]
    lr = jnp.concatenate([cums_t[2 * p : 2 * p + 1, :], cums_t[2 * p + 1 : 2 * p + 2, :]], axis=1)
    return jnp.exp2(jnp.minimum(lc - lr, 0.0))


def two_heads(v, head_size):
    lane = lax.broadcasted_iota(jnp.int32, v.shape, 1)
    zero = jnp.zeros_like(v)
    return jnp.concatenate([jnp.where(lane < head_size, v, zero), jnp.where(lane < head_size, zero, v)], 0)


def within_kernel(sc, cums3, cums_t, scores, exl, y_out):
    own, width = y_out.shape
    wide = dot(cums3[...], exl[...])
    for c in range(own // chunk):
        rows = rows_of(c)
        lcol = wide[rows]
        allowed = tile_lanes(scores[0, c], 2 * lanes)
        for p in range(width // lanes):
            e = pair_parts(lcol, cums_t[0, c], p)
            m = (e * allowed).astype(bf16)
            cols = slice(p * lanes, (p + 1) * lanes)
            y_out[rows, cols] = dot(m, two_heads(sc[rows, cols], lanes // 2))


def row_scale_of(sumsq, inner):
    return lax.rsqrt(jnp.sum(sumsq, axis=1, keepdims=True) / inner + epsilon)


def put_width_parts(sent, value):
    rank = value.shape[0]
    dp, tp, _, _ = sent.shape
    size = value.shape[1] // dp
    for d in range(dp):
        piece = value[:, d * size : (d + 1) * size].astype(bf16)
        for t in range(tp):
            sent[d, t, :rank, :size] = piece


def put_inner_parts(sent, to, value, order, offset):
    rank = value.shape[0]
    dp = sent.shape[0]
    hp = value.shape[1] // dp
    moved = dot(value.astype(bf16), order[...]).astype(bf16)
    for d in range(dp):
        sent[d, to, rank : 2 * rank, offset : offset + hp] = moved[:, d * hp : (d + 1) * hp]


def middle_kernel(sel, left, *refs, weights, hops, inner):
    zs, outs, refs = refs[:weights], refs[weights : 2 * weights], refs[2 * weights :]
    s_ins, refs = refs[:hops], refs[hops:]
    (ranks, a_up, params, yw, u, sc, tables, own_in, keep, ex, b_t, c_t, in_c, cot, tokens, b_up, b_down, order, red,
     states, mixed, sent, gh_out, lz_out, g_out, ahead,
     ys, heads, gate_z, gated, gg, sumsq, dots, acc, cots, g_rank, rank, low) = refs
    phase, g = pl.program_id(0), pl.program_id(1)
    last = pl.num_programs(1) - 1
    half = g // 2
    own, width = gh_out.shape
    step = min(width, 256)
    blocks = own // chunk

    @pl.when((phase == 0) & (g == 0))
    def _():
        ahead[...] = jnp.zeros_like(ahead)
        sumsq[...] = jnp.zeros_like(sumsq)
        acc[...] = jnp.zeros_like(acc)
        rank[...] = jnp.zeros_like(rank)
        dots[...] = jnp.zeros_like(dots)
        sent[...] = jnp.zeros_like(sent)
        for j in range(8):
            at = pl.ds(pl.multiple_of(sel[korder[j]] * lanes, lanes), lanes)
            cots[:, j * lanes : (j + 1) * lanes] = cot[:, at]
        g_rank[...] = parts_of(dot_nt(cot[...], b_up[...]), 2)

    @pl.when(phase == 0)
    def _():
        def body(parts):
            first = left.shape[0] - own
            gate_z[g] = times(lambda at: left[first:, at], parts) + dot(ranks[...], a_up[...])

        with_weight(zs, body, half)
        in_wide, out_wide = dot(tables[:, :lanes], ex[...]), dot(tables[:, lanes:], ex[...])
        for n in range(width // step):
            cols = slice(n * step, (n + 1) * step)
            new = []
            for c in range(blocks):
                rows = rows_of(c)
                moved = (out_wide[rows, cols] * sc[rows, cols].astype(f32)).astype(bf16)
                new.append(dot(b_t[:, rows], moved))
            s = sum(r[:, cols].astype(f32) for r in s_ins)
            for c in range(blocks):
                states[c, :, cols] = s.astype(bf16)
                s = s * keep[c : c + 1, cols] + new[c]
            for c in range(blocks):
                rows = rows_of(c)
                y = yw[rows, cols] + in_wide[rows, cols] * dot(in_c[rows, :], states[c, :, cols])
                ys[g, rows, cols] = y
                head = y + params[0, 6:7, cols] * silu(u[rows, cols])
                heads[g, rows, cols] = head
                gd = head * silu(gate_z[g, rows, cols])
                gated[g, rows, cols] = gd
                sq = gd * gd
                total = sumsq[rows, :]
                for i in range(step // lanes):
                    total = total + sq[:, i * lanes : (i + 1) * lanes]
                sumsq[rows, :] = total

    @pl.when(phase == 1)
    def _():
        scale = row_scale_of(sumsq[...], inner)
        normed_inner = gated[g] * scale * params[0, 5:6, :]
        high, rest = halves(normed_inner)
        low[...] = high
        rank[...] += dot_nt(high, b_down[...]) + dot_nt(rest, b_down[...])
        size = rank.shape[1]
        both = dot_tn(g_rank[...], high)
        put_inner_parts(sent, sel[8 + g], both[:size] + both[size:], order, 0)

        def body(parts):
            twice = jnp.concatenate([b_down[...], b_down[...]], axis=0)
            value = (times(lambda at: cots[:, at], parts) + dot(g_rank[...], twice)) * params[0, 5:6, :]
            gg[g] = value
            prod = value * gated[g]
            total = dots[...]
            for i in range(width // lanes):
                total = total + prod[:, i * lanes : (i + 1) * lanes]
            dots[...] = total
            add_times_transposed(acc, low[...], parts)

        with_weight(outs, body, half)

    @pl.when((phase == 1) & (g == last))
    def _():
        put_width_parts(sent, dot2_tn(rank[...], cot[...]))
        mixed[...] = tokens[...].astype(f32) + dot2(rank[...], b_up[...])
        for j in range(8):
            at = pl.ds(pl.multiple_of(sel[korder[j]] * lanes, lanes), lanes)
            mixed[:, at] += acc[:, j * lanes : (j + 1) * lanes]

    @pl.when(phase == 2)
    def _():
        scale = row_scale_of(sumsq[...], inner)
        coef = scale * scale * scale * (jnp.sum(dots[...], axis=1, keepdims=True) / inner)
        own_wide = dot(own_in[...], ex[...])
        for c in range(blocks):
            rows = rows_of(c)
            sc_rows, co_rows = scale[rows], coef[rows]
            for n in range(width // step):
                cols = slice(n * step, (n + 1) * step)
                g_gated = gg[g, rows, cols] * sc_rows - gated[g, rows, cols] * co_rows
                gate, slope = silu_parts(gate_z[g, rows, cols])
                lz_out[rows, cols] = (g_gated * heads[g, rows, cols] * slope).astype(bf16)
                gh = g_gated * gate
                gh_out[rows, cols] = gh
                low[rows, cols] = (own_wide[rows, cols] * gh).astype(bf16)
                ys[g, rows, cols] = ys[g, rows, cols] * gh
        ahead[...] += dot2(ys[g], red[...])
        g_out[...] = dot(c_t[...], low[...]).astype(bf16)


def back_within_kernel(gh, ahead_in, sc, cums3, cums_t, scores, exl, red, dv_out, ds_out, ahead, prod):
    g = pl.program_id(0)

    @pl.when(g == 0)
    def _():
        ds_out[...] = jnp.zeros_like(ds_out)
        ahead[...] = ahead_in[...]

    own, width = dv_out.shape
    wide = dot(cums3[...], exl[...])
    for c in range(own // chunk):
        rows = rows_of(c)
        lcol = wide[rows]
        allowed = tile_lanes(scores[0, c], 2 * lanes)
        ds = jnp.zeros((chunk, lanes), f32)
        for p in range(width // lanes):
            cols = slice(p * lanes, (p + 1) * lanes)
            e = pair_parts(lcol, cums_t[0, c], p)
            m = (e * allowed).astype(bf16)
            v = sc[rows, cols]
            dy = gh[rows, cols]
            high, low = halves(dy)
            both = two_heads(v, lanes // 2)
            parts = jnp.concatenate([high, low], axis=1)
            dm = dot_nt(parts, jnp.concatenate([both, both], axis=1))
            eds = e * dm
            ds = ds + eds[:, :lanes] + eds[:, lanes:]
            dvb = dot_tn(m, high) + dot_tn(m, low)
            lane = lax.broadcasted_iota(jnp.int32, (chunk, lanes), 1)
            dv = jnp.where(lane < lanes // 2, dvb[:chunk], dvb[chunk:])
            dv_out[rows, cols] = dv
            prod[rows, cols] = v.astype(f32) * dv
        ds_out[c] += ds
    ahead[...] -= dot2(prod[...], red[...])


def conv_back(cur, params, masks, rows, width):
    total = params[3:4, :] * cur[:chunk]
    for k in range(1, 4):
        shifted = pltpu.roll(cur, cur.shape[0] - k, 0)[:chunk]
        total = total + params[3 - k : 4 - k, :] * (shifted * tile_lanes(masks[k - 1, rows, :], width))
    return total


def back_state_kernel(*refs, hops):
    grads_in, refs = refs[:hops], refs[hops:]
    (states, gh, sc, dv, u, params, bc, c_t, tables, keep, decays, ex, red, ds, ahead, allowed, rows_in, masks, lx_out, gbc_out,
     ldt_out, edges, tail, db, dc, behind, direct, carry, prods, carries) = refs
    state = c_t.shape[0]
    g = pl.program_id(0)

    @pl.when(g == 0)
    def _():
        for ref in (db, dc, behind, direct, carry, carries):
            ref[...] = jnp.zeros_like(ref)

    own, width = lx_out.shape
    step = min(width, 256)
    blocks = own // chunk
    dt_wide, in_wide = dot(tables[:, :lanes], ex[...]), dot(tables[:, 2 * lanes : 3 * lanes], ex[...])
    out_wide = dot(tables[:, 3 * lanes :], ex[...])
    for n in range(width // step):
        cols = slice(n * step, (n + 1) * step)
        gs = sum(r[:, cols].astype(f32) for r in grads_in)
        following = jnp.zeros((8, step), f32)
        for c in reversed(range(blocks)):
            rows = rows_of(c)
            low_g = gs.astype(bf16)
            kept = keep[c : c + 1, cols]
            low_s = states[c, :, cols]
            scaled = sc[rows, cols].astype(f32)
            eo = out_wide[rows, cols]
            dvs = eo * dot(bc[rows, :state], low_g)
            db[rows, :] += dot_nt((eo * scaled).astype(bf16), low_g)
            dy = gh[rows, cols]
            moved = (in_wide[rows, cols] * dy).astype(bf16)
            dc[rows, :] += dot_nt(moved, low_s)
            carried = jnp.sum(low_s.astype(f32) * gs, axis=0, keepdims=True) * kept
            carries[c : c + 1, cols] = carried
            gs = gs * kept + dot(c_t[:, rows], moved)
            g_sc = dv[rows, cols] + dvs
            v, slope = silu_parts(u[rows, cols])
            prods[0, rows, cols] = (scaled * dvs).astype(bf16)
            prods[1, rows, cols] = (v * g_sc).astype(bf16)
            g_v = dt_wide[rows, cols] * g_sc + params[0, 6:7, cols] * dy
            g_u = g_v * slope
            g_x = conv_back(jnp.concatenate([g_u, following], axis=0), params[0, :, cols], masks, rows, step)
            lx_out[rows, cols] = g_x.astype(bf16)
            following = g_u[:8]
            if c == blocks - 1:
                tail[:, cols] = g_x[-edge:]
            if c == 0:
                at = pl.ds(pl.multiple_of(g * width + n * step, lanes), step)
                edges[:, at] = g_u[:edge].astype(bf16)
    behind[...] += dot(prods[0], red[...])
    direct[...] += dot(prods[1], red[...])
    carry[...] += dot2(carries[...], red[...])

    @pl.when(g == pl.num_programs(0) - 1)
    def _():
        i = lax.broadcasted_iota(jnp.int32, (chunk, chunk), 0)
        j = lax.broadcasted_iota(jnp.int32, (chunk, chunk), 1)
        at_most = jnp.where(i <= j, 1.0, 0.0).astype(bf16)
        below = jnp.where(j < i, 1.0, 0.0).astype(bf16)
        decay_row = decays[6:7, :]
        for c in range(blocks):
            rows = rows_of(c)

            g_logs = sums3(at_most, ahead[rows, :]) + sums3(below, behind[rows, :]) + carry[c : c + 1, :]
            heads = ldt_out.shape[1]
            g_dt = (direct[rows, :] + g_logs * decay_row) * rows_in[rows, 2 * state :]
            ldt_out[rows, :] = g_dt[:, :heads].astype(bf16)
            g_scores = ds[c] * allowed[0, c]
            low_ds = g_scores.astype(bf16)
            gc = dc[rows, :] + dot(low_ds, bc[rows, :state])
            gb = db[rows, :] + dot_tn(low_ds, bc[rows, state:])
            g_bc = jnp.concatenate([gb, gc], axis=1)
            _, slope = silu_parts(rows_in[rows, : 2 * state])
            gbc_out[rows, :] = g_bc * slope
            if c == 0:
                edges[:, edges.shape[1] - g_bc.shape[1] :] = (g_bc * slope)[:edge].astype(bf16)


def in_z_kernel(lz, *refs, weights):
    ws, refs = refs[:weights], refs[weights:]
    a_up, ranks, acc, g_rank, p_up = refs

    @pl.when(pl.program_id(0) == 0)
    def _():
        acc[...] = jnp.zeros_like(acc)
        g_rank[...] = jnp.zeros_like(g_rank)

    size = g_rank.shape[1]
    g_rank[...] += dot_nt(lz[...], a_up[...])
    both = dot_tn(ranks[...], lz[...])
    p_up[0] = both[:size] + both[size:]
    with_weight(ws, lambda parts: add_times_transposed(acc, lz[...], parts), pl.program_id(0) // 2)


def in_x_kernel(sel, lx, tail, halo, a_up, ranks, params, masks, g_rank_z, p_up_z, order, normed,
                fixed, g_rank, sent, low):
    g = pl.program_id(0)

    @pl.when(g == 0)
    def _():
        g_rank[...] = g_rank_z[...]
        sent[...] = jnp.zeros_like(sent)

    own, width = low.shape
    beyond = jnp.concatenate([jnp.zeros((edge, width), f32), halo[...].astype(f32)[:8]], axis=0)
    total = tail[...]
    for k in range(1, 4):
        shifted = pltpu.roll(beyond, beyond.shape[0] - k, 0)[:edge]
        total = total + params[0, 3 - k : 4 - k, :] * (
            shifted * tile_lanes(masks[k - 1, own - edge :, :], width)
        )
    fixed[...] = total.astype(bf16)
    low[: own - edge, :] = lx[: own - edge, :]
    low[own - edge :, :] = total.astype(bf16)
    size = g_rank.shape[1]
    g_rank[...] += dot_nt(low[...], a_up[...])
    both = dot_tn(ranks[...], low[...])
    to = sel[8 + g]
    moved = dot(jnp.concatenate([p_up_z[0], both[:size] + both[size:]], axis=0).astype(bf16), order[...]).astype(bf16)
    hp = width // sent.shape[0]
    for d in range(sent.shape[0]):
        for n in range(2):
            piece = moved[n * size : (n + 1) * size, d * hp : (d + 1) * hp]
            sent[d, to, size : 2 * size, n * hp : (n + 1) * hp] = piece

    @pl.when(g == pl.num_programs(0) - 1)
    def _():
        put_width_parts(sent, dot2_tn(g_rank[...], normed[...]))


def tokens_kernel(sel, lx, *refs, weights):
    ws, refs = refs[:weights], refs[weights:]
    (acc_z, g_rank, gbc, halo_bc, params_bc, w_bc, ldt, dt_t, ad, masks, tokens, cot, norm_gain, grad, acc, lbc,
     g_norm) = refs
    g = pl.program_id(0)

    @pl.when(g == 0)
    def _():
        acc[...] = acc_z[...]

    with_weight(ws, lambda parts: add_times_transposed(acc, lx[...], parts), pl.program_id(0) // 2)

    @pl.when(g == pl.num_programs(0) - 1)
    def _():
        own, width = grad.shape
        blocks = own // chunk
        for c in range(blocks):
            rows = rows_of(c)
            if c < blocks - 1:
                cur = gbc[c * chunk : (c + 1) * chunk + 8, :]
            else:
                cur = jnp.concatenate([gbc[rows, :], halo_bc[...].astype(f32)[:8]], axis=0)
            lbc[rows, :] = conv_back(cur, params_bc[...], masks, rows, gbc.shape[1]).astype(bf16)
        g_norm[...] = (
            dot_nt(lbc[...], w_bc[...]) + dot(ldt[...], dt_t[...])
            + dot(parts_of(g_rank[...], 2), jnp.concatenate([ad[...], ad[...]], axis=0))
        )
        for j in range(8):
            at = pl.ds(pl.multiple_of(sel[korder[j]] * lanes, lanes), lanes)
            g_norm[:, at] += acc[:, j * lanes : (j + 1) * lanes]
        for c in range(blocks):
            rows = rows_of(c)
            wide = tokens[rows, :].astype(f32)
            scale = lax.rsqrt(jnp.sum(wide * wide, axis=1, keepdims=True) / width + epsilon)
            gn = g_norm[rows, :] * norm_gain[...]
            row_dot = jnp.sum(gn * wide, axis=1, keepdims=True)
            grad[rows, :] = (
                cot[rows, :].astype(f32) + gn * scale - wide * (scale * scale * scale * row_dot / width)
            )


def collect_kernel(picks, arrived, up_out, down_out, down_in, up_in, sums):
    dp, tp, rows, _ = arrived.shape
    rank = rows // 4
    sums[...] = jnp.zeros_like(sums)
    for d in range(dp):
        one = arrived[d, 0].astype(f32)
        for t in range(1, tp):
            one = one + arrived[d, t].astype(f32)
        sums[picks[d]] += one
    for b in range(up_out.shape[0]):
        total = sums[b]
        up_out[b] = total[:rank, : up_out.shape[2]]
        down_out[b] = total[rank : 2 * rank].T[: down_out.shape[1]]
        down_in[b] = total[2 * rank : 3 * rank, : down_in.shape[2]]
        up_in[b] = total[3 * rank :].T[: up_in.shape[1]]


def up(x):
    n = lax.axis_size("tensor")
    return lax.ppermute(x, "tensor", [(i, i + 1) for i in range(n - 1)])


def down(x):
    n = lax.axis_size("tensor")
    return lax.ppermute(x, "tensor", [(i + 1, i) for i in range(n - 1)])


def around_tensor(x):
    n = lax.axis_size("tensor")
    return [x] + [lax.ppermute(x, "tensor", [(i, (i + s) % n) for i in range(n)]) for s in range(1, n)]


def swap(x, bit):
    n = lax.axis_size("dp")
    return lax.ppermute(x, "dp", [(i, i ^ (1 << bit)) for i in range(n)])


def all_dp(x):
    count = lax.axis_size("dp").bit_length() - 1
    cur = x.reshape((1,) * count + x.shape)
    for bit in list(range(1, count)) + [0]:
        cur = jnp.concatenate([cur, swap(cur, bit)], axis=count - 1 - bit)
    return cur.reshape((-1,) + x.shape)


def joined_with(x, axis, bit):
    n = lax.axis_size(axis)
    return jnp.concatenate([x, lax.ppermute(x, axis, [(i, i ^ (1 << bit)) for i in range(n)])])


def after(x, *events):
    return lax.optimization_barrier((x, events))[0]


def spread_dp(rotated, events):
    out = []
    curs = [after(jnp.stack(rotated[2 * j : 2 * j + 2]), *events) for j in range(2)]
    firsts = [swap(cur, 1 + j) for j, cur in enumerate(curs)]
    pairs = [jnp.stack([cur, first]) for cur, first in zip(curs, firsts)]
    fars = [swap(pair, 2 - j) for j, pair in enumerate(pairs)]
    for pair, far in zip(pairs, fars):
        out += [pair, far, swap(pair, 0), swap(far, 0)]
    return out, firsts


def gather_plain(x):
    n, tp = lax.axis_size("dp"), lax.axis_size("tensor")
    whole = lax.all_gather(x, ("dp", "tensor")).reshape((n, tp) + x.shape)
    return [whole.transpose(1, 0, 2, 3).reshape(tp, n * x.shape[0], x.shape[1])]


def pad_lanes(x):
    return jnp.pad(x, ((0, 0), (0, lanes - x.shape[1])))


def shards(
    tokens,
    cotangent,
    doc_ids,
    adapter_pick,
    norm_gain,
    gate_x_weight,
    bc_weight,
    dt_weight,
    conv_x_weight,
    conv_bc_weight,
    conv_x_bias,
    conv_bc_bias,
    dt_bias,
    a_log,
    skip_gain,
    inner_gain,
    out_weight,
    in_down,
    in_up,
    out_down,
    out_up,
):
    dp_size, tp_size = lax.axis_size("dp"), lax.axis_size("tensor")
    both = ("dp", "tensor")
    seq_count, own, width = tokens.shape
    assert seq_count == 1 and width == 8 * lanes
    group = gate_x_weight.shape[2]
    inner = group * tp_size
    part = dt_weight.shape[1]
    heads = part * tp_size
    head_size = inner // heads
    assert head_size * 2 == lanes
    state = bc_weight.shape[1] // 2
    rank = in_down.shape[2]
    adapters = in_down.shape[0]
    hops = min(1 + (doc_most - 2) // own, tp_size - 1)
    blocks = own // chunk
    d_rows = gate_x_weight.shape[0]
    p_part = in_up.shape[4]
    hp = part * p_part
    mine, place_at = lax.axis_index("dp"), lax.axis_index("tensor")
    by_exchange = dp_size == 8 and tp_size == 4 and d_rows == lanes
    cot, tok = cotangent[0], tokens[0]

    local_x, local_z, local_out = gate_x_weight[:, 1], gate_x_weight[:, 0], out_weight.T
    if by_exchange:
        ring_x = around_tensor(local_x)

    cuts = [d_rows, d_rows, adapters * 2 * rank, adapters * 2 * rank, 16, 16]
    starts = [sum(cuts[:n]) for n in range(len(cuts))]
    if by_exchange:
        small_in = [
            bc_weight, dt_weight.T, in_down.transpose(0, 2, 1), out_up,
            in_up.transpose(0, 2, 3, 4, 1).reshape(adapters, 2 * hp, rank), out_down.reshape(adapters, hp, rank),
        ]
        vmem = pl.BlockSpec(memory_space=pltpu.VMEM)
        small = pl.pallas_call(
            pack_kernel,
            name="pack_kernel",
            out_shape=jax.ShapeDtypeStruct((sum(cuts), lanes), bf16),
            in_specs=[vmem] * 6 + [pl.BlockSpec(memory_space=pltpu.SMEM)],
            out_specs=vmem,
        )(*small_in, adapter_pick)
    else:
        small = [
            bc_weight[:, :state],
            bc_weight[:, state:],
            jnp.concatenate([in_down.transpose(0, 2, 1), out_up], axis=1).reshape(-1, d_rows),
            jnp.concatenate(
                [in_up.reshape(adapters, rank, 2 * hp),
                 jnp.pad(out_down.reshape(adapters, hp, rank).transpose(0, 2, 1), ((0, 0), (0, 0), (0, hp)))],
                axis=1,
            ).reshape(-1, 2 * hp),
            jnp.pad(dt_weight.T, ((0, 16 - part), (0, 0))),
            jnp.broadcast_to(adapter_pick.astype(bf16)[:, None], (16, lanes)),
        ]
        small = lax.all_gather(jnp.concatenate([pad_lanes(x) for x in small]), "dp")
    if by_exchange:
        natural = jnp.arange(8) ^ mine
    else:
        natural, small_at = jnp.asarray(np.argsort(korder)), jnp.arange(8)

    last = tok[-edge:].astype(f32)
    last_scale = lax.rsqrt(jnp.mean(last * last, axis=1, keepdims=True) + epsilon)
    halo_in = up((last * last_scale * norm_gain).astype(bf16))

    heads_row = jnp.pad(jnp.concatenate([dt_bias, a_log])[None], ((0, 0), (0, group - 2 * part)))
    params = jnp.concatenate(
        [conv_x_weight, conv_x_bias[None], inner_gain[None], jnp.repeat(skip_gain, head_size)[None], heads_row]
    )

    if by_exchange:
        small = joined_with(joined_with(small[None], "dp", 1), "dp", 2)
        params = jnp.stack(around_tensor(after(params, small)))
        small = jnp.concatenate([small, swap(small, 0)])
        w_x, near_x = spread_dp(ring_x, [])
        ring_z = around_tensor(after(local_z, *ring_x[1:]))
        w_z, near_z = spread_dp(ring_z, near_x)
        small_at = jnp.asarray(np.argsort(korder))[natural]
    else:
        w_x, w_z, w_out = gather_plain(local_x), gather_plain(local_z), gather_plain(local_out)
        params = jnp.stack(around_tensor(params))
    pick = adapter_pick[0]
    taken = [small[:, a : a + c] for a, c in zip(starts, cuts)]
    picks = taken[5][:, 0, 0].astype(jnp.int32)
    inner_t = lax.dynamic_slice_in_dim(taken[3], pick * 2 * rank, 2 * rank, 1)
    dt_own = taken[4][:, :part]
    if by_exchange:
        picks, dt_own = picks[small_at], dt_own[small_at]
    if d_rows != lanes:
        fold = lanes // d_rows

        def rows_first(x):
            return x.reshape(8, fold * d_rows, lanes)

        def lanes_last(x):
            x = x[:, :, :d_rows].reshape(8, fold, x.shape[1], d_rows)
            return x.transpose(0, 2, 1, 3).reshape(8, -1, lanes)

        small = jnp.concatenate([rows_first(taken[0]), rows_first(taken[1]), lanes_last(taken[2])], 1)
        dt_own = lanes_last(dt_own)
    dt_own = dt_own.transpose(1, 0, 2).reshape(part, width)
    inner_rows = inner_t.reshape(-1, lanes)
    dt_rows = dt_own.reshape(-1, lanes)
    ring = jnp.concatenate([inner_rows, dt_rows])
    ring = around_tensor(ring)
    if by_exchange:
        ring_out = around_tensor(after(local_out, *ring[1:], *ring_z[1:]))
        w_out, _ = spread_dp(ring_out, near_z)
    ring = jnp.stack(ring)
    inner_t = ring[:, : inner_rows.shape[0]].reshape(tp_size, dp_size, 2 * rank, lanes)
    dt_t = ring[:, inner_rows.shape[0] :]
    dt_t = dt_t.reshape(heads, width)

    docs = doc_ids[0]
    padded = jnp.concatenate([jnp.full((4,), -1, jnp.int32), docs, jnp.full((4,), -2, jnp.int32)])
    near = lax.dynamic_slice_in_dim(padded, place_at * own, own + 8)
    segs = jnp.stack([near[1 + k : 1 + k + own] for k in range(7)]).astype(f32).reshape(7, blocks, chunk)
    bounds = jnp.stack([near[3 : 3 + own : chunk], near[3 + chunk :: chunk][:blocks]], axis=1).reshape(-1)
    groups = (place_at - jnp.arange(tp_size)) % tp_size
    sel = jnp.concatenate([natural, groups, jnp.arange(tp_size), pick[None], bounds, small_at]).astype(jnp.int32)

    def spread(width_each, copies):
        out = np.zeros((lanes, heads * width_each), np.float32)
        at = np.arange(heads * width_each)
        for n in range(copies):
            out[n * heads + at // width_each, at] = 1.0
        return jnp.asarray(out, bf16)

    ex, exl = spread(head_size, 2), spread(lanes, 3)
    red = jnp.asarray(np.arange(inner)[:, None] // head_size == np.arange(lanes)[None, :], bf16)
    at = np.arange(group)
    place = np.zeros((dp_size, hp, group), np.float32)
    place[at % head_size // p_part, at // head_size * p_part + at % p_part, at] = 1.0
    order = jnp.asarray(place.reshape(group, group).T, bf16)
    place = jnp.asarray(place, bf16)

    def full(*shape):
        return pl.BlockSpec(shape, lambda *s: (0,) * len(shape))

    def cols(rows, size=group, turn=0):
        return pl.BlockSpec((rows, size), lambda g, *s: (0, (g + turn) % tp_size))

    def stacked(*shape, base=0):
        return pl.BlockSpec((1,) + shape, lambda g, *s: (g + base,) + (0,) * len(shape))

    def params_at(base=0):
        return stacked(8, group, base=base)

    def weight_specs(ws, half=None):
        if len(ws) == 1:
            base = (half or 0) * tp_size // 2
            return [pl.BlockSpec((1,) + ws[0].shape[1:], lambda g, s: (s[8 + base + g], 0, 0))]
        shape = (2, 1) + ws[0].shape[2:]
        if half is not None:
            return [pl.BlockSpec(shape, lambda g, *s: (0, g, 0, 0))] * 4
        first = pl.BlockSpec(shape, lambda g, *s: (0, jnp.minimum(g, 1), 0, 0))
        second = pl.BlockSpec(shape, lambda g, *s: (0, jnp.maximum(g - 2, 0), 0, 0))
        return [first] * 4 + [second] * 4

    def call(kernel, out, in_specs, out_specs, scratch, flops, moved, steps=tp_size, grant=vmem_bytes, in_place=None):
        kernel, kernel_takes_sel, name = kernel

        def body(sel_ref, *refs):
            return kernel(sel_ref, *refs) if kernel_takes_sel else kernel(*refs)

        return pl.pallas_call(
            body,
            name=name,
            input_output_aliases={1 + i: to for i, to in (in_place or {}).items()},
            out_shape=[jax.ShapeDtypeStruct(s, d) for s, d in out],
            grid_spec=pltpu.PrefetchScalarGridSpec(
                num_scalar_prefetch=1,
                grid=steps if isinstance(steps, tuple) else (steps,),
                in_specs=in_specs,
                out_specs=out_specs,
                scratch_shapes=scratch,
            ),
            compiler_params=pltpu.CompilerParams(
                dimension_semantics=("arbitrary",) * (len(steps) if isinstance(steps, tuple) else 1),
                vmem_limit_bytes=grant,
            ),
            cost_estimate=pl.CostEstimate(flops=flops, bytes_accessed=moved, transcendentals=0),
        )

    def plain(kernel, **static):
        return (lambda *refs: kernel(*refs, **static)), False, kernel.__name__

    def selecting(kernel, **static):
        return (lambda *refs: kernel(*refs, **static)), True, kernel.__name__

    n_w = len(w_x)
    big = (own, inner)
    ext = own + edge
    mat = 2 * own * width * inner
    mega = 1 << 20
    params_bc = jnp.concatenate([conv_bc_weight, conv_bc_bias[None], jnp.zeros((3, 2 * state), f32)])
    prep_out = [
        ((ext, width), bf16), ((own, width), bf16), ((ext, 2 * rank), bf16), ((own, 2 * rank), bf16),
        ((own, 6 * lanes), bf16), ((own, 2 * state), bf16),
        ((2 * state, own), bf16), ((2, blocks, chunk, chunk), f32), ((own, 2 * state + lanes), f32),
        ((tp_size, blocks, part, chunk), f32), ((8, inner), f32), ((5 * rank, inner), bf16),
        ((2 * rank, width), bf16), ((width, 2 * state), bf16), ((6, own, lanes), f32),
    ]
    at_pick = 8 + 2 * tp_size
    prep_in = [tok, halo_in, norm_gain[None], small, small, dt_t, inner_t, place, params, params_bc, segs, ex]
    prep_specs = [full(*x.shape) for x in prep_in]
    prep_specs[3] = full(8, 2 * lanes, lanes)
    prep_specs[4] = pl.BlockSpec((8, 2 * rank, lanes), lambda g, s: (0, lanes // rank + s[at_pick], 0))
    normed_moved, normed, ranks, ranks_own, tables, bc, bc_t, scores, rows_f32, cums_t, keep, ups, wides, w_bc, masks = call(
        selecting(prep_kernel, rank=rank, state=state, moved_blocks=by_exchange),
        prep_out,
        prep_specs,
        [full(*s) for s, _ in prep_out],
        [pltpu.VMEM((ext, width), bf16)],
        mat // 4, 6 * mega, 1, grant=vmem_bytes * 5 // 4,
    )(sel, *prep_in)

    def part_at(row, col, *shape):
        return pl.BlockSpec(shape, lambda *s: (row, col))

    def up_at(row, rows, base=0):
        return pl.BlockSpec((rows, group), lambda g, *s: (row, g + base))

    def first_at(row, *shape):
        return pl.BlockSpec(shape, lambda g, *s: (row,) + (0,) * (len(shape) - 1))

    scores_spec, allowed_spec = (first_at(n, 1, blocks, chunk, chunk) for n in range(2))
    b_t_spec, c_t_spec = part_at(0, 0, state, own), part_at(1, 0, state, own)
    masks_spec, masks_after_spec = first_at(0, 3, own, lanes), first_at(1, 3, own, lanes)
    ad_spec, b_up_spec = part_at(0, 0, rank, width), part_at(1, 0, rank, width)
    chunk_rows = stacked(blocks, part, chunk)
    z_specs = weight_specs(w_z)
    p_spec = params_at()
    order_spec = full(group, group)
    u, scaled, sent_state = call(
        plain(proj_kernel, weights=n_w),
        [(big, f32), (big, bf16), ((state, inner), bf16)],
        [full(ext, width)] + weight_specs(w_x)
        + [full(ext, 2 * rank), up_at(1, 2 * rank), p_spec, masks_spec, part_at(0, 0, own, 2 * lanes), cols(lanes),
           b_t_spec],
        [cols(own), cols(own), cols(state)],
        [pltpu.VMEM((ext, group), f32), pltpu.VMEM((own, group), bf16)],
        mat, 12 * mega, grant=vmem_bytes * 5 // 4,
    )(sel, normed_moved, *w_x, ranks, ups, params, masks, tables, ex, bc_t)

    def chain(x, step, sign, *events):
        out, moved = [step(x)], x
        for hop in range(1, hops):
            kept = jnp.roll(keep[7:8], sign * hop * group, axis=1)
            moved = (after(out[-1], *events).astype(f32) * kept).astype(bf16)
            out.append(step(moved))
        return out, moved

    within_specs = [cols(own), part_at(0, 5, own, lanes), chunk_rows, scores_spec, cols(lanes, part * lanes)]
    states_in, moved_state = chain(sent_state, up, -1)
    (y_within,) = call(
        plain(within_kernel), [(big, f32)], within_specs, [cols(own)], [], mat, 6 * mega
    )(sel, after(scaled, moved_state), tables, cums_t, scores, exl)

    states_spec = pl.BlockSpec((blocks, state, group), lambda g, *s: (0, 0, g))
    def steps_in(phase, first, then):
        return lambda p, g: jnp.where(p == phase, g, jnp.where(p < phase, first, then))

    def moving(phase, make):
        at = steps_in(phase, 0, tp_size - 1)
        return lambda p, g, s: make(at(p, g), s)

    def cols_in(phase, rows, size=group, turn=0):
        return pl.BlockSpec((rows, size), moving(phase, lambda i, s: (0, (i + turn) % tp_size)))

    def up_in(phase, row, rows):
        return pl.BlockSpec((rows, group), moving(phase, lambda i, s: (row, i)))

    def weights_in(phase, ws):
        if len(ws) == 1:
            return [pl.BlockSpec((1,) + ws[0].shape[1:], moving(phase, lambda i, s: (s[8 + i], 0, 0)))]
        shape = (2, 1) + ws[0].shape[2:]
        first = pl.BlockSpec(shape, moving(phase, lambda i, s: (0, jnp.minimum(i, 1), 0, 0)))
        second = pl.BlockSpec(shape, moving(phase, lambda i, s: (0, jnp.maximum(i - 2, 0), 0, 0)))
        return [first] * 4 + [second] * 4

    def cols_always(rows, size):
        return pl.BlockSpec((rows, size), lambda p, g, s: (0, g))

    sent_shape = (dp_size, tp_size, 2 * rank, max(d_rows, 2 * hp))
    cot = cotangent[0]
    big3 = (tp_size, own, group)
    states, mixed, sent_out, g_heads, low_z, sent_grad, ahead_sums = call(
        selecting(middle_kernel, weights=n_w, hops=hops, inner=inner),
        [((blocks, state, inner), bf16), ((own, width), f32), (sent_shape, bf16), (big, f32), (big, bf16),
         ((state, inner), bf16), ((own, lanes), f32)],
        [full(ext, width)] + weights_in(0, w_z) + weights_in(1, w_out)
        + [cols_in(0, state, group, -h) for h in range(1, hops + 1)]
        + [full(own, 2 * rank), up_in(0, 0, 2 * rank), pl.BlockSpec((1, 8, group), lambda p, g, s: (g, 0, 0)),
           cols_in(0, own), cols_in(0, own), cols_in(0, own), part_at(0, 1, own, 2 * lanes),
           part_at(0, 4, own, lanes), cols_in(0, 8), cols_always(lanes, group), b_t_spec, c_t_spec,
           part_at(0, 1, own, state), full(own, width), full(own, width), b_up_spec, up_in(1, 4, rank), order_spec,
           pl.BlockSpec((group, lanes), moving(2, lambda i, s: (i, 0)))],
        [pl.BlockSpec((blocks, state, group), moving(0, lambda i, s: (0, 0, i))), full(own, width),
         full(*sent_shape), cols_in(2, own), cols_in(2, own), cols_in(2, state), full(own, lanes)],
        [pltpu.VMEM(big3, f32), pltpu.VMEM(big3, f32), pltpu.VMEM(big3, f32), pltpu.VMEM(big3, f32),
         pltpu.VMEM(big3, f32),
         pltpu.VMEM((own, lanes), f32), pltpu.VMEM((own, lanes), f32), pltpu.VMEM((own, width), f32),
         pltpu.VMEM((own, width), bf16), pltpu.VMEM((own, 2 * rank), bf16), pltpu.VMEM((own, rank), f32),
         pltpu.VMEM((own, group), bf16)],
        4 * mat, 40 * mega, (3, tp_size), grant=vmem_bytes * 5 // 4,
    )(sel, normed_moved, *w_z, *w_out, *states_in, ranks_own, ups, params, y_within, u, scaled, tables, tables, keep,
      ex, bc_t, bc_t, bc, cot, tok, wides, ups, order, red)
    red_spec = pl.BlockSpec((group, lanes), lambda g, *s: (g, 0))
    d_within, d_scores, ahead = call(
        plain(back_within_kernel),
        [(big, f32), ((blocks, chunk, chunk), f32), ((own, lanes), f32)],
        [cols(own), full(own, lanes)] + within_specs + [red_spec],
        [cols(own), full(blocks, chunk, chunk), full(own, lanes)],
        [pltpu.VMEM((own, group), f32)],
        2 * mat, 14 * mega, grant=vmem_bytes * 5 // 4,
    )(sel, g_heads, ahead_sums, scaled, tables, cums_t, scores, exl, red)
    grads_in, moved_grad = chain(sent_grad, down, 1, ahead)
    low_z = after(low_z, moved_grad)

    acc_z, g_rank_z, p_up_z = call(
        plain(in_z_kernel, weights=n_w),
        [((own, width), f32), ((own, rank), f32), ((tp_size, rank, group), f32)],
        [cols(own)] + z_specs + [up_at(0, rank), full(own, 2 * rank)],
        [full(own, width), full(own, rank), stacked(rank, group)],
        [],
        mat, 8 * mega,
    )(sel, low_z, *w_z, ups, ranks_own)

    grads_in = [after(x, acc_z) for x in grads_in]
    edges_shape = (edge, inner + 2 * state)
    low_x, g_u_bc, low_dt, edges, tail = call(
        plain(back_state_kernel, hops=hops),
        [(big, bf16), ((own, 2 * state), f32), ((own, heads), bf16), (edges_shape, bf16), ((edge, inner), f32)],
        [cols(state, group, h) for h in range(1, hops + 1)]
        + [states_spec, cols(own), cols(own), cols(own), cols(own), p_spec, full(own, 2 * state), c_t_spec,
           part_at(0, 0, own, 4 * lanes), cols(8), part_at(0, 0, 8, lanes), cols(lanes), red_spec,
           full(blocks, chunk, chunk), full(own, lanes), allowed_spec, full(own, 2 * state + lanes),
           masks_after_spec],
        [cols(own), full(own, 2 * state), full(own, heads), full(*edges_shape), cols(edge)],
        [pltpu.VMEM((own, state), f32), pltpu.VMEM((own, state), f32), pltpu.VMEM((own, lanes), f32),
         pltpu.VMEM((own, lanes), f32), pltpu.VMEM((8, lanes), f32), pltpu.VMEM((2, own, group), bf16),
         pltpu.VMEM((8, group), f32)],
        mat, 24 * mega,
    )(sel, *grads_in, states, g_heads, scaled, d_within, u, params, bc, bc_t, tables, keep, keep, ex, red, d_scores,
      ahead, scores, rows_f32, masks)

    halo = down(edges)
    low_x, g_rank, sent_in = call(
        selecting(in_x_kernel),
        [(big, bf16), ((own, rank), f32), (sent_shape, bf16)],
        [cols(own), cols(edge), cols(edge, group, 1), up_at(2, rank), full(own, 2 * rank), p_spec, masks_after_spec,
         full(own, rank), stacked(rank, group), order_spec, full(own, width)],
        [pl.BlockSpec((edge, group), lambda g, *s: (own // edge - 1, g)), full(own, rank), full(*sent_shape)],
        [pltpu.VMEM((own, group), bf16)],
        mat // 8, 8 * mega, in_place={0: 0},
    )(sel, low_x, tail, halo, ups, ranks_own, params, masks, g_rank_z, p_up_z, order, normed)

    (tokens_grad,) = call(
        selecting(tokens_kernel, weights=n_w),
        [((own, width), f32)],
        [cols(own)] + weight_specs(w_x)
        + [full(own, width), full(own, rank), full(own, 2 * state),
           pl.BlockSpec((edge, 2 * state), lambda g, *s: (0, inner // (2 * state))),
           full(8, 2 * state), full(width, 2 * state), full(own, heads), full(heads, width), ad_spec,
           masks_after_spec, full(own, width), full(own, width), full(1, width)],
        [full(own, width)],
        [pltpu.VMEM((own, width), f32), pltpu.VMEM((own, 2 * state), bf16), pltpu.VMEM((own, width), f32)],
        mat, 14 * mega, grant=vmem_bytes * 5 // 4,
    )(sel, low_x, *w_x, acc_z, g_rank, g_u_bc, halo, params_bc, w_bc, low_dt, dt_t, wides, masks, tok, cot,
      norm_gain[None])

    sent = jnp.concatenate([sent_out, sent_in], axis=2)
    arrived = lax.all_to_all(sent.reshape((-1,) + sent.shape[2:]), both, 0, 0, tiled=True)
    arrived = arrived.reshape(sent.shape)
    shapes = [(adapters, rank, d_rows), (adapters, hp, rank), (adapters, rank, d_rows), (adapters, 2 * hp, rank)]
    grad_out_up, grad_out_down, grad_in_down, grad_in_up = call(
        selecting(collect_kernel), [(s, f32) for s in shapes], [full(*sent.shape)],
        [full(*s) for s in shapes], [pltpu.VMEM((adapters,) + sent.shape[2:], f32)], mega, mega, 1,
    )(picks, arrived)

    grad_out_down = grad_out_down.reshape(out_down.shape)
    grad_in_down = grad_in_down.transpose(0, 2, 1)
    grad_in_up = grad_in_up.reshape(adapters, 2, part, p_part, rank).transpose(0, 4, 1, 2, 3)
    return (mixed[None], tokens_grad[None], grad_in_down, grad_in_up, grad_out_down, grad_out_up)


def solution(mesh):
    placed = (
        P("dp", "tensor", None),
        P("dp", "tensor", None),
        P("dp", None),
        P("dp"),
        P(),
        P("dp", None, "tensor"),
        P("dp", None),
        P("dp", "tensor"),
        P(None, "tensor"),
        P(),
        P("tensor"),
        P(),
        P("tensor"),
        P("tensor"),
        P("tensor"),
        P("tensor"),
        P("tensor", "dp"),
        P(None, "dp", None),
        P(None, None, None, "tensor", "dp"),
        P(None, "tensor", "dp", None),
        P(None, None, "dp"),
    )
    return jax.shard_map(
        shards,
        mesh=mesh,
        in_specs=placed,
        out_specs=(
            P("dp", "tensor", None),
            P("dp", "tensor", None),
            P(None, "dp", None),
            P(None, None, None, "tensor", "dp"),
            P(None, "tensor", "dp", None),
            P(None, None, "dp"),
        ),
        check_vma=False,
    )
```
